32 devices in a mesh: dp: 8 (over z, x), tr: 2 (over y), tc: 2 (over core).
Axes of the slice: x: 2, y: 2, z: 4, core: 2. Of those that a mesh axis runs over, the one named last changes fastest.
Arguments:
- tokens_in: bfloat16 [16928, 768], P(('dp', 'tr', 'tc')), may hold values from -6 to 6
- valid_len: int32 [32], P(('dp', 'tr', 'tc')), may hold values from 40 to 529, as said below
- mask_pos: int32 [32, 132], P(('dp', 'tr', 'tc')), may hold values from 0 to 528, as said below
- encoder_gains: bfloat16 [768, 2], P(('dp', 'tr', 'tc')), may hold values from 0.5 to 1.5
- encoder_biases: bfloat16 [768, 5], P(('dp', 'tr', 'tc')), may hold values from -1 to 1
- encoder_inproj: bfloat16 [768, 2304], P(('dp', 'tr', 'tc')), may hold values from -0.21875 to 0.21875
- encoder_outproj: bfloat16 [768, 768], P(('dp', 'tr', 'tc')), may hold values from -0.625 to 0.625
- encoder_up: bfloat16 [768, 3072], P('tc', 'tr'), may hold values from -0.21875 to 0.21875
- encoder_upbias: bfloat16 [3072], P('tr'), may hold values from -1 to 1
- encoder_down: bfloat16 [3072, 768], P('tr', 'tc'), may hold values from -0.109375 to 0.109375
- encoder_downbias: bfloat16 [768], P('tc'), may hold values from -1 to 1
- embed_weight: bfloat16 [768, 512], P(('dp', 'tr', 'tc')), may hold values from -0.21875 to 0.21875
- mask_token: bfloat16 [512], P(('dp', 'tr', 'tc')), may hold values from -4 to 4
- decoder_gains: bfloat16 [512, 2], P(('dp', 'tr', 'tc')), may hold values from 0.5 to 1.5
- decoder_biases: bfloat16 [512, 6], P(('dp', 'tr', 'tc')), may hold values from -1 to 1
- decoder_inproj: bfloat16 [512, 1536], P(('dp', 'tr', 'tc')), may hold values from -0.25 to 0.25
- decoder_outproj: bfloat16 [512, 512], P(('dp', 'tr', 'tc')), may hold values from -0.75 to 0.75
- decoder_up: bfloat16 [512, 2048], P('tc', 'tr'), may hold values from -0.25 to 0.25
- decoder_upbias: bfloat16 [2048], P('tr'), may hold values from -1 to 1
- decoder_down: bfloat16 [2048, 512], P('tr', 'tc'), may hold values from -0.125 to 0.125
- decoder_downbias: bfloat16 [512], P('tc'), may hold values from -1 to 1
- cotangent: bfloat16 [16928, 512], P(('dp', 'tr', 'tc')), may hold values from -6 to 6
Outputs:
- decoder_output: float32 [16928, 512], P(('dp', 'tr', 'tc'))
- input_grad: float32 [16928, 768], P(('dp', 'tr', 'tc'))
- encoder_gains_grad: float32 [768, 2], P(('dp', 'tr', 'tc'))
- encoder_biases_grad: float32 [768, 5], P(('dp', 'tr', 'tc'))
- encoder_inproj_grad: float32 [768, 2304], P(('dp', 'tr', 'tc'))
- encoder_outproj_grad: float32 [768, 768], P(('dp', 'tr', 'tc'))
- encoder_up_grad: float32 [768, 3072], P('tc', 'tr')
- encoder_upbias_grad: float32 [3072], P('tr')
- encoder_down_grad: float32 [3072, 768], P('tr', 'tc')
- encoder_downbias_grad: float32 [768], P('tc')
- embed_grad: float32 [768, 512], P(('dp', 'tr', 'tc'))
- mask_token_grad: float32 [512], P(('dp', 'tr', 'tc'))
- decoder_gains_grad: float32 [512, 2], P(('dp', 'tr', 'tc'))
- decoder_biases_grad: float32 [512, 6], P(('dp', 'tr', 'tc'))
- decoder_inproj_grad: float32 [512, 1536], P(('dp', 'tr', 'tc'))
- decoder_outproj_grad: float32 [512, 512], P(('dp', 'tr', 'tc'))
- decoder_up_grad: float32 [512, 2048], P('tc', 'tr')
- decoder_upbias_grad: float32 [2048], P('tr')
- decoder_down_grad: float32 [2048, 512], P('tr', 'tc')
- decoder_downbias_grad: float32 [512], P('tc')
The draws below stay inside these ranges and needn't reach their ends.
Inputs may be any that keep to these rules, and one draw needn't show every extreme that they name: `valid_len`: some sentence has exactly 529 valid patches and some exactly 40. `mask_pos`: the 132 positions of a sentence are distinct; exactly valid_len // 4 of them lie below the sentence's valid_len, the others at or beyond it.
All inputs are finite; a program needn't handle non-finite values.
Results may differ from the reference program's by a relative error of at most 0.02.
Values may be sent and summed in bfloat16 or wider, within the bound.
No kernel may reach another device: no remote copies, remote signals or barrier semaphores. Data moves between devices by JAX's collectives and lax.ppermute only.
A program may use at most 320 MiB of HBM per device.

```python
from functools import partial
import jax
import jax.numpy as jnp
from jax import lax

D = 768
HEADS = 12
FF = 3072
D2 = 512
HEADS2 = 16
FF2 = 2048
LEN = 529
MIN_LEN = 40
MASKS = 132
SEQS = 32
TOKENS = 16928


def item_lengths(key):
    drawn = jax.random.randint(key, (SEQS,), MIN_LEN, LEN + 1)
    order = jax.random.permutation(jax.random.fold_in(key, 7), SEQS)
    places = jnp.arange(SEQS)
    drawn = jnp.where(places == order[0], LEN, drawn)
    drawn = jnp.where(places == order[1], MIN_LEN, drawn)
    return drawn.astype(jnp.int32)


def draw_valid_len(key, part):
    lengths = item_lengths(key)
    return lengths


def draw_mask_pos(key, part):
    lengths = item_lengths(key)
    key = jax.random.fold_in(key, 3)
    noise = jax.random.randint(key, (SEQS, LEN), 0, 2 ** 19)
    places = lax.broadcasted_iota(jnp.int32, (SEQS, LEN), 1)
    inside = places < lengths[:, None]
    scores = noise * 1024 + places + jnp.where(inside, 2 ** 30, 0)
    ranked, order = lax.top_k(scores, LEN)
    chosen = lengths // 4
    slots = lax.broadcasted_iota(jnp.int32, (SEQS, MASKS), 1)
    source = jnp.where(slots < chosen[:, None], slots, lengths[:, None] + slots - chosen[:, None])
    return jnp.take_along_axis(order, source, axis=1).astype(jnp.int32)


def raised(values, own_key, source, target, shards_of, factor):
    def block_of(axis_at):
        return (jnp.arange(values.shape[axis_at]) // (values.shape[axis_at] // shards_of)).reshape((-1,) + (1,) * (values.ndim - 1 - axis_at))

    near = jax.random.permutation(own_key, shards_of)[block_of(target)]
    second = (block_of(target) + shards_of // 2) % shards_of
    return jnp.where((block_of(source) == near) | (block_of(source) == second), factor * values, values)


def steps_of(stream_key, shape, split, low, top_value):
    level = 1.0
    for dim, shards_of in split:
        draws = jax.random.uniform(jax.random.fold_in(jax.random.fold_in(stream_key, 6), dim), (shards_of,), jnp.float32, low / len(split), top_value / len(split))
        level = level * jnp.repeat(jnp.exp(draws), shape[dim] // shards_of).reshape((-1,) + (1,) * (len(shape) - 1 - dim))
    return level


def bell_draw(stream_key, shape, scale, reach, split=(), dtype=jnp.bfloat16):
    level = steps_of(stream_key, shape, split, -0.22, 0.18) if split else 1.0
    array = jax.random.normal(stream_key, shape, jnp.float32) * scale * level
    return jnp.minimum(jnp.maximum(array, -reach), reach).astype(dtype)


def bell_draw_with(own_key, shape, scale, bound, pieces, heavy, kind=jnp.bfloat16):
    entries = scale * jax.random.normal(own_key, shape, jnp.float32)
    if pieces:
        entries = entries * steps_of(own_key, shape, pieces, -0.22, 0.18)
    return jnp.clip(raised(entries, jax.random.fold_in(own_key, 3), *heavy), -bound, bound).astype(kind)


def setup_inputs(seed: int = 0) -> dict:
    streams_of = jax.random.split(jax.random.key(seed), 23)
    return {
        "tokens_in": bell_draw_with(streams_of[0], (TOKENS, D), 1.0, 6.0, ((0, 32),), (0, 1, 32, 2.75)),
        "valid_len": draw_valid_len(jax.random.fold_in(streams_of[22], 71), 0),
        "mask_pos": draw_mask_pos(jax.random.fold_in(streams_of[22], 71), 0),
        "encoder_gains": jnp.clip(1.0 + 0.1 * jax.random.normal(streams_of[3], (D, 2), jnp.float32), 0.5, 1.5).astype(jnp.bfloat16),
        "encoder_biases": bell_draw(streams_of[4], (D, 5), 0.2, 1.0, ((0, 32),)),
        "encoder_inproj": bell_draw(streams_of[5], (D, 3 * D), D ** -0.5, 0.21875, ((0, 32),)),
        "encoder_outproj": bell_draw(streams_of[6], (D, D), (D // 8) ** -0.5, 0.625, ((0, 32),)),
        "encoder_up": bell_draw(streams_of[7], (D, FF), D ** -0.5, 0.21875, ((0, 2), (1, 2))),
        "encoder_upbias": bell_draw(streams_of[8], (FF,), 0.2, 1.0, ((0, 2),)),
        "encoder_down": bell_draw(streams_of[9], (FF, D), FF ** -0.5, 0.109375, ((0, 2), (1, 2))),
        "encoder_downbias": bell_draw(streams_of[10], (D,), 0.2, 1.0, ((0, 2),)),
        "embed_weight": bell_draw(streams_of[11], (D, D2), D ** -0.5, 0.21875, ((0, 32),)),
        "mask_token": bell_draw(streams_of[12], (D2,), 1.0, 4.0, ((0, 32),)),
        "decoder_gains": jnp.clip(1.0 + 0.1 * jax.random.normal(streams_of[13], (D2, 2), jnp.float32), 0.5, 1.5).astype(jnp.bfloat16),
        "decoder_biases": bell_draw(streams_of[14], (D2, 6), 0.2, 1.0, ((0, 32),)),
        "decoder_inproj": bell_draw(streams_of[15], (D2, 3 * D2), D2 ** -0.5, 0.25, ((0, 32),)),
        "decoder_outproj": bell_draw(streams_of[16], (D2, D2), (D2 // 8) ** -0.5, 0.75, ((0, 32),)),
        "decoder_up": bell_draw(streams_of[17], (D2, FF2), D2 ** -0.5, 0.25, ((0, 2), (1, 2))),
        "decoder_upbias": bell_draw(streams_of[18], (FF2,), 0.2, 1.0, ((0, 2),)),
        "decoder_down": bell_draw(streams_of[19], (FF2, D2), FF2 ** -0.5, 0.125, ((0, 2), (1, 2))),
        "decoder_downbias": bell_draw(streams_of[20], (D2,), 0.2, 1.0, ((0, 2),)),
        "cotangent": bell_draw(streams_of[21], (TOKENS, D2), 1.0, 6.0, ((0, 32),)),
    }


@jax.custom_vjp
def low(v):
    return lax.optimization_barrier(v.astype(jnp.bfloat16)).astype(jnp.float32)

@jax.custom_vjp
def low_back(v):
    return v

def low_keep(v):
    return (low(v), None)

def low_pass(kept, grad):
    return (grad,)

def back_keep(v):
    return (v, None)

def back_low(kept, grad):
    return (low(grad),)
low.defvjp(low_keep, low_pass)
low_back.defvjp(back_keep, back_low)
highest = lax.Precision.HIGHEST
epsilon = 1e-06
masked_score = -1e+30

def matmul(operand, matrix):
    return jnp.dot(operand, matrix, precision=highest)

def normalize(values, gain, shift):
    center = values - lax.optimization_barrier(jnp.mean(values, axis=-1, keepdims=True))
    spread = lax.optimization_barrier(jnp.mean(center * center, axis=-1, keepdims=True))
    return center * lax.rsqrt(spread + epsilon) * gain + shift

def attend(head_count, inputs):
    packed, key_mask = inputs
    model_width = packed.shape[1] // 3
    head_size = model_width // head_count
    query_rows = packed[:, :model_width].reshape(-1, head_count, head_size)
    key_rows = packed[:, model_width:2 * model_width].reshape(-1, head_count, head_size)
    value_rows = packed[:, 2 * model_width:].reshape(-1, head_count, head_size)
    scores = jnp.einsum('qhd,khd->hqk', query_rows, key_rows, precision=highest) * head_size ** (-0.5)
    scores = low_back(scores)
    scores = jnp.where(key_mask[None, None, :], scores, masked_score)
    weights = low(jax.nn.softmax(scores, axis=-1))
    output = jnp.einsum('hqk,khd->qhd', weights, value_rows, precision=highest)
    return output.reshape(-1, model_width)

def residual_block(stream, params, key_mask, head_count):
    gains, biases, inproj, outproj, up_weight, up_bias, down_weight, down_bias = params
    model_width = stream.shape[1]
    normed = low(normalize(stream, gains[:, 0], biases[:, 0]))
    bias_row = jnp.concatenate([biases[:, 1], jnp.zeros_like(biases[:, 1]), biases[:, 2]])
    packed = low_back(low(matmul(normed, inproj) + bias_row))
    per_item = packed.reshape(-1, LEN, 3 * model_width)
    attended = lax.map(jax.checkpoint(partial(attend, head_count)), (per_item, key_mask))
    attended = low_back(low(attended.reshape(-1, model_width)))
    branch = low_back(matmul(attended, outproj) + biases[:, 3])
    middle = stream + branch
    normed_two = low_back(low(normalize(middle, gains[:, 1], biases[:, 4])))
    hidden = low_back(matmul(normed_two, up_weight) + up_bias)
    active = low_back(low(jax.nn.gelu(hidden, approximate=False)))
    result = low_back(low(matmul(active, down_weight) + down_bias))
    return middle + result

def forward(params, stream, lengths, positions):
    encoder_params, embed_weight, mask_token, decoder_params = params
    places = lax.broadcasted_iota(jnp.int32, (lengths.shape[0], LEN), 1)
    inside = places < lengths[:, None]
    covered = jnp.any(positions[:, None, :] == places[:, :, None], axis=2)
    encoder_keys = jnp.logical_and(inside, jnp.logical_not(covered))
    encoded = residual_block(stream, encoder_params, encoder_keys, HEADS)
    decoder_biases = decoder_params[1]
    embedded = low_back(matmul(low(encoded), embed_weight) + decoder_biases[:, 5])
    decoded = jnp.where(covered.reshape(-1, 1), mask_token[None, :], embedded)
    return residual_block(decoded, decoder_params, inside, HEADS2)

def to_float(values):
    return values.astype(jnp.float32)

def reference(tokens_in, valid_len, mask_pos, encoder_gains, encoder_biases, encoder_inproj, encoder_outproj, encoder_up, encoder_upbias, encoder_down, encoder_downbias, embed_weight, mask_token, decoder_gains, decoder_biases, decoder_inproj, decoder_outproj, decoder_up, decoder_upbias, decoder_down, decoder_downbias, cotangent):
    encoder_params = tuple((to_float(values) for values in (encoder_gains, encoder_biases, encoder_inproj, encoder_outproj, encoder_up, encoder_upbias, encoder_down, encoder_downbias)))
    decoder_params = tuple((to_float(values) for values in (decoder_gains, decoder_biases, decoder_inproj, decoder_outproj, decoder_up, decoder_upbias, decoder_down, decoder_downbias)))
    params = (encoder_params, to_float(embed_weight), to_float(mask_token), decoder_params)
    per_group = 8
    groups = SEQS // per_group
    group_rows = per_group * LEN
    streams = tokens_in.astype(jnp.float32).reshape(groups, group_rows, D)
    cotangents = cotangent.astype(jnp.float32).reshape(groups, group_rows, D2)
    lengths = valid_len.reshape(groups, per_group)
    positions = mask_pos.reshape(groups, per_group, MASKS)

    def group_step(totals, inputs):
        stream, cot_rows, length_rows, position_rows = inputs
        output, pullback = jax.vjp(lambda weights, values: forward(weights, values, length_rows, position_rows), params, stream)
        grad_params, grad_stream = pullback(cot_rows)
        totals = jax.tree.map(jnp.add, totals, grad_params)
        return (totals, (output, grad_stream))
    zero_grads = jax.tree.map(jnp.zeros_like, params)
    totals, (outputs, grad_streams) = lax.scan(group_step, zero_grads, (streams, cotangents, lengths, positions))
    encoder_grads, embed_grad, mask_grad, decoder_grads = totals
    return (outputs.reshape(TOKENS, D2), grad_streams.reshape(TOKENS, D), encoder_grads[0], encoder_grads[1], encoder_grads[2], encoder_grads[3], encoder_grads[4], encoder_grads[5], encoder_grads[6], encoder_grads[7], embed_grad, mask_grad, decoder_grads[0], decoder_grads[1], decoder_grads[2], decoder_grads[3], decoder_grads[4], decoder_grads[5], decoder_grads[6], decoder_grads[7])
```

```python
import math
from functools import partial

import jax
import jax.numpy as jnp
from jax import lax
from jax.experimental import pallas as pl
from jax.experimental.pallas import tpu as pltpu
from jax.sharding import PartitionSpec as P

HEADS = 12
HEADS2 = 16
ALL = ("dp", "tr", "tc")
EPS = 1e-06
MASKED = -1e30
LOG2E = math.log2(math.e)
F32 = jnp.float32
BF = jnp.bfloat16
VMEM_BYTES = 58 * 1024 * 1024


def dot_nn(a, b):
    return lax.dot_general(a, b, (((1,), (0,)), ((), ())), preferred_element_type=F32)


def dot_nt(a, b):
    return lax.dot_general(a, b, (((1,), (1,)), ((), ())), preferred_element_type=F32)


def cost(us):
    return pl.CostEstimate(flops=int(us * 1e9), bytes_accessed=int(us * 3e6), transcendentals=0)


def call(body, outs, args, scratch=(), smem=0, us=2):
    specs = [pl.BlockSpec(memory_space=pltpu.SMEM)] * smem
    specs += [pl.BlockSpec(memory_space=pltpu.VMEM)] * (len(args) - smem)
    return pl.pallas_call(
        body,
        out_shape=[jax.ShapeDtypeStruct(s, d) for s, d in outs],
        in_specs=specs,
        out_specs=[pl.BlockSpec(memory_space=pltpu.VMEM)] * len(outs),
        scratch_shapes=[pltpu.VMEM(s, d) for s, d in scratch],
        compiler_params=pltpu.CompilerParams(vmem_limit_bytes=VMEM_BYTES),
        cost_estimate=cost(us),
    )(*args)


def norm_parts(v):
    center = v - jnp.mean(v, axis=-1, keepdims=True)
    r = lax.rsqrt(jnp.mean(center * center, axis=-1, keepdims=True) + EPS)
    return center * r, r


def norm_back(u, r, gain, y):
    e = y * gain
    back = r * (e - jnp.mean(e, axis=-1, keepdims=True) - u * jnp.mean(e * u, axis=-1, keepdims=True))
    return back, jnp.sum(y * u, axis=0, keepdims=True), jnp.sum(y, axis=0, keepdims=True)


def split3(v):
    hi = v.astype(BF)
    rest = v - hi.astype(F32)
    mid = rest.astype(BF)
    return hi, mid, (rest - mid.astype(F32)).astype(BF)


def head_masks(head_size):
    lane = lax.broadcasted_iota(jnp.int32, (1, 128), 1) // head_size
    return [(lane == h).astype(F32).astype(BF) for h in range(128 // head_size)]


def stack_heads(rows, masks):
    return jnp.concatenate([rows * m for m in masks], axis=0)


def prep_body(kept, mp_col, mp_row, tokens, cot, x_out, cot_out, place_out):
    rows, span = x_out.shape[0], tokens.shape[0]
    wide = lax.broadcasted_iota(jnp.int32, (mp_col.shape[0], span), 1)
    below = jnp.sum((mp_col[...] < wide).astype(F32), axis=0, keepdims=True)
    here = jnp.sum((mp_col[...] == wide).astype(F32), axis=0, keepdims=True)
    place = jnp.where(here > 0, kept, wide[:1] - below.astype(jnp.int32))
    pick = lax.broadcasted_iota(jnp.int32, (rows, span), 0) == place
    pick_f = pick.astype(F32)
    cot_out[...] = dot_nn(pick_f.astype(BF), cot[...])
    keep = lax.broadcasted_iota(jnp.int32, (rows, span), 0) < kept
    x_out[...] = dot_nn(jnp.where(keep, pick_f, 0.0).astype(BF), tokens[...]).astype(BF)
    tall = lax.broadcasted_iota(jnp.int32, (span, mp_row.shape[1]), 0)
    below_t = jnp.sum((mp_row[...] < tall).astype(F32), axis=1, keepdims=True)
    here_t = jnp.sum((mp_row[...] == tall).astype(F32), axis=1, keepdims=True)
    place_out[...] = jnp.where(here_t > 0, kept, tall[:, :1] - below_t.astype(jnp.int32))


def spread_back(place, rows, limit):
    at = lax.broadcasted_iota(jnp.int32, (place.shape[0], rows), 1)
    return jnp.where(at < limit, (at == place).astype(F32), 0.0).astype(BF)


def key_bias(lens, kept, rows, with_mask_row):
    at = lax.broadcasted_iota(jnp.int32, (rows, 1), 0)
    bias = jnp.where(at < lens[0], 0.0, MASKED)
    if with_mask_row:
        count = jnp.full((rows, 1), lens[1], jnp.int32).astype(F32)
        bias = jnp.where(at == kept, jnp.log(count) * LOG2E, bias)
    return bias


def attention_forward(packed, att_t, lse, bias, head_size):
    width = packed.shape[1] // 3
    rows = packed.shape[0]
    masks = head_masks(head_size)
    scale = head_size**-0.5 * LOG2E

    def group(g, carry):
        at = pl.multiple_of(g * 128, 128)
        q = packed[:, pl.ds(at, 128)]
        k = packed[:, pl.ds(width + at, 128)]
        v_t = packed[:, pl.ds(2 * width + at, 128)].T
        scores = dot_nt(k, stack_heads(q, masks)) * scale + bias
        peak = jnp.max(scores, axis=0, keepdims=True)
        weights = jnp.exp2(scores - peak)
        total = jnp.sum(weights, axis=0, keepdims=True)
        out = dot_nn(v_t, weights.astype(BF)) * (1.0 / total)
        for h in range(len(masks)):
            block = out[h * head_size : (h + 1) * head_size, h * rows : (h + 1) * rows]
            att_t[pl.ds(at + h * head_size, head_size), :] = block.astype(BF)
        lse[pl.ds(g, 1), :] = peak + jnp.log(total) * LOG2E
        return carry

    lax.fori_loop(0, width // 128, group, 0)


def attention_backward(packed, g_att, lse, g_packed, gq_t, bias, head_size):
    width = packed.shape[1] // 3
    rows = packed.shape[0]
    masks = head_masks(head_size)
    scale = head_size**-0.5

    def group(g, carry):
        at = pl.multiple_of(g * 128, 128)
        q = packed[:, pl.ds(at, 128)]
        k = packed[:, pl.ds(width + at, 128)]
        v = packed[:, pl.ds(2 * width + at, 128)]
        q_s = stack_heads(q, masks)
        g_s = stack_heads(g_att[:, pl.ds(at, 128)], masks)
        scores = dot_nt(k, q_s) * (scale * LOG2E) + bias
        probs = jnp.exp2(scores - lse[pl.ds(g, 1), :])
        g_v = dot_nn(probs.astype(BF), g_s)
        g_probs = dot_nt(v, g_s)
        delta = jnp.sum(g_probs * probs, axis=0, keepdims=True)
        g_scores = (probs * (g_probs - delta)).astype(BF)
        g_k = dot_nn(g_scores, q_s) * scale
        out = dot_nn(k.T, g_scores) * scale
        for h in range(len(masks)):
            block = out[h * head_size : (h + 1) * head_size, h * rows : (h + 1) * rows]
            gq_t[pl.ds(at + h * head_size, head_size), :] = block.astype(BF)
        g_packed[:, pl.ds(width + at, 128)] = g_k.astype(BF)
        g_packed[:, pl.ds(2 * width + at, 128)] = g_v.astype(BF)
        return carry

    lax.fori_loop(0, width // 128, group, 0)
    g_packed[:, :width] = gq_t[...].T


def project_in(stream, params, inproj, normed_out, packed_out):
    u, r = norm_parts(stream)
    normed = (u * params[0:1, :] + params[2:3, :]).astype(BF)
    normed_out[...] = normed
    width = stream.shape[1]
    step = 256
    for part in range(3):
        for at in range(0, width, step):
            lo = part * width + at
            value = dot_nn(normed, inproj[:, lo : lo + step])
            if part == 0:
                value = value + params[3:4, at : at + step]
            if part == 2:
                value = value + params[4:5, at : at + step]
            packed_out[:, lo : lo + step] = value.astype(BF)


GATHER_A = (("dp", 4), ("tr", 1), ("dp", 2), ("dp", 1))
GATHER_B = (("dp", 4), ("tr", 1), ("dp", 1), ("dp", 2))
GATHER_C = (("tr", 1), ("dp", 4), ("dp", 2), ("dp", 1))
GATHER_D = (("tr", 1), ("dp", 4), ("dp", 1), ("dp", 2))
SCATTER_A = (("tr", 1), ("dp", 1), ("dp", 2), ("dp", 4))
SCATTER_B = (("dp", 1), ("tr", 1), ("dp", 2), ("dp", 4))
SCATTER_C = (("dp", 2), ("dp", 1), ("tr", 1), ("dp", 4))


def differences(order, bits):
    dp = tr = 0
    for (axis, distance), bit in zip(order, bits):
        if axis == "dp":
            dp = dp + distance * bit
        else:
            tr = tr + bit
    return dp, tr


def gathered_block(order, j, last):
    return differences(order, (j & 1, (j >> 1) & 1, (j >> 2) & 1, last))


def scattered_block(order, m):
    return differences(order, (m >> 3, (m >> 2) & 1, (m >> 1) & 1, m & 1))


def feed_block(m):
    return (m & 1) * 4 + ((m >> 1) & 1) * 2 + (m >> 2)


def place_rows(place, order, sources, block, put):
    first = place[2] == 0
    for x in range(2):
        own_ref, oth_ref = sources[x], sources[2 + x]
        count = own_ref.shape[0] // block

        def one(j, carry, own_ref=own_ref, oth_ref=oth_ref, x=x):
            dp, tr = gathered_block(order, j, x)
            chip = (place[0] ^ dp) * 2 + (place[1] ^ tr)
            at = pl.multiple_of(j * block, block)
            own = own_ref[pl.ds(at, block), :].astype(F32)
            oth = oth_ref[pl.ds(at, block), :].astype(F32)
            put(chip, jnp.where(first, own, oth), jnp.where(first, oth, own))
            return carry

        lax.fori_loop(0, count, one, 0)


def place_halves(place, order, sources, cuts):
    block = sources[0].shape[0] // 8
    half = block // 2

    def put(chip, low, high):
        at = pl.multiple_of(chip * block, block)
        top = jnp.concatenate([low[:half], high[:half]], axis=0).astype(BF)
        bottom = jnp.concatenate([low[half:], high[half:]], axis=0).astype(BF)
        lo = 0
        for target, first, width, shift in cuts:
            target[pl.ds(at, block), first : first + width] = top[:, lo : lo + width]
            if shift is not None:
                right = first + shift
                target[pl.ds(at, block), right : right + width] = bottom[:, lo : lo + width]
            lo += width

    place_rows(place, order, sources, block, put)


def place_whole(place, order, sources, cuts):
    block = sources[0].shape[0] // 8

    def put(chip, low, high):
        at = pl.multiple_of(chip * 2 * block, 2 * block)
        both = jnp.concatenate([low, high], axis=0).astype(BF)
        lo = 0
        for target, width in cuts:
            target[pl.ds(at, 2 * block), :] = both[:, lo : lo + width]
            lo += width

    place_rows(place, order, sources, block, put)


def param_rows(columns):
    return columns[...].astype(F32).T[:16]


def reorder_rows(place, order, source, target):
    block = source.shape[0] // 32
    for core in range(2):
        for m in range(16):
            dp, tr = scattered_block(order, m)
            device = ((place[0] ^ dp) * 2 + (place[1] ^ tr)) * 2 + (place[2] ^ core)
            at = pl.multiple_of(device * block, 8)
            to = (core * 16 + m) * block
            target[to : to + block, :] = source[pl.ds(at, block), :]


def write_halves(ordered, columns, outs, first=0, count=None):
    half_rows = ordered.shape[0] // 2
    block = half_rows // 16
    width = columns.shape[1] // 2
    count = width if count is None else count
    step = max(n for n in (384, 320, 256) if count % n == 0) if count != 640 else 640
    for core in range(2):
        rows = ordered[core * half_rows : (core + 1) * half_rows, :].astype(BF)
        for at in range(first, first + count, step):
            left = dot_nn(rows, columns[:, at : at + step])
            right = dot_nn(rows, columns[:, width + at : width + at + step])
            for m in range(16):
                both = [left[m * block : (m + 1) * block], right[m * block : (m + 1) * block]]
                outs[core][m * 2 * block : (m + 1) * 2 * block, at - first : at - first + step] = (
                    jnp.concatenate(both, axis=0).astype(BF)
                )


def write_whole(ordered, columns, outs, lo):
    half_rows = ordered.shape[0] // 2
    width = columns.shape[1]
    for core in range(2):
        rows = ordered[core * half_rows : (core + 1) * half_rows, :].astype(BF)
        for at in range(0, width, 256):
            outs[core][:, lo + at : lo + at + 256] = dot_nn(rows, columns[:, at : at + 256]).astype(BF)


def small_columns(small):
    table = jnp.concatenate([small[...], jnp.zeros((112, small.shape[1]), F32)], axis=0)
    return table.T


def pack_body(
    e_gains, e_biases, e_in, e_out, embed, d_gains, d_biases, token, d_in, d_out, one_a, one_b, two, three
):
    def columns(parts):
        total, lo = 0.0, 0
        for part in parts:
            count, rows = part.shape
            spot = lax.broadcasted_iota(jnp.int32, (count, 128), 1)
            want = lax.broadcasted_iota(jnp.int32, (count, 128), 0) + lo
            table = (spot == want).astype(F32).astype(BF)
            total = total + lax.dot_general(
                part[...], table, (((0,), (0,)), ((), ())), preferred_element_type=F32
            )
            lo += count
        return total

    e_par = columns([e_gains, e_biases])

    def halves(v):
        v = v[...].astype(F32)
        width = v.shape[1] // 2
        return jnp.concatenate([v[:, :width], v[:, width:]], axis=0).astype(BF)

    n = one_a.shape[1]
    m = one_b.shape[1] - 128
    both = halves(e_in)
    one_a[...] = both[:, :n]
    one_b[:, :m] = both[:, n:]
    one_b[:, m:] = jnp.concatenate([e_par, jnp.zeros_like(e_par)], axis=0).astype(BF)
    n = e_out.shape[1] // 2
    two[:, :n] = halves(e_out)
    two[:, n:] = halves(embed)
    n = d_in.shape[1]
    m = n + d_out.shape[1]
    three[:, :n] = d_in[...]
    three[:, n:m] = d_out[...]
    three[:, m:] = columns([d_gains, d_biases, token]).astype(BF)


def enc_attn_body(
    kept, place, x, s0, s1, s2, s3, r0, r1, r2, r3,
    normed, packed, att_t, lse, inproj, par_t, par_c,
):
    width = x.shape[1]
    n, shift = s0.shape[1], 3 * width // 2
    place_halves(place, GATHER_A, (s0, s1, s2, s3), ((inproj, 0, n, shift),))
    place_halves(
        place, GATHER_B, (r0, r1, r2, r3), ((inproj, n, shift - n, shift), (par_c, 0, 128, None))
    )
    par_t[...] = param_rows(par_c)
    project_in(x[...].astype(F32), par_t, inproj, normed, packed)
    bias = key_bias((place[5], place[6]), kept, x.shape[0], False)
    attention_forward(packed, att_t, lse, bias, width // HEADS)


def dec_attn_body(
    kept, place, e_low, embed, s0, s1, s2, s3,
    stream, normed, packed, att_t, lse, inproj, outproj, params, par_c,
):
    rows = e_low.shape[0]
    width = stream.shape[1]
    place_whole(
        place, GATHER_D, (s0, s1, s2, s3), ((inproj, 3 * width), (outproj, width), (par_c, 128))
    )
    params[...] = param_rows(par_c)
    embedded = dot_nn(e_low[...], embed[...]) + params[7:8, :]
    at = lax.broadcasted_iota(jnp.int32, (rows, 1), 0)
    decoded = jnp.where(at < kept, embedded, params[8:9, :])
    stream[...] = decoded
    project_in(decoded, params, inproj, normed, packed)
    bias = key_bias((place[5], place[6]), kept, rows, True)
    attention_forward(packed, att_t, lse, bias, width // HEADS2)


def load_feed(place, ups, downs, up, down, sems, part=0):
    copies = []
    half = up.shape[0] // 2
    units = up.shape[1] // 2
    for tr in range(2):
        for core in range(2):
            at = pl.multiple_of((place[4] ^ core) * half, 128)
            n = 2 * (2 * tr + core)
            here = pl.ds(part * units, units)
            to_up = up.at[pl.ds(at, half), pl.ds(tr * units, units)]
            to_down = down.at[pl.ds(tr * units, units), pl.ds(at, half)]
            copies.append(pltpu.make_async_copy(ups[2 * tr + core].at[:, here], to_up, sems.at[n]))
            copies.append(
                pltpu.make_async_copy(downs[2 * tr + core].at[here, :], to_down, sems.at[n + 1])
            )
    for copy in copies:
        copy.start()
    return copies


def middle_of(stream, att_t, outproj, params):
    return stream + dot_nn(att_t[...].T, outproj[...]) + params[5:6, :]


def feed_forward(normed_two, up, up_bias, down, active_out, slope_out, total, step):
    hidden_units = up.shape[1]
    total[...] = jnp.zeros_like(total)

    def chunk(c, carry):
        at = pl.multiple_of(c * step, step)
        hidden = dot_nn(normed_two, up[:, pl.ds(at, step)]) + up_bias[:, pl.ds(at, step)]
        phi = 0.5 * (1.0 + lax.erf(hidden * math.sqrt(0.5)))
        bell = jnp.exp2(hidden * hidden * (-0.5 * LOG2E)) * (1.0 / math.sqrt(2 * math.pi))
        active = (hidden * phi).astype(BF)
        active_out[:, pl.ds(at, step)] = active
        slope_out[:, pl.ds(at, step)] = (phi + hidden * bell).astype(BF)
        total[...] += dot_nn(active, down[pl.ds(at, step), :])
        return carry

    lax.fori_loop(0, hidden_units // step, chunk, 0)


def feed_backward(
    place, part, parts, g_result, normed_two, active, slope, up, down,
    g_ups, g_downs, g_upbias, g_normed, step, normed_t, ordered_t, act_t, act_o, g_cols,
):
    width = normed_two.shape[1]
    half = width // 2
    count = up.shape[1] // 2
    units = count * parts
    block, hidden_block = half // 8, count // 8
    g_cols[:, :half] = g_result[:, pl.ds(pl.multiple_of(place[4] * half, 128), half)]
    g_cols[:, half:] = g_result[:, pl.ds(pl.multiple_of((1 - place[4]) * half, 128), half)]
    normed_t[...] = normed_two[...].T
    for core in range(2):
        for m in range(8):
            at = ((place[4] ^ core) * 8 + (place[3] ^ feed_block(m))) * block
            to = (core * 8 + m) * block
            ordered_t[to : to + block, :] = normed_t[pl.ds(pl.multiple_of(at, block), block), :]
    for tr in range(2):
        base = tr * units + part * count
        out_base = pl.multiple_of((place[7] ^ tr) * units + part * count, 128)
        act_t[...] = active[:, base : base + count].T
        for m in range(8):
            at = pl.multiple_of((place[3] ^ feed_block(m)) * hidden_block, hidden_block)
            to = m * hidden_block
            act_o[to : to + hidden_block, :] = act_t[pl.ds(at, hidden_block), :]

        def chunk(c, carry, tr=tr, base=base, out_base=out_base):
            at = pl.multiple_of(c * step, step)
            here = pl.ds(pl.multiple_of(tr * count + at, 128), step)
            g_active = dot_nt(g_result[...], down[here, :]).astype(BF).astype(F32)
            there = pl.ds(pl.multiple_of(base + at, 128), step)
            g_hidden = (slope[:, there].astype(F32) * g_active).astype(BF)
            g_upbias[:, pl.ds(pl.multiple_of(out_base + at, 128), step)] = jnp.sum(
                g_hidden.astype(F32), axis=0, keepdims=True
            )
            g_up = dot_nn(ordered_t[...], g_hidden).astype(BF)
            g_ups[2 * tr][:, pl.ds(at, step)] = g_up[:half]
            g_ups[2 * tr + 1][:, pl.ds(at, step)] = g_up[half:]
            g_down = dot_nn(act_o[pl.ds(at, step), :], g_cols[...]).astype(BF)
            g_downs[2 * tr][pl.ds(at, step), :] = g_down[:, :half]
            g_downs[2 * tr + 1][pl.ds(at, step), :] = g_down[:, half:]
            g_normed[...] += dot_nt(g_hidden, up[:, here])
            return carry

        lax.fori_loop(0, count // step, chunk, 0)


def after_feed_backward(
    place, order, g_out, g_normed, middle, params, att_t, outproj, g_middle, g_att, small, att_f, att_o
):
    u, r = norm_parts(middle)
    y = g_normed.astype(BF).astype(F32)
    back, g_gain, g_shift = norm_back(u, r, params[1:2, :], y)
    grad = g_out + back
    g_middle[...] = grad
    branch = grad.astype(BF)
    att_f[...] = att_t[...].astype(F32)
    reorder_rows(place, order, att_f, att_o)
    g_att[...] = dot_nt(branch, outproj[...]).astype(BF)
    small[1:2, :] = g_gain
    small[5:6, :] = jnp.sum(branch.astype(F32), axis=0, keepdims=True)
    small[6:7, :] = g_shift
    return branch


def enc_feed_body(
    place, x, att_t, s0, s1, s2, s3, params, up_bias, down_bias, u0, u1, u2, u3, d0, d1, d2, d3,
    middle, normed_two, active, slope, e_low, outproj, embed, up, down, total, sems,
):
    copies = load_feed(place, (u0, u1, u2, u3), (d0, d1, d2, d3), up, down, sems)
    width = x.shape[1]
    n, m = width // 2, embed.shape[1] // 2
    place_halves(
        place, GATHER_C, (s0, s1, s2, s3), ((outproj, 0, n, n), (embed, 0, m, m))
    )
    mid = middle_of(x[...].astype(F32), att_t, outproj, params)
    middle[...] = mid
    u, r = norm_parts(mid)
    n2 = (u * params[1:2, :] + params[6:7, :]).astype(BF)
    normed_two[...] = n2
    for copy in copies:
        copy.wait()
    feed_forward(n2, up, up_bias, down, active, slope, total, 512)
    result = (total[...] + down_bias[...]).astype(BF)
    e_low[...] = (middle[...] + result.astype(F32)).astype(BF)


def dec_feed_body(
    kept, place, stream, att_t, outproj, params, up_bias, down_bias, cot, spots,
    u0, u1, u2, u3, d0, d1, d2, d3,
    output, gu0, gu1, gu2, gu3, gd0, gd1, gd2, gd3, g_middle, g_att, go0, go1, small, biases,
    up, down, active, slope, total, n2_s, g_res, normed_t, ordered_t, act_t, act_o, g_cols,
    att_f, att_o, branch_s, sems,
):
    copies = load_feed(place, (u0, u1, u2, u3), (d0, d1, d2, d3), up, down, sems)
    mid = middle_of(stream[...], att_t, outproj, params)
    u, r = norm_parts(mid)
    n2 = (u * params[1:2, :] + params[6:7, :]).astype(BF)
    n2_s[...] = n2
    for copy in copies:
        copy.wait()
    feed_forward(n2, up, up_bias, down, active, slope, total, 512)
    result = (total[...] + down_bias[...]).astype(BF)
    out = mid + result.astype(F32)
    pick = spread_back(spots[...], out.shape[0], kept + 1)
    hi, mid_part, low = split3(out)
    output[...] = dot_nn(pick, hi) + dot_nn(pick, mid_part) + dot_nn(pick, low)
    g_out = cot[...]
    g_res[...] = g_out.astype(BF)
    small[...] = jnp.zeros_like(small)
    units = up.shape[1]
    biases[:, units:] = jnp.sum(g_res[...].astype(F32), axis=0, keepdims=True)
    total[...] = jnp.zeros_like(total)
    feed_backward(
        place, 0, 1, g_res, n2_s, active, slope, up, down, (gu0, gu1, gu2, gu3),
        (gd0, gd1, gd2, gd3), biases, total, 512, normed_t, ordered_t, act_t, act_o, g_cols,
    )
    branch = after_feed_backward(
        place, SCATTER_A, g_out, total[...], mid, params, att_t, outproj, g_middle, g_att, small, att_f, att_o
    )
    branch_s[...] = branch
    write_whole(att_o, branch_s, (go0, go1), 0)


def enc_feed_back_one_body(
    place, g_enc, normed_two, active, slope, u0, u1, u2, u3, d0, d1, d2, d3,
    gu0, gu1, gu2, gu3, gd0, gd1, gd2, gd3, total, biases,
    up, down, g_res, normed_t, ordered_t, act_t, act_o, g_cols, sems,
):
    copies = load_feed(place, (u0, u1, u2, u3), (d0, d1, d2, d3), up, down, sems)
    g_res[...] = g_enc[...].astype(BF)
    total[...] = jnp.zeros_like(total)
    biases[:, 2 * up.shape[1] :] = jnp.sum(g_res[...].astype(F32), axis=0, keepdims=True)
    for copy in copies:
        copy.wait()
    feed_backward(
        place, 0, 2, g_res, normed_two, active, slope, up, down, (gu0, gu1, gu2, gu3),
        (gd0, gd1, gd2, gd3), biases, total, 384, normed_t, ordered_t, act_t, act_o, g_cols,
    )


def enc_feed_back_two_body(
    place, g_enc, normed_two, active, slope, total_in, biases_in, biases_dec, middle, params, att_t,
    outproj, u0, u1, u2, u3, d0, d1, d2, d3,
    gu0, gu1, gu2, gu3, gd0, gd1, gd2, gd3, g_middle, g_att, go0, go1, small, biases,
    total, up, down, g_res, normed_t, ordered_t, act_t, act_o, g_cols, att_f, att_o, branch_s, sems,
):
    copies = load_feed(place, (u0, u1, u2, u3), (d0, d1, d2, d3), up, down, sems, 1)
    g_res[...] = g_enc[...].astype(BF)
    total[...] = total_in[...]
    count = biases_in.shape[1]
    biases[:, :count] = biases_in[...]
    biases[:, count:] = biases_dec[...]
    small[...] = jnp.zeros_like(small)
    for copy in copies:
        copy.wait()
    feed_backward(
        place, 1, 2, g_res, normed_two, active, slope, up, down, (gu0, gu1, gu2, gu3),
        (gd0, gd1, gd2, gd3), biases, total, 384, normed_t, ordered_t, act_t, act_o, g_cols,
    )
    branch = after_feed_backward(
        place, SCATTER_C, g_enc[...], total[...], middle[...], params, att_t, outproj, g_middle, g_att, small,
        att_f, att_o,
    )
    branch_s[...] = branch
    write_halves(att_o, branch_s, (go0, go1))


def project_back(place, order, stream, normed, g_packed, g_middle, params, inproj, small, first, rows_f, rows_o):
    width = stream.shape[1]
    rows_f[...] = normed[...].astype(F32).T
    reorder_rows(place, order, rows_f, rows_o)
    g_normed = dot_nt(g_packed[...], inproj[...])
    u, r = norm_parts(stream)
    back, g_gain, g_shift = norm_back(u, r, params[0:1, :], g_normed)
    small[...] = first[...]
    small[0:1, :] = g_gain
    small[2:3, :] = g_shift
    small[3:4, :] = jnp.sum(g_packed[:, :width].astype(F32), axis=0, keepdims=True)
    small[4:5, :] = jnp.sum(g_packed[:, 2 * width :].astype(F32), axis=0, keepdims=True)
    return g_middle[...] + back


def dec_attn_back_body(
    kept, place, packed, g_att, lse, stream, normed, g_middle, params, inproj, embed, e_low, first,
    go0, go1, gi0, gi1, ge0, ge1, g_enc, small, g_packed, gq_t, rows_f, rows_o, cols, cols_o,
    emb_f, emb_o, g_emb,
):
    rows = stream.shape[0]
    width = stream.shape[1]
    bias = key_bias((place[5], place[6]), kept, rows, True)
    attention_backward(packed, g_att, lse, g_packed, gq_t, bias, width // HEADS2)
    g_stream = project_back(
        place, SCATTER_A, stream[...], normed, g_packed, g_middle, params, inproj, small, first, rows_f, rows_o,
    )
    write_whole(rows_o, g_packed, (gi0, gi1), 0)
    at = lax.broadcasted_iota(jnp.int32, (rows, 1), 0)
    small[8:9, :] = jnp.sum(jnp.where(at == kept, g_stream, 0.0), axis=0, keepdims=True)
    g_embedded = jnp.where(at < kept, g_stream, 0.0).astype(BF)
    small[7:8, :] = jnp.sum(g_embedded.astype(F32), axis=0, keepdims=True)
    g_emb[...] = g_embedded
    g_enc[...] = dot_nt(g_embedded, embed[...])
    emb_f[...] = e_low[...].astype(F32).T
    reorder_rows(place, SCATTER_B, emb_f, emb_o)
    write_halves(emb_o, g_emb, (ge0, ge1))
    cols[...] = small_columns(small)
    reorder_rows(place, SCATTER_A, cols, cols_o)
    n = cols_o.shape[0] // 2
    for core, (gi, go) in enumerate(((gi0, go0), (gi1, go1))):
        gi[:, 3 * width : 4 * width] = go[...]
        gi[:, 4 * width :] = cols_o[core * n : (core + 1) * n, :].astype(BF)


def enc_attn_back_body(
    kept, place, packed, g_att, lse, x, normed, g_middle, params, inproj, first, spots,
    ga0, ga1, gb0, gb1, g_tokens, small, g_packed, gq_t, rows_f, rows_o, cols, cols_o,
):
    rows = x.shape[0]
    width = x.shape[1]
    bias = key_bias((place[5], place[6]), kept, rows, False)
    attention_backward(packed, g_att, lse, g_packed, gq_t, bias, width // HEADS)
    g_stream = project_back(
        place, SCATTER_A, x[...].astype(F32), normed, g_packed, g_middle, params, inproj, small, first,
        rows_f, rows_o,
    )
    n = ga0.shape[1]
    write_halves(rows_o, g_packed, (ga0, ga1), 0, n)
    reorder_rows(place, SCATTER_B, rows_f, rows_o)
    m = 3 * width // 2 - n
    write_halves(rows_o, g_packed, (gb0, gb1), n, m)
    cols[...] = small_columns(small)
    reorder_rows(place, SCATTER_B, cols, cols_o)
    count = cols_o.shape[0] // 2
    block = count // 16
    for core, out in enumerate((gb0, gb1)):
        for k in range(16):
            part = cols_o[core * count + k * block : core * count + (k + 1) * block, :]
            both = jnp.concatenate([part, jnp.zeros_like(part)], axis=0).astype(BF)
            out[k * 2 * block : (k + 1) * 2 * block, m:] = both
    pick = spread_back(spots[...], rows, kept)
    hi, mid, low = split3(g_stream)
    g_tokens[...] = dot_nn(pick, hi) + dot_nn(pick, mid) + dot_nn(pick, low)


def out_feed_body(parts, place, *refs):
    n = 4 * parts
    g_up, g_down = refs[n:]
    units = g_up.shape[1] // parts
    for part in range(parts):
        for x in range(2):
            u_ref, d_ref = refs[4 * part + x], refs[4 * part + 2 + x]
            block, hidden_block = u_ref.shape[0] // 4, d_ref.shape[0] // 4
            for m in range(4):
                dp = place[3] ^ feed_block(4 * x + m)
                at = pl.multiple_of(dp * block, block)
                g_up[pl.ds(at, block), part * units : (part + 1) * units] = u_ref[
                    m * block : (m + 1) * block, :
                ].astype(F32)
                at = pl.multiple_of(part * units + dp * hidden_block, hidden_block)
                g_down[pl.ds(at, hidden_block), :] = d_ref[
                    m * hidden_block : (m + 1) * hidden_block, :
                ].astype(F32)


def out_dec_body(mine, theirs, g_in, g_out, g_gains, g_biases, g_token):
    total = mine[...].astype(F32) + theirs[...].astype(F32)
    n, m = g_in.shape[1], g_in.shape[1] + g_out.shape[1]
    g_in[...] = total[:, :n]
    g_out[...] = total[:, n:m]
    rows = total[:, m:].T
    g_gains[...] = rows[0:2]
    g_biases[...] = rows[2:8]
    g_token[...] = rows[8:9]


def out_halves_body(mine, theirs, out):
    total = mine[...].astype(F32) + theirs[...].astype(F32)
    n, width = out.shape[0], out.shape[1] // 2
    out[:, :width] = total[:n]
    out[:, width:] = total[n:]


def out_enc_body(mine_a, theirs_a, mine_b, theirs_b, g_in, g_gains, g_biases):
    a = mine_a[...].astype(F32) + theirs_a[...].astype(F32)
    b = mine_b[...].astype(F32) + theirs_b[...].astype(F32)
    n, width, cut = g_in.shape[0], g_in.shape[1] // 2, a.shape[1]
    rest = width - cut
    g_in[:, :cut] = a[:n]
    g_in[:, cut:width] = b[:n, :rest]
    g_in[:, width : width + cut] = a[n:]
    g_in[:, width + cut :] = b[n:, :rest]
    rows = b[:n, rest:].T
    g_gains[...] = rows[0:2]
    g_biases[...] = rows[2:7]


def out_bias_body(place, biases, up1, down1, up2, down2):
    lo = 0
    for k, (out, at) in enumerate(((up1, place[7]), (down1, place[4]), (up2, place[7]), (down2, place[4]))):
        n = out.shape[1]
        out[...] = biases[:, pl.ds(pl.multiple_of(lo + at * n, 128), n)]
        lo += 2 * n


def swap(v, axis, distance=1):
    return lax.ppermute(v, axis, [(i, i ^ distance) for i in range(lax.axis_size(axis))])


def add(a, b):
    return (a.astype(F32) + b.astype(F32)).astype(BF)


class Flight:
    def __init__(self, steps):
        self.steps, self.result = steps, None
        self.waits = next(steps)

    def land(self, arrays):
        try:
            self.waits = self.steps.send(arrays)
        except StopIteration as end:
            self.waits, self.result = None, end.value


def land(flights, outs=()):
    flights = [f for f in flights if f.waits is not None]
    outs, arrays = lax.optimization_barrier((outs, [f.waits for f in flights]))
    for flight, landed in zip(flights, arrays):
        flight.land(landed)
    return outs


def finish(flight):
    while flight.waits is not None:
        flight.land(flight.waits)
    return flight.result


def gather_all(v, order):
    for axis, distance in order[:-1]:
        (got,) = yield (swap(v, axis, distance),)
        v = jnp.concatenate([v, got], axis=0)
    (last,) = yield (swap(v, *order[-1]),)
    a, b = yield (swap(v, "tc"), swap(last, "tc"))
    return v, last, a, b


def scatter_all(pair, order):
    own, oth = pair
    (got,) = yield (swap(oth, "tc"),)
    v = add(own, got)
    for axis, distance in order[:-1]:
        half = v.shape[0] // 2
        (got,) = yield (swap(v[half:], axis, distance),)
        v = add(v[:half], got)
    half = v.shape[0] // 2
    (got,) = yield (swap(v[half:], *order[-1]),)
    return v[:half], got


def reduce_feed(parts, x_first):
    one, two = yield (swap(parts[1], "tc"), swap(parts[3], "tc"))
    near, far = add(parts[0], one), add(parts[2], two)
    half = near.shape[0] // 2
    if x_first:
        one, two = yield (swap(near[half:], "dp", 1), swap(far[half:], "dp", 1))
        near, far = add(near[:half], one), add(far[:half], two)
    (got,) = yield (swap(far, "tr"),)
    v = add(near, got)
    for distance in (2, 4) if x_first else (1, 2, 4):
        half = v.shape[0] // 2
        (got,) = yield (swap(v[half:], "dp", distance),)
        v = add(v[:half], got)
    for distance in (4, 2):
        (got,) = yield (swap(v, "dp", distance),)
        v = jnp.concatenate([v, got], axis=0)
    (got,) = yield (swap(v, "dp", 1),)
    return v, got


def reduce_small(v):
    for axis, distance in (("tc", 1),) + SCATTER_A:
        (got,) = yield (swap(v, axis, distance),)
        v = v + got
    return v


def from_far(v):
    (far,) = yield (swap(v, "tr"),)
    (other,) = yield (swap(far, "tc"),)
    return far, other


def near_far(v):
    (far,) = yield (swap(v, "tr"),)
    return far


def near_swap(*arrays):
    got = yield tuple(swap(v, "tc") for v in arrays)
    return got


def chip_axes(order):
    return [{("dp", 4): 0, ("dp", 2): 1, ("dp", 1): 2, ("tr", 1): 3}[step] for step in order]


def cut_gathered(whole, order, halves):
    rows, width = whole.shape
    if halves:
        v = whole.reshape(32, rows // 32, 2, width // 2).transpose(0, 2, 1, 3)
        v = v.reshape(32, rows // 16, width // 2)
    else:
        v = whole.reshape(32, rows // 32, width)
    v = v.reshape((2, 2, 2, 2, 2) + v.shape[1:])
    first = chip_axes(order)
    v = v.transpose(first[3], 4, first[2], first[1], first[0], 5, 6)
    v = v.reshape(2, 2, -1, v.shape[-1])
    return v[0, 0], v[1, 0], v[0, 1], v[1, 1]


def join_scattered(pair, order, halves):
    v = jnp.stack(pair)
    v = v.reshape(2, 2, 2, 2, 2, v.shape[1] // 16, v.shape[2])
    first = chip_axes(order)
    v = v.transpose(*(1 + first.index(k) for k in range(4)), 0, 5, 6)
    v = v.reshape(32, v.shape[5], v.shape[6])
    if halves:
        v = v.reshape(32, 2, v.shape[1] // 2, v.shape[2]).transpose(0, 2, 1, 3)
        v = v.reshape(32, v.shape[1], -1)
    return v.reshape(-1, v.shape[-1])


def call2(body, outs, args, scratch=(), any_args=0, sems=0, us=2):
    count = len(args) - 1 - any_args
    specs = [pl.BlockSpec(memory_space=pltpu.SMEM)]
    specs += [pl.BlockSpec(memory_space=pltpu.VMEM)] * count
    specs += [pl.BlockSpec(memory_space=pl.ANY)] * any_args
    shapes = [pltpu.VMEM(s, d) for s, d in scratch]
    if sems:
        shapes.append(pltpu.SemaphoreType.DMA((sems,)))
    return pl.pallas_call(
        body,
        out_shape=[jax.ShapeDtypeStruct(s, d) for s, d in outs],
        in_specs=specs,
        out_specs=[pl.BlockSpec(memory_space=pltpu.VMEM)] * len(outs),
        scratch_shapes=shapes,
        compiler_params=pltpu.CompilerParams(vmem_limit_bytes=VMEM_BYTES),
        cost_estimate=cost(us),
    )(*args)


class Sentence:
    def __init__(self, place, tokens, mask_pos, cot):
        self.place = place
        span, self.width = tokens.shape
        masks = mask_pos.shape[1]
        self.span, self.kept = span, span - masks
        self.rows = -(-(self.kept + 1) // 16) * 16
        self.width2 = cot.shape[1]
        self.x, self.cot, self.spots = call(
            partial(prep_body, self.kept),
            [((self.rows, self.width), BF), ((self.rows, self.width2), F32), ((span, 1), jnp.int32)],
            [mask_pos.reshape(masks, 1), mask_pos, tokens, cot],
            us=3,
        )

    def enc_attn(self, one_a, one_b):
        rows, width = self.rows, self.width
        self.normed, self.packed, self.att_t, self.lse, self.e_in, self.e_par = call2(
            partial(enc_attn_body, self.kept),
            [((rows, width), BF), ((rows, 3 * width), BF), ((width, rows), BF),
             ((width // 128, rows * (128 * HEADS // width)), F32), ((width, 3 * width), BF),
             ((16, width), F32)],
            [self.place, self.x, *one_a, *one_b],
            scratch=[((width, 128), BF)],
            us=12,
        )

    def enc_feed(self, two, ups, downs, up_bias, down_bias):
        rows, width, hidden = self.rows, self.width, up_bias.shape[1]
        self.e_ups, self.e_downs = ups, downs
        self.middle, self.normed_two, self.active, self.slope, self.e_low, self.e_out, self.embed = call2(
            enc_feed_body,
            [((rows, width), F32), ((rows, width), BF), ((rows, hidden), BF), ((rows, hidden), BF),
             ((rows, width), BF), ((width, width), BF), ((width, self.width2), BF)],
            [self.place, self.x, self.att_t, *two, self.e_par, up_bias, down_bias, *ups, *downs],
            scratch=[((width, hidden), BF), ((hidden, width), BF), ((rows, width), F32)],
            any_args=8,
            sems=8,
            us=15,
        )

    def dec_attn(self, three):
        rows, width = self.rows, self.width2
        (self.stream2, self.normed2, self.packed2, self.att2_t, self.lse2, self.d_in, self.d_out,
         self.d_par) = call2(
            partial(dec_attn_body, self.kept),
            [((rows, width), F32), ((rows, width), BF), ((rows, 3 * width), BF), ((width, rows), BF),
             ((width // 128, rows * (128 * HEADS2 // width)), F32), ((width, 3 * width), BF),
             ((width, width), BF), ((16, width), F32)],
            [self.place, self.e_low, self.embed, *three],
            scratch=[((width, 128), BF)],
            us=11,
        )

    def dec_feed(self, ups, downs, up_bias, down_bias):
        rows, width, hidden = self.rows, self.width2, up_bias.shape[1]
        ff = [((width // 2, hidden // 2), BF)] * 4 + [((hidden // 2, width // 2), BF)] * 4
        (self.output, *g_ff, self.g_middle2, self.g_att2, self.go20, self.go21, self.small2,
         self.biases2) = call2(
            partial(dec_feed_body, self.kept),
            [((self.span, width), F32), *ff, ((rows, width), F32), ((rows, width), BF),
             ((width // 2, width), BF), ((width // 2, width), BF), ((16, width), F32),
             ((1, hidden + width), F32)],
            [self.place, self.stream2, self.att2_t, self.d_out, self.d_par, up_bias, down_bias,
             self.cot, self.spots, *ups, *downs],
            scratch=[((width, hidden), BF), ((hidden, width), BF), ((rows, hidden), BF),
                     ((rows, hidden), BF), ((rows, width), F32), ((rows, width), BF),
                     ((rows, width), BF), ((width, rows), BF), ((width, rows), BF),
                     ((hidden // 2, rows), BF), ((hidden // 2, rows), BF), ((rows, width), BF),
                     ((width, rows), F32), ((width, rows), F32), ((rows, width), BF)],
            any_args=8,
            sems=8,
            us=18,
        )
        return g_ff[:4], g_ff[4:]

    def dec_attn_back(self):
        rows, width = self.rows, self.width2
        gi0, gi1, ge0, ge1, self.g_enc, _ = call2(
            partial(dec_attn_back_body, self.kept),
            [((width // 2, 4 * width + 128), BF)] * 2 + [((self.width, width // 2), BF)] * 2
            + [((rows, self.width), F32), ((16, width), F32)],
            [self.place, self.packed2, self.g_att2, self.lse2, self.stream2, self.normed2,
             self.g_middle2, self.d_par, self.d_in, self.embed, self.e_low, self.small2, self.go20,
             self.go21],
            scratch=[((rows, 3 * width), BF), ((width, rows), BF), ((width, rows), F32),
                     ((width, rows), F32), ((width, 128), F32), ((width, 128), F32),
                     ((self.width, rows), F32), ((self.width, rows), F32), ((rows, width), BF)],
            us=16,
        )
        return (gi0, gi1), (ge0, ge1)

    def _feed_back(self, hidden):
        rows, width = self.rows, self.width
        ff = [((width // 2, hidden // 4), BF)] * 4 + [((hidden // 4, width // 2), BF)] * 4
        scratch = [((width, hidden // 2), BF), ((hidden // 2, width), BF), ((rows, width), BF),
                   ((width, rows), BF), ((width, rows), BF), ((hidden // 4, rows), BF),
                   ((hidden // 4, rows), BF), ((rows, width), BF)]
        return ff, scratch

    def enc_feed_back_one(self):
        rows, width, hidden = self.rows, self.width, self.active.shape[1]
        ff, scratch = self._feed_back(hidden)
        (*g_ff, self.total, self.biases1) = call2(
            enc_feed_back_one_body,
            [*ff, ((rows, width), F32), ((1, hidden + width), F32)],
            [self.place, self.g_enc, self.normed_two, self.active, self.slope, *self.e_ups, *self.e_downs],
            scratch=scratch,
            any_args=8,
            sems=8,
            us=15,
        )
        return g_ff[:4], g_ff[4:]

    def enc_feed_back_two(self):
        rows, width, hidden = self.rows, self.width, self.active.shape[1]
        ff, scratch = self._feed_back(hidden)
        (*g_ff, self.g_middle, self.g_att, go0, go1, self.small, biases) = call2(
            enc_feed_back_two_body,
            [*ff, ((rows, width), F32), ((rows, width), BF), ((width, width // 2), BF),
             ((width, width // 2), BF), ((16, width), F32),
             ((1, self.biases1.shape[1] + self.biases2.shape[1]), F32)],
            [self.place, self.g_enc, self.normed_two, self.active, self.slope, self.total, self.biases1,
             self.biases2, self.middle, self.e_par, self.att_t, self.e_out, *self.e_ups, *self.e_downs],
            scratch=[((rows, width), F32), *scratch, ((width, rows), F32), ((width, rows), F32),
                     ((rows, width), BF)],
            any_args=8,
            sems=8,
            us=19,
        )
        return g_ff[:4], g_ff[4:], (go0, go1), biases

    def enc_attn_back(self, cut):
        rows, width = self.rows, self.width
        n = 3 * width // 2 + 128
        ga0, ga1, gb0, gb1, g_tokens, _ = call2(
            partial(enc_attn_back_body, self.kept),
            [((width, cut), BF)] * 2 + [((width, n - cut), BF)] * 2
            + [((self.span, width), F32), ((16, width), F32)],
            [self.place, self.packed, self.g_att, self.lse, self.x, self.normed, self.g_middle,
             self.e_par, self.e_in, self.small, self.spots],
            scratch=[((rows, 3 * width), BF), ((width, rows), BF), ((width, rows), F32),
                     ((width, rows), F32), ((width, 128), F32), ((width, 128), F32)],
            us=20,
        )
        return (ga0, ga1), (gb0, gb1), g_tokens

    def land(self, flights, names):
        for name, value in zip(names, land(flights, [getattr(self, n) for n in names])):
            setattr(self, name, value)


CUT = 640


def whole_weights(params, inproj, outproj, embed=None):
    columns = jnp.pad(params, ((0, 0), (0, 128 - params.shape[1])))
    if embed is None:
        return (jnp.concatenate([inproj, outproj, columns], axis=1),)
    n, m, k = inproj.shape[1] // 2, outproj.shape[1] // 2, embed.shape[1] // 2
    one_a = [inproj[:, :CUT], inproj[:, n : n + CUT]]
    one_b = [inproj[:, CUT:n], columns, inproj[:, n + CUT :], jnp.zeros_like(columns)]
    two = [outproj[:, :m], embed[:, :k], outproj[:, m:], embed[:, k:]]
    return tuple(jnp.concatenate(v, axis=1) for v in (one_a, one_b, two))


def local(
    tokens_in, valid_len, mask_pos,
    encoder_gains, encoder_biases, encoder_inproj, encoder_outproj,
    encoder_up, encoder_upbias, encoder_down, encoder_downbias,
    embed_weight, mask_token,
    decoder_gains, decoder_biases, decoder_inproj, decoder_outproj,
    decoder_up, decoder_upbias, decoder_down, decoder_downbias,
    cotangent,
):
    dp, tr, tc = (lax.axis_index(a) for a in ALL)
    blocks = tuple(lax.axis_size(a) for a in ALL) == (8, 2, 2)
    width, width2 = tokens_in.shape[1], cotangent.shape[1]
    hidden, hidden2 = 2 * encoder_up.shape[1], 2 * decoder_up.shape[1]
    masked = jnp.sum((mask_pos[0] < valid_len[0]).astype(jnp.int32))
    at = (dp, tr, tc, dp) if blocks else (0, 0, 0, 0)
    place = jnp.stack([jnp.int32(v) for v in (*at, tc, valid_len[0] - masked, masked, tr)])

    biases = [encoder_upbias, decoder_upbias, encoder_downbias, decoder_downbias]
    biases = [v.reshape(1, -1).astype(F32) for v in biases]
    up_biases, down_biases = jnp.concatenate(biases[:2], axis=1), jnp.concatenate(biases[2:], axis=1)
    near = Flight(near_swap(encoder_up, encoder_down, decoder_up, decoder_down, down_biases))
    if blocks:
        weights = call(
            pack_body,
            [((48, CUT), BF), ((48, 3 * width // 2 + 128 - CUT), BF), ((48, width // 2 + width2 // 2), BF),
             ((16, 4 * width2 + 128), BF)],
            [encoder_gains.T, encoder_biases.T, encoder_inproj, encoder_outproj, embed_weight,
             decoder_gains.T, decoder_biases.T, mask_token[None], decoder_inproj, decoder_outproj],
        )
        orders = (GATHER_A, GATHER_B, GATHER_C, GATHER_D)
        one_a, one_b, two, three = (Flight(gather_all(v, o)) for v, o in zip(weights, orders))
        land([one_a, one_b, two, three])
        far_bias, up_far, down_far = land([one_a, one_b, near], (up_biases, encoder_up, encoder_down))
        far_bias, up_far = Flight(near_far(far_bias)), Flight(from_far(up_far))
        land([one_a, one_b, two, far_bias])
        land([one_a, one_b, two, three, up_far])
        down_far = Flight(from_far(down_far))
        land([one_a, one_b, up_far])
        sentence = Sentence(place, tokens_in, mask_pos, cotangent)
        one_a, one_b = one_a.result, one_b.result
    else:
        def whole(v):
            return lax.all_gather(v, ALL, axis=0, tiled=True)

        e_par = whole(jnp.concatenate([encoder_gains, encoder_biases], axis=1))
        d_par = whole(jnp.concatenate([decoder_gains, decoder_biases, mask_token[:, None]], axis=1))
        one_a, one_b, two = whole_weights(
            e_par, whole(encoder_inproj), whole(encoder_outproj), whole(embed_weight)
        )
        (three,) = whole_weights(d_par, whole(decoder_inproj), whole(decoder_outproj))
        one_a, one_b = cut_gathered(one_a, GATHER_A, True), cut_gathered(one_b, GATHER_B, True)
        two = cut_gathered(two, GATHER_C, True)
        three = cut_gathered(three, GATHER_D, False)
        far_bias, up_far, down_far = (
            Flight(near_far(up_biases)), Flight(from_far(encoder_up)), Flight(from_far(encoder_down))
        )
        finish(near), finish(far_bias), finish(up_far)
        sentence = Sentence(place, tokens_in, mask_pos, cotangent)

    e_up, e_down, d_up, d_down, far_down_biases = near.result
    far_biases = far_bias.result
    first = tc == 0

    def row_of(own, far, lo, n, switch):
        own, far = own[:, lo : lo + n], far[:, lo : lo + n]
        pair = jnp.concatenate([own, far], axis=1)
        return jnp.where(first, pair, jnp.concatenate([far, own], axis=1)) if switch else pair

    e_upb = row_of(up_biases, far_biases, 0, hidden // 2, False)
    d_upb = row_of(up_biases, far_biases, hidden // 2, hidden2 // 2, False)
    e_downb = row_of(down_biases, far_down_biases, 0, width // 2, True)
    d_downb = row_of(down_biases, far_down_biases, width // 2, width2 // 2, True)

    gathers = [two, three] if blocks else []
    sentence.enc_attn(one_a, one_b)
    sentence.land([*gathers, down_far], ["att_t", "e_par"])
    dec_up, dec_down = lax.optimization_barrier((decoder_up, decoder_down, sentence.e_par))[:2]
    up_far2 = Flight(from_far(dec_up))
    sentence.land([*gathers[:1], down_far], ["att_t", "e_par"])
    two = two.result if blocks else two
    ups, downs = (encoder_up, e_up, *up_far.result), (encoder_down, e_down, *down_far.result)
    sentence.enc_feed(two, ups, downs, e_upb, e_downb)
    sentence.land([*gathers[1:], up_far2], ["e_low", "embed"])
    dec_down, _ = lax.optimization_barrier((dec_down, sentence.e_low))
    down_far2 = Flight(from_far(dec_down))
    sentence.land([*gathers[1:]], ["e_low", "embed"])
    three = three.result if blocks else three
    sentence.dec_attn(three)
    sentence.land([up_far2, down_far2], ["stream2", "att2_t"])
    sentence.land([down_far2], ["stream2", "att2_t"])
    ups = (decoder_up, d_up, *up_far2.result)
    downs = (decoder_down, d_down, *down_far2.result)
    g_ups2, g_downs2 = sentence.dec_feed(ups, downs, d_upb, d_downb)

    if blocks:
        ff2 = [Flight(reduce_feed(g_ups2, False)), Flight(reduce_feed(g_downs2, True))]
        sentence.land(ff2, ["g_middle2", "g_att2"])
        gi2, ge = sentence.dec_attn_back()
        sentence.land(ff2, ["g_enc"])
        att2 = [Flight(scatter_all(gi2, SCATTER_A)), Flight(scatter_all(ge, SCATTER_B))]
        sentence.land(att2, ["g_enc"])
        g_ups, g_downs = sentence.enc_feed_back_one()
        sentence.land(ff2 + att2, ["total", "biases1"])
        ff_a = [Flight(reduce_feed(g_ups, False)), Flight(reduce_feed(g_downs, True))]
        sentence.land(ff_a, ["total", "biases1"])
        g_ups, g_downs, go, biases = sentence.enc_feed_back_two()
        sentence.land(ff2 + att2 + ff_a, ["g_middle", "g_att", "small"])
        ff_b = [Flight(reduce_feed(g_ups, False)), Flight(reduce_feed(g_downs, True))]
        out, biases = Flight(scatter_all(go, SCATTER_C)), Flight(reduce_small(biases))
        sentence.land([*ff_b, out, biases], ["g_middle", "g_att", "small"])
        ga, gb, g_tokens = sentence.enc_attn_back(CUT)
        (g_tokens,) = land([*ff2, *att2, *ff_a, *ff_b, out, biases], (g_tokens,))
        gi = [Flight(scatter_all(ga, SCATTER_A)), Flight(scatter_all(gb, SCATTER_B))]
        halves2 = [*finish(ff2[0]), *finish(ff2[1])]
        halves = [v for f in (*ff_a, *ff_b) for v in finish(f)]
        biases = finish(biases)
    else:
        gi2, ge = sentence.dec_attn_back()
        g_ups, g_downs = sentence.enc_feed_back_one()
        g_ups_b, g_downs_b, go, biases = sentence.enc_feed_back_two()
        ga, gb, g_tokens = sentence.enc_attn_back(CUT)

        def halves_of(v):
            near, far = add(v[0], swap(v[1], "tc")), add(v[2], swap(v[3], "tc"))
            v = lax.psum(add(near, swap(far, "tr")), "dp")
            return [v[: v.shape[0] // 2], v[v.shape[0] // 2 :]]

        halves2 = halves_of(g_ups2) + halves_of(g_downs2)
        halves = [h for v in (g_ups, g_downs, g_ups_b, g_downs_b) for h in halves_of(v)]
        biases = lax.psum(biases, ALL)

    def feed_out(rows, units, parts, arrays):
        outs = [((rows, units), F32), ((units, rows), F32)]
        return call2(partial(out_feed_body, parts), outs, [place, *arrays])

    g_up2, g_down2 = feed_out(width2 // 2, hidden2 // 2, 1, halves2)
    g_up, g_down = feed_out(width // 2, hidden // 2, 2, halves)
    b_up, b_down, b_up2, b_down2 = call2(
        out_bias_body,
        [((1, hidden // 2), F32), ((1, width // 2), F32), ((1, hidden2 // 2), F32), ((1, width2 // 2), F32)],
        [place, biases],
    )
    if blocks:
        n = width // 32
        n2 = width2 // 32
        g_in2, g_out2, g_gains2, g_biases2, g_token = call(
            out_dec_body,
            [((n2, 3 * width2), F32), ((n2, width2), F32), ((2, n2), F32), ((6, n2), F32), ((1, n2), F32)],
            finish(att2[0]),
        )
        (g_embed,) = call(out_halves_body, [((n, width2), F32)], finish(att2[1]))
        (g_out,) = call(out_halves_body, [((n, width), F32)], finish(out))
        g_in, g_gains, g_biases = call(
            out_enc_body,
            [((n, 3 * width), F32), ((2, n), F32), ((5, n), F32)],
            [*finish(gi[0]), *finish(gi[1])],
        )
        g_gains, g_biases, g_gains2, g_biases2 = g_gains.T, g_biases.T, g_gains2.T, g_biases2.T
        g_token = g_token[0]
    else:
        def scatter(v):
            return lax.psum_scatter(v, ALL, scatter_dimension=0, tiled=True).astype(F32)

        a, b = join_scattered(ga, SCATTER_A, True), join_scattered(gb, SCATTER_B, True)
        m = 3 * width // 2 - CUT
        k = m + 128
        g_in = [a[:, :CUT], b[:, :m], a[:, CUT:], b[:, k : k + m]]
        g_in = scatter(jnp.concatenate(g_in, axis=1))
        small = scatter(b[:, m:k])
        g_gains, g_biases = small[:, :2], small[:, 2:7]
        g_out = scatter(join_scattered(go, SCATTER_C, True))
        g_embed = scatter(join_scattered(ge, SCATTER_B, True))
        v = join_scattered(gi2, SCATTER_A, False)
        g_in2, g_out2 = scatter(v[:, : 3 * width2]), scatter(v[:, 3 * width2 : 4 * width2])
        small = scatter(v[:, 4 * width2 :])
        g_gains2, g_biases2, g_token = small[:, :2], small[:, 2:8], small[:, 8]
    return (
        sentence.output, g_tokens, g_gains, g_biases, g_in, g_out, g_up, b_up[0], g_down, b_down[0],
        g_embed, g_token, g_gains2, g_biases2, g_in2, g_out2, g_up2, b_up2[0], g_down2, b_down2[0],
    )


def solution(mesh):
    rows = P(ALL, None)
    attention = (rows, rows, rows, rows)
    feed = (P("tc", "tr"), P("tr"), P("tr", "tc"), P("tc"))
    in_specs = (
        (rows, P(ALL), rows) + attention + feed + (rows, P(ALL)) + attention + feed + (rows,)
    )
    out_specs = (rows, rows) + attention + feed + (rows, P(ALL)) + attention + feed
    return jax.shard_map(local, mesh=mesh, in_specs=in_specs, out_specs=out_specs, check_vma=False)
```

```python
import math
from functools import partial

import jax
import jax.numpy as jnp
from jax import lax
from jax.experimental import pallas as pl
from jax.experimental.pallas import tpu as pltpu
from jax.sharding import PartitionSpec as P

HEADS = 12
HEADS2 = 16
ALL = ("dp", "tr", "tc")
EPS = 1e-06
MASKED = -1e30
LOG2E = math.log2(math.e)
F32 = jnp.float32
BF = jnp.bfloat16
SPARE_BYTES = 12 * 1024 * 1024
LAST = 0.01
WHOLE_BYTES = 58 * 1024 * 1024


def dot_nn(a, b):
    return lax.dot_general(a, b, (((1,), (0,)), ((), ())), preferred_element_type=F32)


def dot_nt(a, b):
    return lax.dot_general(a, b, (((1,), (1,)), ((), ())), preferred_element_type=F32)


def cost(us):
    return pl.CostEstimate(flops=int(us * 1e9), bytes_accessed=int(us * 3e6), transcendentals=0)


def vmem(arrays):
    total = sum(math.prod(s) * jnp.dtype(d).itemsize for s, d in arrays)
    return pltpu.CompilerParams(vmem_limit_bytes=SPARE_BYTES + total)


SAVES = []


def save(ref, columns=None):
    for entry in SAVES[-1]:
        if entry["buffer"] is ref:
            source, target = ref, entry["out"]
            if columns is not None:
                source, target = source.at[:, columns], target.at[:, columns]
            pltpu.make_async_copy(source, target, entry["sem"]).start()
            entry["started"] = True


def call(body, outs, args, scratch=(), smem=0, hbm_args=0, sems=0, keep=(), us=2, alone=False):
    count = len(args) - smem - hbm_args
    specs = [pl.BlockSpec(memory_space=pltpu.SMEM)] * smem
    specs += [pl.BlockSpec(memory_space=pltpu.VMEM)] * count
    specs += [pl.BlockSpec(memory_space=pltpu.HBM)] * hbm_args
    buffers = [outs[k] for k in keep]
    shapes = [pltpu.VMEM(s, d) for s, d in [*buffers, *scratch]]
    shapes += [pltpu.SemaphoreType.DMA((max(n, 1),)) for n in (len(keep), sems)]

    def kernel(*refs):
        ins, rest = refs[: len(args)], refs[len(args) :]
        results, rest = list(rest[: len(outs)]), rest[len(outs) :]
        own, keep_sems, own_sems = rest[:-2], rest[-2], rest[-1]
        entries = []
        for n, k in enumerate(keep):
            entries.append({"buffer": own[n], "out": results[k], "sem": keep_sems.at[n], "started": False})
            results[k] = own[n]
        SAVES.append(entries)
        body(*ins, *results, *own[len(keep) :], *((own_sems,) if sems else ()))
        SAVES.pop()
        for entry in entries:
            copy = pltpu.make_async_copy(entry["buffer"], entry["out"], entry["sem"])
            if not entry["started"]:
                copy.start()
        for entry in entries:
            pltpu.make_async_copy(entry["buffer"], entry["out"], entry["sem"]).wait()

    spaces = [pltpu.HBM if k in keep else pltpu.VMEM for k in range(len(outs))]
    return pl.pallas_call(
        kernel,
        out_shape=[jax.ShapeDtypeStruct(s, d) for s, d in outs],
        in_specs=specs,
        out_specs=[pl.BlockSpec(memory_space=space) for space in spaces],
        scratch_shapes=shapes,
        compiler_params=pltpu.CompilerParams(vmem_limit_bytes=WHOLE_BYTES) if alone else vmem([*buffers, *scratch]),
        cost_estimate=cost(us),
    )(*args)


def norm_parts(v):
    center = v - jnp.mean(v, axis=-1, keepdims=True)
    r = lax.rsqrt(jnp.mean(center * center, axis=-1, keepdims=True) + EPS)
    return center * r, r


def norm_back(u, r, gain, y):
    e = y * gain
    back = r * (e - jnp.mean(e, axis=-1, keepdims=True) - u * jnp.mean(e * u, axis=-1, keepdims=True))
    return back, jnp.sum(y * u, axis=0, keepdims=True), jnp.sum(y, axis=0, keepdims=True)


def split3(v):
    hi = v.astype(BF)
    rest = v - hi.astype(F32)
    mid = rest.astype(BF)
    return hi, mid, (rest - mid.astype(F32)).astype(BF)


def head_masks(head_size):
    lane = lax.broadcasted_iota(jnp.int32, (1, 128), 1) // head_size
    return [(lane == h).astype(F32).astype(BF) for h in range(128 // head_size)]


def stack_heads(rows, masks):
    return jnp.concatenate([rows * m for m in masks], axis=0)


def prep_body(kept, mp_col, mp_row, tokens, cot, x_out, cot_out, place_out):
    rows, span = x_out.shape[0], tokens.shape[0]
    wide = lax.broadcasted_iota(jnp.int32, (mp_col.shape[0], span), 1)
    below = jnp.sum((mp_col[...] < wide).astype(F32), axis=0, keepdims=True)
    here = jnp.sum((mp_col[...] == wide).astype(F32), axis=0, keepdims=True)
    place = jnp.where(here > 0, kept, wide[:1] - below.astype(jnp.int32))
    pick = lax.broadcasted_iota(jnp.int32, (rows, span), 0) == place
    pick_f = pick.astype(F32)
    cot_out[...] = dot_nn(pick_f.astype(BF), cot[...])
    keep = lax.broadcasted_iota(jnp.int32, (rows, span), 0) < kept
    x_out[...] = dot_nn(jnp.where(keep, pick_f, 0.0).astype(BF), tokens[...]).astype(BF)
    tall = lax.broadcasted_iota(jnp.int32, (span, mp_row.shape[1]), 0)
    below_t = jnp.sum((mp_row[...] < tall).astype(F32), axis=1, keepdims=True)
    here_t = jnp.sum((mp_row[...] == tall).astype(F32), axis=1, keepdims=True)
    place_out[...] = jnp.where(here_t > 0, kept, tall[:, :1] - below_t.astype(jnp.int32))


def spread_back(place, rows, limit):
    at = lax.broadcasted_iota(jnp.int32, (place.shape[0], rows), 1)
    return jnp.where(at < limit, (at == place).astype(F32), 0.0).astype(BF)


def key_bias(lens, kept, rows, with_mask_row):
    at = lax.broadcasted_iota(jnp.int32, (rows, 1), 0)
    bias = jnp.where(at < lens[0], 0.0, MASKED)
    if with_mask_row:
        count = jnp.full((rows, 1), lens[1], jnp.int32).astype(F32)
        bias = jnp.where(at == kept, jnp.log(count) * LOG2E, bias)
    return bias


def attention_forward(packed, att_t, lse, bias, head_size):
    width = packed.shape[1] // 3
    rows = packed.shape[0]
    masks = head_masks(head_size)
    scale = head_size**-0.5 * LOG2E

    def group(g, carry):
        at = pl.multiple_of(g * 128, 128)
        q = packed[:, pl.ds(at, 128)]
        k = packed[:, pl.ds(width + at, 128)]
        v_t = packed[:, pl.ds(2 * width + at, 128)].T
        scores = dot_nt(k, stack_heads(q, masks)) * scale + bias
        peak = jnp.max(scores, axis=0, keepdims=True)
        weights = jnp.exp2(scores - peak)
        total = jnp.sum(weights, axis=0, keepdims=True)
        out = dot_nn(v_t, weights.astype(BF)) * (1.0 / total)
        for h in range(len(masks)):
            block = out[h * head_size : (h + 1) * head_size, h * rows : (h + 1) * rows]
            att_t[pl.ds(at + h * head_size, head_size), :] = block.astype(BF)
        lse[pl.ds(g, 1), :] = peak + jnp.log(total) * LOG2E
        return carry

    lax.fori_loop(0, width // 128, group, 0)


def attention_backward(packed, g_att, lse, g_packed, gq_t, bias, head_size):
    width = packed.shape[1] // 3
    rows = packed.shape[0]
    masks = head_masks(head_size)
    scale = head_size**-0.5

    def group(g, carry):
        at = pl.multiple_of(g * 128, 128)
        q = packed[:, pl.ds(at, 128)]
        k = packed[:, pl.ds(width + at, 128)]
        v = packed[:, pl.ds(2 * width + at, 128)]
        q_s = stack_heads(q, masks)
        g_s = stack_heads(g_att[:, pl.ds(at, 128)], masks)
        scores = dot_nt(k, q_s) * (scale * LOG2E) + bias
        probs = jnp.exp2(scores - lse[pl.ds(g, 1), :])
        g_v = dot_nn(probs.astype(BF), g_s)
        g_probs = dot_nt(v, g_s)
        delta = jnp.sum(g_probs * probs, axis=0, keepdims=True)
        g_scores = (probs * (g_probs - delta)).astype(BF)
        g_k = dot_nn(g_scores, q_s) * scale
        out = dot_nn(k.T, g_scores) * scale
        for h in range(len(masks)):
            block = out[h * head_size : (h + 1) * head_size, h * rows : (h + 1) * rows]
            gq_t[pl.ds(at + h * head_size, head_size), :] = block.astype(BF)
        g_packed[:, pl.ds(width + at, 128)] = g_k.astype(BF)
        g_packed[:, pl.ds(2 * width + at, 128)] = g_v.astype(BF)
        return carry

    lax.fori_loop(0, width // 128, group, 0)
    g_packed[:, :width] = gq_t[...].T


def project_in(stream, params, inproj, normed_out, packed_out):
    u, r = norm_parts(stream)
    normed = (u * params[0:1, :] + params[2:3, :]).astype(BF)
    normed_out[...] = normed
    save(normed_out)
    width = stream.shape[1]
    step = 256
    for part in range(3):
        for at in range(0, width, step):
            lo = part * width + at
            value = dot_nn(normed, inproj[:, lo : lo + step])
            if part == 0:
                value = value + params[3:4, at : at + step]
            if part == 2:
                value = value + params[4:5, at : at + step]
            packed_out[:, lo : lo + step] = value.astype(BF)
    save(packed_out)


GATHER_A = (("tr", 1), ("dp", 4), ("dp", 2), ("dp", 1))
GATHER_B = (("tr", 1), ("dp", 4), ("dp", 1), ("dp", 2))
GATHER_C = (("tr", 1), ("dp", 4), ("dp", 2), ("dp", 1))
GATHER_D = (("tr", 1), ("dp", 4), ("dp", 1), ("dp", 2))
SCATTER_A = (("dp", 1), ("tr", 1), ("dp", 2), ("dp", 4))
SCATTER_B = (("tr", 1), ("dp", 1), ("dp", 2), ("dp", 4))
FEED = (("dp", 1), ("dp", 2), ("dp", 4))


def differences(order, bits):
    dp = tr = 0
    for (axis, distance), bit in zip(order, bits):
        if axis == "dp":
            dp = dp + distance * bit
        else:
            tr = tr + bit
    return dp, tr


def gathered_block(order, j, last):
    return differences(order, (j & 1, (j >> 1) & 1, (j >> 2) & 1, last))


def scattered_block(order, m):
    return differences(order, (m >> 3, (m >> 2) & 1, (m >> 1) & 1, m & 1))


def feed_block(m):
    return differences(FEED, (m >> 2, (m >> 1) & 1, m & 1))[0]


def place_rows(place, order, sources, block, put):
    first = place[2] == 0
    for x in range(2):
        own_ref, oth_ref = sources[x], sources[2 + x]
        count = own_ref.shape[0] // block

        def one(j, carry, own_ref=own_ref, oth_ref=oth_ref, x=x):
            dp, tr = gathered_block(order, j, x)
            chip = (place[0] ^ dp) * 2 + (place[1] ^ tr)
            at = pl.multiple_of(j * block, block)
            own = own_ref[pl.ds(at, block), :].astype(F32)
            oth = oth_ref[pl.ds(at, block), :].astype(F32)
            put(chip, jnp.where(first, own, oth), jnp.where(first, oth, own))
            return carry

        lax.fori_loop(0, count, one, 0)


def place_halves(place, order, sources, cuts):
    block = sources[0].shape[0] // 8
    half = block // 2

    def put(chip, low, high):
        at = pl.multiple_of(chip * block, block)
        top = jnp.concatenate([low[:half], high[:half]], axis=0).astype(BF)
        bottom = jnp.concatenate([low[half:], high[half:]], axis=0).astype(BF)
        lo = 0
        for target, first, width, shift in cuts:
            target[pl.ds(at, block), first : first + width] = top[:, lo : lo + width]
            if shift is not None:
                right = first + shift
                target[pl.ds(at, block), right : right + width] = bottom[:, lo : lo + width]
            lo += width

    place_rows(place, order, sources, block, put)


def place_whole(place, order, sources, cuts):
    block = sources[0].shape[0] // 8

    def put(chip, low, high):
        at = pl.multiple_of(chip * 2 * block, 2 * block)
        both = jnp.concatenate([low, high], axis=0).astype(BF)
        lo = 0
        for target, width in cuts:
            target[pl.ds(at, 2 * block), :] = both[:, lo : lo + width]
            lo += width

    place_rows(place, order, sources, block, put)


def param_rows(columns):
    return columns[...].astype(F32).T[:16]


def reorder_rows(place, order, source, target):
    block = source.shape[0] // 32
    for core in range(2):
        for m in range(16):
            dp, tr = scattered_block(order, m)
            device = ((place[0] ^ dp) * 2 + (place[1] ^ tr)) * 2 + (place[2] ^ core)
            at = pl.multiple_of(device * block, 8)
            to = (core * 16 + m) * block
            target[to : to + block, :] = source[pl.ds(at, block), :]


def write_halves(ordered, columns, outs, first=0, count=None):
    half_rows = ordered.shape[0] // 2
    block = half_rows // 16
    width = columns.shape[1] // 2
    count = width if count is None else count
    step = max(n for n in (384, 320, 256) if count % n == 0) if count != 640 else 640
    for core in range(2):
        rows = ordered[core * half_rows : (core + 1) * half_rows, :].astype(BF)
        for at in range(first, first + count, step):
            left = dot_nn(rows, columns[:, at : at + step])
            right = dot_nn(rows, columns[:, width + at : width + at + step])
            for m in range(16):
                both = [left[m * block : (m + 1) * block], right[m * block : (m + 1) * block]]
                outs[core][m * 2 * block : (m + 1) * 2 * block, at - first : at - first + step] = (
                    jnp.concatenate(both, axis=0).astype(BF)
                )


def write_whole(ordered, columns, outs, lo):
    half_rows = ordered.shape[0] // 2
    width = columns.shape[1]
    for core in range(2):
        rows = ordered[core * half_rows : (core + 1) * half_rows, :].astype(BF)
        for at in range(0, width, 256):
            outs[core][:, lo + at : lo + at + 256] = dot_nn(rows, columns[:, at : at + 256]).astype(BF)


def small_columns(small):
    table = jnp.concatenate([small[...], jnp.zeros((112, small.shape[1]), F32)], axis=0)
    return table.T


def pack_body(
    e_gains, e_biases, e_in, e_out, embed, d_gains, d_biases, token, d_in, d_out, one, two, three
):
    def columns(parts):
        total, lo = 0.0, 0
        for part in parts:
            count, rows = part.shape
            spot = lax.broadcasted_iota(jnp.int32, (count, 128), 1)
            want = lax.broadcasted_iota(jnp.int32, (count, 128), 0) + lo
            table = (spot == want).astype(F32).astype(BF)
            total = total + lax.dot_general(
                part[...], table, (((0,), (0,)), ((), ())), preferred_element_type=F32
            )
            lo += count
        return total

    e_par = columns([e_gains, e_biases])

    def halves(v):
        v = v[...].astype(F32)
        width = v.shape[1] // 2
        return jnp.concatenate([v[:, :width], v[:, width:]], axis=0).astype(BF)

    n = e_in.shape[1] // 2
    one[:, :n] = halves(e_in)
    one[:, n:] = jnp.concatenate([e_par, jnp.zeros_like(e_par)], axis=0).astype(BF)
    n = e_out.shape[1] // 2
    two[:, :n] = halves(e_out)
    two[:, n:] = halves(embed)
    n = d_in.shape[1]
    m = n + d_out.shape[1]
    three[:, :n] = d_in[...]
    three[:, n:m] = d_out[...]
    three[:, m:] = columns([d_gains, d_biases, token]).astype(BF)


def enc_attn_body(
    kept, place, x, s0, s1, s2, s3, r0, r1, r2, r3,
    normed, packed, att_t, lse, inproj, par_t, par_c,
):
    width = x.shape[1]
    n, shift = s0.shape[1], 3 * width // 2
    place_halves(place, GATHER_A, (s0, s1, s2, s3), ((inproj, 0, n, shift),))
    place_halves(
        place, GATHER_B, (r0, r1, r2, r3), ((inproj, n, shift - n, shift), (par_c, 0, 128, None))
    )
    save(inproj)
    par_t[...] = param_rows(par_c)
    project_in(x[...].astype(F32), par_t, inproj, normed, packed)
    bias = key_bias((place[5], place[6]), kept, x.shape[0], False)
    attention_forward(packed, att_t, lse, bias, width // HEADS)


def dec_attn_body(
    kept, place, e_low, embed, s0, s1, s2, s3,
    stream, normed, packed, att_t, lse, inproj, outproj, params, par_c,
):
    rows = e_low.shape[0]
    width = stream.shape[1]
    place_whole(
        place, GATHER_D, (s0, s1, s2, s3), ((inproj, 3 * width), (outproj, width), (par_c, 128))
    )
    save(inproj)
    save(outproj)
    params[...] = param_rows(par_c)
    embedded = dot_nn(e_low[...], embed[...]) + params[7:8, :]
    at = lax.broadcasted_iota(jnp.int32, (rows, 1), 0)
    decoded = jnp.where(at < kept, embedded, params[8:9, :])
    stream[...] = decoded
    save(stream)
    project_in(decoded, params, inproj, normed, packed)
    bias = key_bias((place[5], place[6]), kept, rows, True)
    attention_forward(packed, att_t, lse, bias, width // HEADS2)


def pack_feed_body(up, up_bias, down, down_bias, out):
    rows, width = up.shape[0], down.shape[1]
    out[:rows, :] = up[...]
    for at in range(0, up.shape[1], width):
        out[rows : 2 * rows, at : at + width] = down[at : at + width, :]
    row = lax.broadcasted_iota(jnp.int32, (16, up.shape[1]), 0)
    value = jnp.where(row == 0, up_bias[...].astype(F32), 0.0)
    out[2 * rows :, :] = value.astype(BF)
    row = lax.broadcasted_iota(jnp.int32, (16, width), 0)
    value = jnp.where(row == 1, down_bias[...].astype(F32), value[:, :width])
    out[2 * rows :, :width] = value.astype(BF)


def load_feed(place, gathered, up, down, sems, part=0, biases=None):
    copies = []
    half = up.shape[0] // 2
    units = up.shape[1] // 2
    block = gathered.shape[0] // 4

    def start(source, target):
        copies.append(pltpu.make_async_copy(source, target, sems.at[len(copies)]))
        copies[-1].start()

    for tr in range(2):
        for core in range(2):
            base = ((place[7] ^ tr) * 2 + core) * block

            def rows(at, count, base=base):
                return pl.ds(pl.multiple_of(base + at, 16), count)

            columns = pl.ds(tr * units, units)
            start(
                gathered.at[rows(0, half), pl.ds(part * units, units)],
                up.at[pl.ds(core * half, half), columns],
            )
            for at in range(0, units, half):
                start(
                    gathered.at[rows(half, half), pl.ds(part * units + at, half)],
                    down.at[pl.ds(tr * units + at, half), pl.ds(core * half, half)],
                )
            if biases is not None:
                start(gathered.at[rows(2 * half, 16), :], biases.at[2 * tr + core])
    return copies


def bias_rows(biases, half):
    up = jnp.concatenate([biases[0, 0:1, :], biases[2, 0:1, :]], axis=1)
    down = jnp.concatenate([biases[0, 1:2, :half], biases[1, 1:2, :half]], axis=1)
    return up.astype(F32), down.astype(F32)


def middle_of(stream, att_t, outproj, params):
    return stream + dot_nn(att_t[...].T, outproj[...]) + params[5:6, :]


def feed_forward(normed_two, up, up_bias, down, active_out, slope_out, total, step):
    hidden_units = up.shape[1]
    total[...] = jnp.zeros_like(total)

    def chunk(c, carry):
        at = pl.multiple_of(c * step, step)
        hidden = dot_nn(normed_two, up[:, pl.ds(at, step)]) + up_bias[:, pl.ds(at, step)]
        phi = 0.5 * (1.0 + lax.erf(hidden * math.sqrt(0.5)))
        bell = jnp.exp2(hidden * hidden * (-0.5 * LOG2E)) * (1.0 / math.sqrt(2 * math.pi))
        active = (hidden * phi).astype(BF)
        active_out[:, pl.ds(at, step)] = active
        slope_out[:, pl.ds(at, step)] = (phi + hidden * bell).astype(BF)
        save(active_out, pl.ds(at, step))
        save(slope_out, pl.ds(at, step))
        total[...] += dot_nn(active, down[pl.ds(at, step), :])
        return carry

    lax.fori_loop(0, hidden_units // step, chunk, 0)


def order_feed(place, source, target):
    block = source.shape[0] // 16
    for core in range(2):
        for m in range(8):
            at = ((place[4] ^ core) * 8 + (place[3] ^ feed_block(m))) * block
            to = (core * 8 + m) * block
            target[to : to + block, :] = source[pl.ds(pl.multiple_of(at, block), block), :]


def feed_backward(
    place, part, parts, g_result, normed_two, active, slope, up, down,
    g_ups, g_downs, g_upbias, g_normed, step, rows_t, ordered_n, ordered_g,
):
    width = normed_two.shape[1]
    count = up.shape[1] // 2
    units = count * parts
    half = width // 2
    rows_t[...] = normed_two[...].T
    order_feed(place, rows_t, ordered_n)
    rows_t[...] = g_result[...].T
    order_feed(place, rows_t, ordered_g)
    for tr in range(2):
        base = tr * units + part * count
        out_base = pl.multiple_of((place[7] ^ tr) * units + part * count, 128)

        def chunk(c, carry, tr=tr, base=base, out_base=out_base):
            at = pl.multiple_of(c * step, step)
            here = pl.ds(pl.multiple_of(tr * count + at, 128), step)
            g_active = dot_nt(g_result[...], down[here, :]).astype(BF).astype(F32)
            there = pl.ds(pl.multiple_of(base + at, 128), step)
            g_hidden = (slope[:, there].astype(F32) * g_active).astype(BF)
            g_upbias[:, pl.ds(pl.multiple_of(out_base + at, 128), step)] = jnp.sum(
                g_hidden.astype(F32), axis=0, keepdims=True
            )
            g_normed[...] += dot_nt(g_hidden, up[:, here])
            g_up = dot_nn(ordered_n[...], g_hidden).astype(BF)
            g_down = dot_nn(ordered_g[...], active[:, there]).astype(BF)
            for core in range(2):
                g_ups[2 * tr + core][:, pl.ds(at, step)] = g_up[core * half : (core + 1) * half]
                g_downs[2 * tr + core][:, pl.ds(at, step)] = g_down[core * half : (core + 1) * half]
            return carry

        lax.fori_loop(0, count // step, chunk, 0)


def after_feed_backward(
    place, order, g_out, g_normed, middle, params, att_t, outproj, g_middle, g_att, small, att_f, att_o
):
    u, r = norm_parts(middle)
    y = g_normed.astype(BF).astype(F32)
    back, g_gain, g_shift = norm_back(u, r, params[1:2, :], y)
    grad = g_out + back
    g_middle[...] = grad
    branch = grad.astype(BF)
    att_f[...] = att_t[...].astype(F32)
    reorder_rows(place, order, att_f, att_o)
    g_att[...] = dot_nt(branch, outproj[...]).astype(BF)
    small[1:2, :] = g_gain
    small[5:6, :] = jnp.sum(branch.astype(F32), axis=0, keepdims=True)
    small[6:7, :] = g_shift
    return branch


def enc_feed_body(
    place, x, att_t, s0, s1, s2, s3, params, weights,
    middle, normed_two, active, slope, e_low, outproj, embed,
    up, down, total, biases, up_bias, sems,
):
    copies = load_feed(place, weights, up, down, sems, 0, biases)
    width = x.shape[1]
    n, m = width // 2, embed.shape[1] // 2
    place_halves(place, GATHER_C, (s0, s1, s2, s3), ((outproj, 0, n, n), (embed, 0, m, m)))
    mid = middle_of(x[...].astype(F32), att_t, outproj, params)
    middle[...] = mid
    u, r = norm_parts(mid)
    n2 = (u * params[1:2, :] + params[6:7, :]).astype(BF)
    normed_two[...] = n2
    for ref in (middle, normed_two, outproj, embed):
        save(ref)
    for copy in copies:
        copy.wait()
    up_bias[...], down_bias = bias_rows(biases, width // 2)
    feed_forward(n2, up, up_bias, down, active, slope, total, 512)
    result = (total[...] + down_bias).astype(BF)
    e_low[...] = (middle[...] + result.astype(F32)).astype(BF)


def dec_feed_body(
    kept, place, stream, att_t, outproj, params, cot, weights,
    out, gu0, gu1, gu2, gu3, gd0, gd1, gd2, gd3, g_middle, g_att, go0, go1, small, g_biases,
    up, down, active, slope, total, n2_s, g_res, rows_t, ordered_n, ordered_g,
    att_f, att_o, branch_s, biases, up_bias, sems,
):
    copies = load_feed(place, weights, up, down, sems, 0, biases)
    mid = middle_of(stream[...], att_t, outproj, params)
    u, r = norm_parts(mid)
    n2 = (u * params[1:2, :] + params[6:7, :]).astype(BF)
    n2_s[...] = n2
    for copy in copies:
        copy.wait()
    up_bias[...], down_bias = bias_rows(biases, up.shape[0] // 2)
    feed_forward(n2, up, up_bias, down, active, slope, total, 512)
    result = (total[...] + down_bias).astype(BF)
    out[...] = mid + result.astype(F32)
    save(out)
    g_out = cot[...]
    g_res[...] = g_out.astype(BF)
    small[...] = jnp.zeros_like(small)
    units = up.shape[1]
    g_biases[:, units:] = jnp.sum(g_res[...].astype(F32), axis=0, keepdims=True)
    total[...] = jnp.zeros_like(total)
    feed_backward(
        place, 0, 1, g_res, n2_s, active, slope, up, down, (gu0, gu1, gu2, gu3), (gd0, gd1, gd2, gd3),
        g_biases, total, 512, rows_t, ordered_n, ordered_g,
    )
    branch = after_feed_backward(
        place, SCATTER_B, g_out, total[...], mid, params, att_t, outproj, g_middle, g_att, small,
        att_f, att_o,
    )
    branch_s[...] = branch
    write_whole(att_o, branch_s, (go0, go1), 0)


def enc_feed_back_one_body(
    place, g_enc, normed_two, active, slope, weights,
    gu0, gu1, gu2, gu3, gd0, gd1, gd2, gd3, total, biases, up, down, g_res, rows_t, ordered_n, ordered_g, sems,
):
    copies = load_feed(place, weights, up, down, sems)
    g_res[...] = g_enc[...].astype(BF)
    total[...] = jnp.zeros_like(total)
    biases[:, 2 * up.shape[1] :] = jnp.sum(g_res[...].astype(F32), axis=0, keepdims=True)
    for copy in copies:
        copy.wait()
    feed_backward(
        place, 0, 2, g_res, normed_two, active, slope, up, down, (gu0, gu1, gu2, gu3),
        (gd0, gd1, gd2, gd3), biases, total, 384, rows_t, ordered_n, ordered_g,
    )


def enc_feed_back_two_body(
    place, g_enc, normed_two, active, slope, total_in, biases_in, biases_dec, middle, params, att_t,
    outproj, weights,
    gu0, gu1, gu2, gu3, gd0, gd1, gd2, gd3, g_middle, g_att, go0, go1, small, biases,
    total, up, down, g_res, rows_t, ordered_n, ordered_g, att_f, att_o, branch_s, sems,
):
    copies = load_feed(place, weights, up, down, sems, 1)
    g_res[...] = g_enc[...].astype(BF)
    total[...] = total_in[...]
    count = biases_in.shape[1]
    biases[:, :count] = biases_in[...]
    biases[:, count:] = biases_dec[...]
    small[...] = jnp.zeros_like(small)
    for copy in copies:
        copy.wait()
    feed_backward(
        place, 1, 2, g_res, normed_two, active, slope, up, down, (gu0, gu1, gu2, gu3),
        (gd0, gd1, gd2, gd3), biases, total, 384, rows_t, ordered_n, ordered_g,
    )
    branch = after_feed_backward(
        place, SCATTER_A, g_enc[...], total[...], middle[...], params, att_t, outproj, g_middle,
        g_att, small, att_f, att_o,
    )
    branch_s[...] = branch
    write_halves(att_o, branch_s, (go0, go1))


def project_back(
    place, order, stream, normed, g_packed, g_middle, params, inproj, small, first, rows_f, rows_o
):
    width = stream.shape[1]
    rows_f[...] = normed[...].astype(F32).T
    reorder_rows(place, order, rows_f, rows_o)
    g_normed = dot_nt(g_packed[...], inproj[...])
    u, r = norm_parts(stream)
    back, g_gain, g_shift = norm_back(u, r, params[0:1, :], g_normed)
    small[...] = first[...]
    small[0:1, :] = g_gain
    small[2:3, :] = g_shift
    small[3:4, :] = jnp.sum(g_packed[:, :width].astype(F32), axis=0, keepdims=True)
    small[4:5, :] = jnp.sum(g_packed[:, 2 * width :].astype(F32), axis=0, keepdims=True)
    return g_middle[...] + back


def dec_attn_back_body(
    kept, place, packed, g_att, lse, stream, normed, g_middle, params, inproj, embed, e_low, first,
    go0, go1, ga0, ga1, gb0, gb1, g_enc, small, g_packed, gq_t, rows_f, rows_o, cols, cols_o,
    emb_f, emb_o, g_emb,
):
    rows = stream.shape[0]
    width = stream.shape[1]
    bias = key_bias((place[5], place[6]), kept, rows, True)
    attention_backward(packed, g_att, lse, g_packed, gq_t, bias, width // HEADS2)
    g_stream = project_back(
        place, SCATTER_A, stream[...], normed, g_packed, g_middle, params, inproj, small, first,
        rows_f, rows_o,
    )
    write_whole(rows_o, g_packed, (ga0, ga1), 0)
    at = lax.broadcasted_iota(jnp.int32, (rows, 1), 0)
    small[8:9, :] = jnp.sum(jnp.where(at == kept, g_stream, 0.0), axis=0, keepdims=True)
    g_embedded = jnp.where(at < kept, g_stream, 0.0).astype(BF)
    small[7:8, :] = jnp.sum(g_embedded.astype(F32), axis=0, keepdims=True)
    g_emb[...] = g_embedded
    g_enc[...] = dot_nt(g_embedded, embed[...])
    emb_f[...] = e_low[...].astype(F32).T
    reorder_rows(place, SCATTER_B, emb_f, emb_o)
    cols[...] = small_columns(small)
    reorder_rows(place, SCATTER_B, cols, cols_o)
    n = cols_o.shape[0] // 2
    half = emb_o.shape[0] // 2
    block, part = half // 16, g_emb.shape[1] // 2
    unit = n // 16
    for core, (gb, go) in enumerate(((gb0, go0), (gb1, go1))):
        gb[:, :width] = go[...]
        gb[:, width : width + 128] = cols_o[core * n : (core + 1) * n, :].astype(BF)
        rows_e = emb_o[core * half : (core + 1) * half, :].astype(BF)
        left, right = dot_nn(rows_e, g_emb[:, :part]), dot_nn(rows_e, g_emb[:, part:])
        for m in range(16):
            both = [left[m * block : (m + 1) * block], right[m * block : (m + 1) * block]]
            both = jnp.concatenate(both, axis=0).astype(BF)
            for k in range(2 * block // unit):
                lo = width + 128 + k * part
                gb[m * unit : (m + 1) * unit, lo : lo + part] = both[k * unit : (k + 1) * unit]


def enc_attn_back_one_body(kept, place, packed, g_att, lse, g_packed, gq_t):
    bias = key_bias((place[5], place[6]), kept, packed.shape[0], False)
    attention_backward(packed, g_att, lse, g_packed, gq_t, bias, g_att.shape[1] // HEADS)


def enc_attn_back_two_body(
    place, g_packed, x, normed, g_middle, params, inproj, first, go0, go1,
    ga0, ga1, gb0, gb1, g_stream, small, rows_f, rows_o, cols, cols_o,
):
    width = x.shape[1]
    g_stream[...] = project_back(
        place, SCATTER_A, x[...].astype(F32), normed, g_packed, g_middle, params, inproj, small, first,
        rows_f, rows_o,
    )
    m = gb0.shape[1] - 128
    n = 3 * width // 2 - m
    write_halves(rows_o, g_packed, (ga0, ga1), 0, n)
    reorder_rows(place, SCATTER_B, rows_f, rows_o)
    write_halves(rows_o, g_packed, (gb0, gb1), n, m)
    cols[...] = small_columns(small)
    reorder_rows(place, SCATTER_B, cols, cols_o)
    count = cols_o.shape[0] // 2
    block = count // 16
    for core, (a, b, go) in enumerate(((ga0, gb0, go0), (ga1, gb1, go1))):
        a[:, n:] = go[...]
        for k in range(16):
            part = cols_o[core * count + k * block : core * count + (k + 1) * block, :]
            both = jnp.concatenate([part, jnp.zeros_like(part)], axis=0).astype(BF)
            b[k * 2 * block : (k + 1) * 2 * block, m:] = both


def spread_body(kept, spots, out, g_stream, output, g_tokens):
    rows = out.shape[0]
    for limit, source, target in ((kept + 1, out, output), (kept, g_stream, g_tokens)):
        pick = spread_back(spots[...], rows, limit)
        hi, mid, low = split3(source[...])
        target[...] = dot_nn(pick, hi) + dot_nn(pick, mid) + dot_nn(pick, low)


def out_feed_body(part, *refs):
    place, halves = refs[0], refs[1:3]
    g_up, g_down, up, turned, down, sems = refs[-6:]
    units = up.shape[1]
    for x, ref in enumerate(halves):
        block = ref.shape[1] // 2
        for m in range(4):
            at = pl.multiple_of((place[3] ^ feed_block(4 * x + m)) * block, block)
            rows = ref[m].astype(F32)
            up[pl.ds(at, block), :] = rows[:block]
            turned[pl.ds(at, block), :] = rows[block:]
    here = pl.ds(part * units, units)
    first = pltpu.make_async_copy(up, g_up.at[:, here], sems.at[0])
    first.start()
    down[...] = turned[...].T
    second = pltpu.make_async_copy(down, g_down.at[here, :], sems.at[1])
    second.start()
    first.wait()
    second.wait()


def out_dec_body(mine, theirs, g_in, g_out, g_gains, g_biases, g_token, g_embed):
    total = mine[...].astype(F32) + theirs[...].astype(F32)
    n = g_in.shape[1]
    m = n + g_out.shape[1]
    g_in[...] = total[:, :n]
    g_out[...] = total[:, n:m]
    rows = total[:, m : m + 128].T
    g_gains[...] = rows[0:2]
    g_biases[...] = rows[2:8]
    g_token[...] = rows[8:9]
    half = g_embed.shape[1] // 2
    units = [total[:, m + 128 + k * half : m + 128 + (k + 1) * half] for k in range(3)]
    both = jnp.concatenate(units, axis=0)
    count = both.shape[0] // 2
    g_embed[:, :half] = both[:count]
    g_embed[:, half:] = both[count:]


def out_enc_body(mine, theirs, g_in, g_out, g_gains, g_biases):
    total = mine[...].astype(F32) + theirs[...].astype(F32)
    n, width, half = g_in.shape[0], g_in.shape[1] // 2, g_out.shape[1] // 2
    first = CUT_BACK
    a, b = total[:, : first + half], total[:, first + half :]
    rest = width - first
    g_in[:, :first] = a[:n, :first]
    g_in[:, first:width] = b[:n, :rest]
    g_in[:, width : width + first] = a[n:, :first]
    g_in[:, width + first :] = b[n:, :rest]
    g_out[:, :half] = a[:n, first:]
    g_out[:, half:] = a[n:, first:]
    rows = b[:n, rest:].T
    g_gains[...] = rows[0:2]
    g_biases[...] = rows[2:7]


def out_bias_body(place, biases, up1, down1, up2, down2):
    lo = 0
    for out, at in ((up1, place[7]), (down1, place[4]), (up2, place[7]), (down2, place[4])):
        n = out.shape[1]
        out[...] = biases[:, pl.ds(pl.multiple_of(lo + at * n, 128), n)]
        lo += 2 * n


def swap(v, axis, distance=1):
    return lax.ppermute(v, axis, [(i, i ^ distance) for i in range(lax.axis_size(axis))])


def add(a, b):
    return (a.astype(F32) + b.astype(F32)).astype(BF)


class Flight:
    def __init__(self, steps):
        self.steps, self.result = steps, None
        self.waits = next(steps)

    def land(self, arrays):
        try:
            self.waits = self.steps.send(arrays)
        except StopIteration as end:
            self.waits, self.result = None, end.value


def land(flights, outs=()):
    flights = [f for f in flights if f.waits is not None]
    outs, arrays = lax.optimization_barrier((outs, [f.waits for f in flights]))
    for flight, landed in zip(flights, arrays):
        flight.land(landed)
    return outs


def finish(flight):
    while flight.waits is not None:
        flight.land(flight.waits)
    return flight.result


def gather_all(v, order):
    for axis, distance in order[:-1]:
        (got,) = yield (swap(v, axis, distance),)
        v = jnp.concatenate([v, got], axis=0)
    (last,) = yield (swap(v, *order[-1]),)
    a, b = yield (swap(v, "tc"), swap(last, "tc"))
    return v, last, a, b


def gather_lanes(v, cut):
    for axis, distance in GATHER_A[:2]:
        (got,) = yield (swap(v, axis, distance),)
        v = jnp.concatenate([v, got], axis=0)
    a, b = v[:, :cut], v[:, cut:]
    one, two = yield (swap(a, *GATHER_A[2]), swap(b, *GATHER_B[2]))
    a, b = jnp.concatenate([a, one], axis=0), jnp.concatenate([b, two], axis=0)
    one, two = yield (swap(a, *GATHER_A[3]), swap(b, *GATHER_B[3]))
    got = yield (swap(a, "tc"), swap(one, "tc"), swap(b, "tc"), swap(two, "tc"))
    return (a, one, *got[:2]), (b, two, *got[2:])


def scatter_lanes(one, two, small=None):
    extra = [] if small is None else [small]
    a, b, *got = yield (swap(one[1], "tc"), swap(two[1], "tc"), *(swap(v, "tc") for v in extra))
    a, b = add(one[0], a), add(two[0], b)
    for k in range(2):
        extra = [v + w for v, w in zip(extra, got)]
        half = a.shape[0] // 2
        one, two, *got = yield (
            swap(a[half:], *SCATTER_A[k]), swap(b[half:], *SCATTER_B[k]), *(swap(v, *SCATTER_A[k]) for v in extra)
        )
        a, b = add(a[:half], one), add(b[:half], two)
    v = jnp.concatenate([a, b], axis=1)
    for k in (2, 3):
        extra = [v + w for v, w in zip(extra, got)]
        half = v.shape[0] // 2
        one, *got = yield (swap(v[half:], *SCATTER_A[k]), *(swap(w, *SCATTER_A[k]) for w in extra))
        v = (v[:half], one) if k == 3 else add(v[:half], one)
    return v, [v + w for v, w in zip(extra, got)]


def reduce_feed(ups, downs):
    got = yield tuple(swap(v, "tc") for v in (ups[1], ups[3], downs[1], downs[3]))
    up, up_far, down, down_far = (
        add(v, w) for v, w in zip((ups[0], ups[2], downs[0], downs[2]), got)
    )
    half = up.shape[0] // 2
    one, two, three = yield (
        swap(up_far, "tr"), swap(down[half:], "dp", 1), swap(down_far[half:], "dp", 1)
    )
    up, down, down_far = add(up, one), add(down[:half], two), add(down_far[:half], three)
    one, two = yield (swap(up[half:], "dp", 1), swap(down_far, "tr"))
    up, down = add(up[:half], one), add(down, two)
    shape = (4, half // 4, up.shape[1])
    v = jnp.concatenate([up.reshape(shape), down.reshape(shape)], axis=1)
    for distance in (2, 4):
        half = v.shape[0] // 2
        (got,) = yield (swap(v[half:], "dp", distance),)
        v = add(v[:half], got)
    for distance in (4, 2):
        (got,) = yield (swap(v, "dp", distance),)
        v = jnp.concatenate([v, got], axis=0)
    (got,) = yield (swap(v, "dp", 1),)
    return v, got


def chip_axes(order):
    return [{("dp", 4): 0, ("dp", 2): 1, ("dp", 1): 2, ("tr", 1): 3}[step] for step in order]


def cut_gathered(whole, order, halves):
    rows, width = whole.shape
    if halves:
        v = whole.reshape(32, rows // 32, 2, width // 2).transpose(0, 2, 1, 3)
        v = v.reshape(32, rows // 16, width // 2)
    else:
        v = whole.reshape(32, rows // 32, width)
    v = v.reshape((2, 2, 2, 2, 2) + v.shape[1:])
    first = chip_axes(order)
    v = v.transpose(first[3], 4, first[2], first[1], first[0], 5, 6)
    v = v.reshape(2, 2, -1, v.shape[-1])
    return v[0, 0], v[1, 0], v[0, 1], v[1, 1]


def join_scattered(pair, order, halves):
    v = jnp.stack(pair)
    v = v.reshape(2, 2, 2, 2, 2, v.shape[1] // 16, v.shape[2])
    first = chip_axes(order)
    v = v.transpose(*(1 + first.index(k) for k in range(4)), 0, 5, 6)
    v = v.reshape(32, v.shape[5], v.shape[6])
    if halves:
        v = v.reshape(32, 2, v.shape[1] // 2, v.shape[2]).transpose(0, 2, 1, 3)
        v = v.reshape(32, v.shape[1], -1)
    return v.reshape(-1, v.shape[-1])


def call2(body, outs, args, **more):
    return call(body, outs, args, smem=1, **more)


class Sentence:
    def __init__(self, place, tokens, mask_pos, cot):
        self.place = place
        span, self.width = tokens.shape
        masks = mask_pos.shape[1]
        self.span, self.kept = span, span - masks
        self.rows = -(-(self.kept + 1) // 16) * 16
        self.width2 = cot.shape[1]
        self.x, self.cot, self.spots = call(
            partial(prep_body, self.kept),
            [((self.rows, self.width), BF), ((self.rows, self.width2), F32), ((span, 1), jnp.int32)],
            [mask_pos.reshape(masks, 1), mask_pos, tokens, cot],
            us=3,
        )

    def enc_attn(self, one_a, one_b):
        rows, width = self.rows, self.width
        self.normed, self.packed, self.att_t, self.lse, self.e_in, self.e_par = call2(
            partial(enc_attn_body, self.kept),
            [((rows, width), BF), ((rows, 3 * width), BF), ((width, rows), BF),
             ((width // 128, rows * (128 * HEADS // width)), F32), ((width, 3 * width), BF),
             ((16, width), F32)],
            [self.place, self.x, *one_a, *one_b],
            scratch=[((width, 128), BF)],
            keep=(0, 1, 3, 4),
            alone=True,
            us=12,
        )

    def enc_feed(self, two, weights):
        rows, width, units = self.rows, self.width, weights.shape[1]
        hidden = 2 * units
        self.e_weights = weights
        self.middle, self.normed_two, self.active, self.slope, self.e_low, self.e_out, self.embed = call2(
            enc_feed_body,
            [((rows, width), F32), ((rows, width), BF), ((rows, hidden), BF), ((rows, hidden), BF),
             ((rows, width), BF), ((width, width), BF), ((width, self.width2), BF)],
            [self.place, self.x, self.att_t, *two, self.e_par, weights],
            scratch=[((width, hidden), BF), ((hidden, width), BF), ((rows, width), F32),
                     ((4, 16, units), BF), ((1, hidden), F32)],
            hbm_args=1,
            sems=8 + 8 * units // width,
            keep=(0, 1, 2, 3, 5),
            alone=True,
            us=15,
        )

    def dec_attn(self, three):
        rows, width = self.rows, self.width2
        (self.stream2, self.normed2, self.packed2, self.att2_t, self.lse2, self.d_in, self.d_out,
         self.d_par) = call2(
            partial(dec_attn_body, self.kept),
            [((rows, width), F32), ((rows, width), BF), ((rows, 3 * width), BF), ((width, rows), BF),
             ((width // 128, rows * (128 * HEADS2 // width)), F32), ((width, 3 * width), BF),
             ((width, width), BF), ((16, width), F32)],
            [self.place, self.e_low, self.embed, *three],
            scratch=[((width, 128), BF)],
            keep=(1, 2, 4, 5),
            alone=True,
            us=11,
        )

    def dec_feed(self, weights):
        rows, width, units = self.rows, self.width2, weights.shape[1]
        hidden = 2 * units
        (self.out, *g_ff, self.g_middle2, self.g_att2, self.go20, self.go21, self.small2,
         self.biases2) = call2(
            partial(dec_feed_body, self.kept),
            [((rows, width), F32), *[((width // 2, hidden // 2), BF)] * 8, ((rows, width), F32),
             ((rows, width), BF), ((width // 2, width), BF), ((width // 2, width), BF),
             ((16, width), F32), ((1, hidden + width), F32)],
            [self.place, self.stream2, self.att2_t, self.d_out, self.d_par, self.cot, weights],
            scratch=[((width, hidden), BF), ((hidden, width), BF), ((rows, hidden), BF),
                     ((rows, hidden), BF), ((rows, width), F32), ((rows, width), BF),
                     ((rows, width), BF), ((width, rows), BF), ((width, rows), BF),
                     ((width, rows), BF), ((width, rows), F32), ((width, rows), F32),
                     ((rows, width), BF), ((4, 16, units), BF), ((1, hidden), F32)],
            hbm_args=1,
            sems=8 + 8 * units // width,
            keep=(0,),
            us=16,
        )
        self.ff2 = (g_ff[:4], g_ff[4:])

    def dec_attn_back(self):
        rows, width = self.rows, self.width2
        ga0, ga1, gb0, gb1, self.g_enc, _ = call2(
            partial(dec_attn_back_body, self.kept),
            [((width // 2, 3 * width), BF)] * 2 + [((width // 2, width + 128 + 3 * width // 2), BF)] * 2
            + [((rows, self.width), F32), ((16, width), F32)],
            [self.place, self.packed2, self.g_att2, self.lse2, self.stream2, self.normed2,
             self.g_middle2, self.d_par, self.d_in, self.embed, self.e_low, self.small2, self.go20,
             self.go21],
            scratch=[((rows, 3 * width), BF), ((width, rows), BF), ((width, rows), F32),
                     ((width, rows), F32), ((width, 128), F32), ((width, 128), F32),
                     ((self.width, rows), F32), ((self.width, rows), F32), ((rows, width), BF)],
            us=16,
        )
        self.gi2 = ((ga0, ga1), (gb0, gb1))

    def _feed_back(self, hidden):
        rows, width = self.rows, self.width
        scratch = [((width, hidden // 2), BF), ((hidden // 2, width), BF), ((rows, width), BF),
                   ((width, rows), BF), ((width, rows), BF), ((width, rows), BF)]
        return [((width // 2, hidden // 4), BF)] * 8, scratch

    def enc_feed_back_one(self):
        rows, width, hidden = self.rows, self.width, self.active.shape[1]
        ff, scratch = self._feed_back(hidden)
        (*g_ff, self.total, self.biases1) = call2(
            enc_feed_back_one_body,
            [*ff, ((rows, width), F32), ((1, hidden + width), F32)],
            [self.place, self.g_enc, self.normed_two, self.active, self.slope, self.e_weights],
            scratch=scratch,
            hbm_args=1,
            sems=4 + 4 * hidden // width,
            us=14,
        )
        self.ffa = (g_ff[:4], g_ff[4:])

    def enc_feed_back_two(self):
        rows, width, hidden = self.rows, self.width, self.active.shape[1]
        ff, scratch = self._feed_back(hidden)
        (*g_ff, self.g_middle, self.g_att, go0, go1, self.small, self.biases) = call2(
            enc_feed_back_two_body,
            [*ff, ((rows, width), F32), ((rows, width), BF), ((width, width // 2), BF),
             ((width, width // 2), BF), ((16, width), F32),
             ((1, self.biases1.shape[1] + self.biases2.shape[1]), F32)],
            [self.place, self.g_enc, self.normed_two, self.active, self.slope, self.total, self.biases1,
             self.biases2, self.middle, self.e_par, self.att_t, self.e_out, self.e_weights],
            scratch=[((rows, width), F32), *scratch, ((width, rows), F32), ((width, rows), F32),
                     ((rows, width), BF)],
            hbm_args=1,
            sems=4 + 4 * hidden // width,
            us=19,
        )
        self.ffb = (g_ff[:4], g_ff[4:])
        self.go = (go0, go1)

    def enc_attn_back_one(self):
        rows, width = self.rows, self.width
        (self.g_packed,) = call2(
            partial(enc_attn_back_one_body, self.kept),
            [((rows, 3 * width), BF)],
            [self.place, self.packed, self.g_att, self.lse],
            scratch=[((width, rows), BF)],
            us=12,
        )

    def enc_attn_back_two(self):
        rows, width = self.rows, self.width
        n = 3 * width // 2 - CUT_BACK
        ga0, ga1, gb0, gb1, self.g_stream, _ = call2(
            enc_attn_back_two_body,
            [((width, CUT_BACK + width // 2), BF)] * 2 + [((width, n + 128), BF)] * 2
            + [((rows, width), F32), ((16, width), F32)],
            [self.place, self.g_packed, self.x, self.normed, self.g_middle, self.e_par, self.e_in,
             self.small, *self.go],
            scratch=[((width, rows), F32), ((width, rows), F32), ((width, 128), F32),
                     ((width, 128), F32)],
            us=9,
        )
        self.gi = ((ga0, ga1), (gb0, gb1))

    def spread(self):
        return call(
            partial(spread_body, self.kept),
            [((self.span, self.width2), F32), ((self.span, self.width), F32)],
            [self.spots, self.out, self.g_stream],
            us=LAST,
        )

    def land(self, flights, names=(), more=()):
        names = ["place", *names]
        values, more = land(flights, ([getattr(self, n) for n in names], more))
        for name, value in zip(names, values):
            setattr(self, name, value)
        return more


CUT = 640
CUT_BACK = 512


def whole_weights(params, inproj, outproj, embed=None):
    columns = jnp.pad(params, ((0, 0), (0, 128 - params.shape[1])))
    if embed is None:
        return (jnp.concatenate([inproj, outproj, columns], axis=1),)
    n, m, k = inproj.shape[1] // 2, outproj.shape[1] // 2, embed.shape[1] // 2
    one_a = [inproj[:, :CUT], inproj[:, n : n + CUT]]
    one_b = [inproj[:, CUT:n], columns, inproj[:, n + CUT :], jnp.zeros_like(columns)]
    two = [outproj[:, :m], embed[:, :k], outproj[:, m:], embed[:, k:]]
    return tuple(jnp.concatenate(v, axis=1) for v in (one_a, one_b, two))


def local(
    tokens_in, valid_len, mask_pos,
    encoder_gains, encoder_biases, encoder_inproj, encoder_outproj,
    encoder_up, encoder_upbias, encoder_down, encoder_downbias,
    embed_weight, mask_token,
    decoder_gains, decoder_biases, decoder_inproj, decoder_outproj,
    decoder_up, decoder_upbias, decoder_down, decoder_downbias,
    cotangent,
):
    dp, tr, tc = (lax.axis_index(a) for a in ALL)
    blocks = tuple(lax.axis_size(a) for a in ALL) == (8, 2, 2)
    width, width2 = tokens_in.shape[1], cotangent.shape[1]
    hidden, hidden2 = 2 * encoder_up.shape[1], 2 * decoder_up.shape[1]
    masked = jnp.sum((mask_pos[0] < valid_len[0]).astype(jnp.int32))
    at = (dp, tr, tc, dp) if blocks else (0, 0, 0, 0)
    place = jnp.stack([jnp.int32(v) for v in (*at, tc, valid_len[0] - masked, masked, tr)])

    def feed(up, up_bias, down, down_bias):
        rows, units = 2 * up.shape[0] + 16, up.shape[1]
        args = [up, up_bias[None], down, down_bias[None]]
        (packed,) = call(pack_feed_body, [((rows, units), BF)], args)
        return lax.all_gather(packed, ("tr", "tc"), axis=0, tiled=True)

    enc = [encoder_up, encoder_upbias, encoder_down, encoder_downbias]
    dec = [decoder_up, decoder_upbias, decoder_down, decoder_downbias]
    if blocks:
        one, two, three = call(
            pack_body,
            [((48, 3 * width // 2 + 128), BF), ((48, width // 2 + width2 // 2), BF),
             ((16, 4 * width2 + 128), BF)],
            [encoder_gains.T, encoder_biases.T, encoder_inproj, encoder_outproj, embed_weight,
             decoder_gains.T, decoder_biases.T, mask_token[None], decoder_inproj, decoder_outproj],
        )
        one = Flight(gather_lanes(one, CUT))
        two, three = Flight(gather_all(two, GATHER_C)), Flight(gather_all(three, GATHER_D))
        place, enc, dec = land([one, two, three], (place, enc, dec))
        enc, dec = feed(*enc), feed(*dec)
        (tokens_in,) = land([one], (tokens_in,))
        sentence = Sentence(place, tokens_in, mask_pos, cotangent)
        sentence.land([one, two], ["x"])
        sentence.land([one], ["x"])
        sentence.land([one, two], ["x"])
        one_a, one_b = one.result
    else:
        def whole(v):
            return lax.all_gather(v, ALL, axis=0, tiled=True)

        e_par = whole(jnp.concatenate([encoder_gains, encoder_biases], axis=1))
        d_par = whole(jnp.concatenate([decoder_gains, decoder_biases, mask_token[:, None]], axis=1))
        one_a, one_b, two = whole_weights(
            e_par, whole(encoder_inproj), whole(encoder_outproj), whole(embed_weight)
        )
        (three,) = whole_weights(d_par, whole(decoder_inproj), whole(decoder_outproj))
        one_a, one_b = cut_gathered(one_a, GATHER_A, True), cut_gathered(one_b, GATHER_B, True)
        two = cut_gathered(two, GATHER_C, True)
        three = cut_gathered(three, GATHER_D, False)
        enc, dec = feed(*enc), feed(*dec)
        sentence = Sentence(place, tokens_in, mask_pos, cotangent)

    def feed_out(rows, units, halves):
        outs = []
        for part, pair in enumerate(halves):
            count = units // len(halves)
            outs = pl.pallas_call(
                partial(out_feed_body, part),
                out_shape=[jax.ShapeDtypeStruct((rows, units), F32), jax.ShapeDtypeStruct((units, rows), F32)],
                in_specs=[pl.BlockSpec(memory_space=pltpu.SMEM)]
                + [pl.BlockSpec(memory_space=pltpu.VMEM)] * 2 + [pl.BlockSpec(memory_space=pltpu.HBM)] * len(outs),
                out_specs=[pl.BlockSpec(memory_space=pltpu.HBM)] * 2,
                scratch_shapes=[pltpu.VMEM((rows, count), F32), pltpu.VMEM((rows, count), F32),
                                pltpu.VMEM((count, rows), F32), pltpu.SemaphoreType.DMA((2,))],
                input_output_aliases={3: 0, 4: 1} if outs else {},
                compiler_params=vmem([((rows, count), F32)] * 3),
                cost_estimate=cost(LAST),
            )(place, *pair, *outs)
        return outs

    def dec_out():
        n, n2 = width // 32, width2 // 32
        return call(
            out_dec_body,
            [((n2, 3 * width2), F32), ((n2, width2), F32), ((2, n2), F32), ((6, n2), F32), ((1, n2), F32),
             ((n, width2), F32)],
            finish(gi2)[0],
            us=LAST,
        )

    def bias_out(biases):
        sizes = [hidden // 2, width // 2, hidden2 // 2, width2 // 2]
        outs = call2(out_bias_body, [((1, n), F32) for n in sizes], [place, biases], us=LAST)
        return [v[0] for v in outs]

    gathers = [two, three] if blocks else []
    sentence.enc_attn(one_a, one_b)
    sentence.land(gathers, ["att_t", "e_par"])
    sentence.land(gathers, ["att_t", "e_par"])
    two = two.result if blocks else two
    sentence.enc_feed(two, enc)
    sentence.land(gathers[1:], ["e_low", "embed"])
    sentence.land(gathers[1:], ["e_low", "embed"])
    three = three.result if blocks else three
    sentence.dec_attn(three)
    sentence.dec_feed(dec)

    if blocks:
        sentence.land([], ["g_middle2", "g_att2", "ff2"])
        ff2 = Flight(reduce_feed(*sentence.ff2))
        sentence.land([ff2], ["g_middle2", "g_att2"])
        sentence.dec_attn_back()
        sentence.land([ff2], ["g_enc", "gi2"])
        gi2 = Flight(scatter_lanes(*sentence.gi2))
        sentence.land([gi2], ["g_enc"])
        sentence.enc_feed_back_one()
        sentence.land([ff2, gi2], ["total", "biases1", "ffa"])
        ffa = Flight(reduce_feed(*sentence.ffa))
        sentence.land([ffa], ["total", "biases1"])
        sentence.enc_feed_back_two()
        sentence.land([ffa, ff2, gi2], ["g_middle", "g_att", "small", "go", "biases", "ffb"])
        ffb = Flight(reduce_feed(*sentence.ffb))
        sentence.land([ffb], ["g_middle", "g_att", "small", "biases"])
        sentence.enc_attn_back_one()
        sentence.land([ffa, ffb, ff2, gi2], ["g_packed"])
        sentence.enc_attn_back_two()
        sentence.land([ffb, ffa, ff2, gi2], ["gi", "g_stream"])
        gi = Flight(scatter_lanes(*sentence.gi, sentence.biases))
        sentence.land([gi])
        dec_outs = dec_out()
        sentence.output, sentence.g_tokens = sentence.spread()
        for flight in (ffb, ffa, ff2, ffb):
            land([flight])
        dec_outs, (sentence.output, sentence.g_tokens) = land(
            [gi], (dec_outs, (sentence.output, sentence.g_tokens))
        )
        for flight in (ffa, ffb, ff2, ffa):
            land([flight])
        land([gi])
        outs2 = feed_out(width2 // 2, hidden2 // 2, [finish(ff2)])
        outs2 = land([gi], outs2)
        for flight in (ffb, ffa, ffb):
            land([flight])
        land([gi])
        outs = feed_out(width // 2, hidden // 2, [finish(ffa), finish(ffb)])
        bias_outs = bias_out(finish(gi)[1][0])
    else:
        sentence.dec_attn_back()
        sentence.enc_feed_back_one()
        sentence.enc_feed_back_two()
        sentence.enc_attn_back_one()
        sentence.enc_attn_back_two()

        def halves_of(ups, downs):
            sums = []
            for v in (ups, downs):
                near, far = add(v[0], swap(v[1], "tc")), add(v[2], swap(v[3], "tc"))
                v = lax.psum(add(near, swap(far, "tr")), "dp")
                sums.append(v.reshape(8, -1, v.shape[1]))
            v = jnp.concatenate(sums, axis=1)
            return [v[:4], v[4:]]

        outs2 = feed_out(width2 // 2, hidden2 // 2, [halves_of(*sentence.ff2)])
        halves = [halves_of(*sentence.ffa), halves_of(*sentence.ffb)]
        outs = feed_out(width // 2, hidden // 2, halves)
        bias_outs = bias_out(lax.psum(sentence.biases, ALL))
        sentence.output, sentence.g_tokens = sentence.spread()

    (g_up2, g_down2), (g_up, g_down) = outs2, outs
    b_up, b_down, b_up2, b_down2 = bias_outs
    if blocks:
        n = width // 32
        g_in2, g_out2, g_gains2, g_biases2, g_token, g_embed = dec_outs
        g_in, g_out, g_gains, g_biases = call(
            out_enc_body,
            [((n, 3 * width), F32), ((n, width), F32), ((2, n), F32), ((5, n), F32)],
            finish(gi)[0],
            us=LAST,
        )
        g_gains, g_biases, g_gains2, g_biases2 = g_gains.T, g_biases.T, g_gains2.T, g_biases2.T
        g_token = g_token[0]
    else:
        def scatter(v):
            return lax.psum_scatter(v, ALL, scatter_dimension=0, tiled=True).astype(F32)

        a = join_scattered(sentence.gi[0], SCATTER_A, True)
        b = join_scattered(sentence.gi[1], SCATTER_B, True)
        m = 3 * width // 2 - CUT_BACK
        k = CUT_BACK + width // 2
        g_in = [a[:, :CUT_BACK], b[:, :m], a[:, k : k + CUT_BACK], b[:, m + 128 : 2 * m + 128]]
        g_in = scatter(jnp.concatenate(g_in, axis=1))
        small = scatter(b[:, m : m + 128])
        g_gains, g_biases = small[:, :2], small[:, 2:7]
        g_out = scatter(jnp.concatenate([a[:, CUT_BACK:k], a[:, k + CUT_BACK :]], axis=1))
        g_in2 = scatter(join_scattered(sentence.gi2[0], SCATTER_A, False))
        k = width2 + 128
        v = join_scattered([g[:, :k] for g in sentence.gi2[1]], SCATTER_B, False)
        g_out2, small = scatter(v[:, :width2]), scatter(v[:, width2:])
        g_gains2, g_biases2, g_token = small[:, :2], small[:, 2:8], small[:, 8]
        v = [g[:, k:].reshape(16, -1, 3, width2 // 2).transpose(0, 2, 1, 3) for g in sentence.gi2[1]]
        v = [g.reshape(-1, width2 // 2) for g in v]
        g_embed = scatter(join_scattered(v, SCATTER_B, True))
    return (
        sentence.output, sentence.g_tokens, g_gains, g_biases, g_in, g_out, g_up, b_up, g_down, b_down,
        g_embed, g_token, g_gains2, g_biases2, g_in2, g_out2, g_up2, b_up2, g_down2, b_down2,
    )


def solution(mesh):
    rows = P(ALL, None)
    attention = (rows, rows, rows, rows)
    feed = (P("tc", "tr"), P("tr"), P("tr", "tc"), P("tc"))
    in_specs = (
        (rows, P(ALL), rows) + attention + feed + (rows, P(ALL)) + attention + feed + (rows,)
    )
    out_specs = (rows, rows) + attention + feed + (rows, P(ALL)) + attention + feed
    return jax.shard_map(local, mesh=mesh, in_specs=in_specs, out_specs=out_specs, check_vma=False)
```

```python
import math
from functools import partial

import jax
import jax.numpy as jnp
from jax import lax
from jax.experimental import pallas as pl
from jax.experimental.pallas import tpu as pltpu
from jax.sharding import PartitionSpec as P

HEADS = 12
HEADS2 = 16
ALL = ("dp", "tr", "tc")
EPS = 1e-06
MASKED = -1e30
LOG2E = math.log2(math.e)
F32 = jnp.float32
BF = jnp.bfloat16
SPARE_BYTES = 12 * 1024 * 1024
LAST = 0.01
WHOLE_BYTES = 58 * 1024 * 1024


def dot_nn(a, b):
    return lax.dot_general(a, b, (((1,), (0,)), ((), ())), preferred_element_type=F32)


def dot_nt(a, b):
    return lax.dot_general(a, b, (((1,), (1,)), ((), ())), preferred_element_type=F32)


def cost(us):
    return pl.CostEstimate(flops=int(us * 1e9), bytes_accessed=int(us * 3e6), transcendentals=0)


def vmem(arrays):
    total = sum(math.prod(s) * jnp.dtype(d).itemsize for s, d in arrays)
    return pltpu.CompilerParams(vmem_limit_bytes=SPARE_BYTES + total)


SAVES = []


def save(ref, columns=None):
    for entry in SAVES[-1]:
        if entry["buffer"] is ref:
            source, target = ref, entry["out"]
            if columns is not None:
                source, target = source.at[:, columns], target.at[:, columns]
            pltpu.make_async_copy(source, target, entry["sem"]).start()
            entry["started"] = True


def call(body, outs, args, scratch=(), smem=0, hbm_args=0, sems=0, keep=(), us=2, alone=False, from_hbm=False):
    count = len(args) - smem - hbm_args
    specs = [pl.BlockSpec(memory_space=pltpu.SMEM)] * smem
    specs += [pl.BlockSpec(memory_space=pltpu.VMEM)] * count
    specs += [pl.BlockSpec(memory_space=pltpu.HBM)] * hbm_args
    buffers = [outs[k] for k in keep]
    shapes = [pltpu.VMEM(s, d) for s, d in [*buffers, *scratch]]
    shapes += [pltpu.SemaphoreType.DMA((max(n, 1),)) for n in (len(keep), sems)]

    def kernel(*refs):
        ins, rest = refs[: len(args)], refs[len(args) :]
        results, rest = list(rest[: len(outs)]), rest[len(outs) :]
        own, keep_sems, own_sems = rest[:-2], rest[-2], rest[-1]
        entries = []
        for n, k in enumerate(keep):
            entries.append({"buffer": own[n], "out": results[k], "sem": keep_sems.at[n], "started": False})
            results[k] = own[n]
        SAVES.append(entries)
        body(*ins, *results, *own[len(keep) :], *((own_sems,) if sems else ()))
        SAVES.pop()
        for entry in entries:
            copy = pltpu.make_async_copy(entry["buffer"], entry["out"], entry["sem"])
            if not entry["started"]:
                copy.start()
        for entry in entries:
            pltpu.make_async_copy(entry["buffer"], entry["out"], entry["sem"]).wait()

    args = list(args)
    for k in range(smem if from_hbm else len(args) - hbm_args, len(args)):
        args[k] = pltpu.with_memory_space_constraint(args[k], pltpu.HBM)
    spaces = [pltpu.HBM if k in keep else pltpu.VMEM for k in range(len(outs))]
    return pl.pallas_call(
        kernel,
        out_shape=[
            pltpu.HBM(s, d) if k in keep else jax.ShapeDtypeStruct(s, d) for k, (s, d) in enumerate(outs)
        ],
        in_specs=specs,
        out_specs=[pl.BlockSpec(memory_space=space) for space in spaces],
        scratch_shapes=shapes,
        compiler_params=pltpu.CompilerParams(vmem_limit_bytes=WHOLE_BYTES) if alone else vmem([*buffers, *scratch]),
        cost_estimate=cost(us),
    )(*args)


def norm_parts(v):
    center = v - jnp.mean(v, axis=-1, keepdims=True)
    r = lax.rsqrt(jnp.mean(center * center, axis=-1, keepdims=True) + EPS)
    return center * r, r


def norm_back(u, r, gain, y):
    e = y * gain
    back = r * (e - jnp.mean(e, axis=-1, keepdims=True) - u * jnp.mean(e * u, axis=-1, keepdims=True))
    return back, jnp.sum(y * u, axis=0, keepdims=True), jnp.sum(y, axis=0, keepdims=True)


def split3(v):
    hi = v.astype(BF)
    rest = v - hi.astype(F32)
    mid = rest.astype(BF)
    return hi, mid, (rest - mid.astype(F32)).astype(BF)


def head_masks(head_size):
    lane = lax.broadcasted_iota(jnp.int32, (1, 128), 1) // head_size
    return [(lane == h).astype(F32).astype(BF) for h in range(128 // head_size)]


def stack_heads(rows, masks):
    return jnp.concatenate([rows * m for m in masks], axis=0)


def prep_body(kept, mp_col, mp_row, tokens, cot, x_out, cot_out, place_out):
    rows, span = x_out.shape[0], tokens.shape[0]
    wide = lax.broadcasted_iota(jnp.int32, (mp_col.shape[0], span), 1)
    below = jnp.sum((mp_col[...] < wide).astype(F32), axis=0, keepdims=True)
    here = jnp.sum((mp_col[...] == wide).astype(F32), axis=0, keepdims=True)
    place = jnp.where(here > 0, kept, wide[:1] - below.astype(jnp.int32))
    pick = lax.broadcasted_iota(jnp.int32, (rows, span), 0) == place
    pick_f = pick.astype(F32)
    cot_out[...] = dot_nn(pick_f.astype(BF), cot[...])
    keep = lax.broadcasted_iota(jnp.int32, (rows, span), 0) < kept
    x_out[...] = dot_nn(jnp.where(keep, pick_f, 0.0).astype(BF), tokens[...]).astype(BF)
    tall = lax.broadcasted_iota(jnp.int32, (span, mp_row.shape[1]), 0)
    below_t = jnp.sum((mp_row[...] < tall).astype(F32), axis=1, keepdims=True)
    here_t = jnp.sum((mp_row[...] == tall).astype(F32), axis=1, keepdims=True)
    place_out[...] = jnp.where(here_t > 0, kept, tall[:, :1] - below_t.astype(jnp.int32))


def spread_back(place, rows, limit):
    at = lax.broadcasted_iota(jnp.int32, (place.shape[0], rows), 1)
    return jnp.where(at < limit, (at == place).astype(F32), 0.0).astype(BF)


def key_bias(lens, kept, rows, with_mask_row):
    at = lax.broadcasted_iota(jnp.int32, (rows, 1), 0)
    bias = jnp.where(at < lens[0], 0.0, MASKED)
    if with_mask_row:
        count = jnp.full((rows, 1), lens[1], jnp.int32).astype(F32)
        bias = jnp.where(at == kept, jnp.log(count) * LOG2E, bias)
    return bias


def attention_forward(packed, att_t, lse, bias, head_size):
    width = packed.shape[1] // 3
    rows = packed.shape[0]
    masks = head_masks(head_size)
    scale = head_size**-0.5 * LOG2E

    def group(g, carry):
        at = pl.multiple_of(g * 128, 128)
        q = packed[:, pl.ds(at, 128)]
        k = packed[:, pl.ds(width + at, 128)]
        v_t = packed[:, pl.ds(2 * width + at, 128)].T
        scores = dot_nt(k, stack_heads(q, masks)) * scale + bias
        peak = jnp.max(scores, axis=0, keepdims=True)
        weights = jnp.exp2(scores - peak)
        total = jnp.sum(weights, axis=0, keepdims=True)
        out = dot_nn(v_t, weights.astype(BF)) * (1.0 / total)
        for h in range(len(masks)):
            block = out[h * head_size : (h + 1) * head_size, h * rows : (h + 1) * rows]
            att_t[pl.ds(at + h * head_size, head_size), :] = block.astype(BF)
        lse[pl.ds(g, 1), :] = peak + jnp.log(total) * LOG2E
        return carry

    lax.fori_loop(0, width // 128, group, 0)


def attention_backward(packed, g_att, lse, g_packed, gq_t, bias, head_size):
    width = packed.shape[1] // 3
    rows = packed.shape[0]
    masks = head_masks(head_size)
    scale = head_size**-0.5

    def group(g, carry):
        at = pl.multiple_of(g * 128, 128)
        q = packed[:, pl.ds(at, 128)]
        k = packed[:, pl.ds(width + at, 128)]
        v = packed[:, pl.ds(2 * width + at, 128)]
        q_s = stack_heads(q, masks)
        g_s = stack_heads(g_att[:, pl.ds(at, 128)], masks)
        scores = dot_nt(k, q_s) * (scale * LOG2E) + bias
        probs = jnp.exp2(scores - lse[pl.ds(g, 1), :])
        g_v = dot_nn(probs.astype(BF), g_s)
        g_probs = dot_nt(v, g_s)
        delta = jnp.sum(g_probs * probs, axis=0, keepdims=True)
        g_scores = (probs * (g_probs - delta)).astype(BF)
        g_k = dot_nn(g_scores, q_s) * scale
        out = dot_nn(k.T, g_scores) * scale
        for h in range(len(masks)):
            block = out[h * head_size : (h + 1) * head_size, h * rows : (h + 1) * rows]
            gq_t[pl.ds(at + h * head_size, head_size), :] = block.astype(BF)
        g_packed[:, pl.ds(width + at, 128)] = g_k.astype(BF)
        g_packed[:, pl.ds(2 * width + at, 128)] = g_v.astype(BF)
        return carry

    lax.fori_loop(0, width // 128, group, 0)
    g_packed[:, :width] = gq_t[...].T


def project_in(stream, params, inproj, normed_out, packed_out):
    u, r = norm_parts(stream)
    normed = (u * params[0:1, :] + params[2:3, :]).astype(BF)
    normed_out[...] = normed
    save(normed_out)
    width = stream.shape[1]
    step = 256
    for part in range(3):
        for at in range(0, width, step):
            lo = part * width + at
            value = dot_nn(normed, inproj[:, lo : lo + step])
            if part == 0:
                value = value + params[3:4, at : at + step]
            if part == 2:
                value = value + params[4:5, at : at + step]
            packed_out[:, lo : lo + step] = value.astype(BF)
    save(packed_out)


GATHER_A = (("tr", 1), ("dp", 4), ("dp", 2), ("dp", 1))
GATHER_B = (("tr", 1), ("dp", 4), ("dp", 1), ("dp", 2))
GATHER_C = (("tr", 1), ("dp", 4), ("dp", 2), ("dp", 1))
GATHER_D = (("tr", 1), ("dp", 1), ("dp", 4), ("dp", 2))
SCATTER_A = (("dp", 1), ("tr", 1), ("dp", 2), ("dp", 4))
SCATTER_B = (("tr", 1), ("dp", 1), ("dp", 2), ("dp", 4))
FEED = (("dp", 1), ("dp", 2), ("dp", 4))


def differences(order, bits):
    dp = tr = 0
    for (axis, distance), bit in zip(order, bits):
        if axis == "dp":
            dp = dp + distance * bit
        else:
            tr = tr + bit
    return dp, tr


def gathered_block(order, j, last):
    return differences(order, (j & 1, (j >> 1) & 1, (j >> 2) & 1, last))


def scattered_block(order, m):
    return differences(order, (m >> 3, (m >> 2) & 1, (m >> 1) & 1, m & 1))


def feed_block(m):
    return differences(FEED, (m >> 2, (m >> 1) & 1, m & 1))[0]


def place_rows(place, order, sources, block, put):
    first = place[2] == 0
    for x in range(2):
        own_ref, oth_ref = sources[x], sources[2 + x]
        count = own_ref.shape[0] // block

        def one(j, carry, own_ref=own_ref, oth_ref=oth_ref, x=x):
            dp, tr = gathered_block(order, j, x)
            chip = (place[0] ^ dp) * 2 + (place[1] ^ tr)
            at = pl.multiple_of(j * block, block)
            own = own_ref[pl.ds(at, block), :].astype(F32)
            oth = oth_ref[pl.ds(at, block), :].astype(F32)
            put(chip, jnp.where(first, own, oth), jnp.where(first, oth, own))
            return carry

        lax.fori_loop(0, count, one, 0)


def place_halves(place, order, sources, cuts):
    block = sources[0].shape[0] // 8
    half = block // 2

    def put(chip, low, high):
        at = pl.multiple_of(chip * block, block)
        top = jnp.concatenate([low[:half], high[:half]], axis=0).astype(BF)
        bottom = jnp.concatenate([low[half:], high[half:]], axis=0).astype(BF)
        lo = 0
        for target, first, width, shift in cuts:
            target[pl.ds(at, block), first : first + width] = top[:, lo : lo + width]
            if shift is not None:
                right = first + shift
                target[pl.ds(at, block), right : right + width] = bottom[:, lo : lo + width]
            lo += width

    place_rows(place, order, sources, block, put)


def place_whole(place, order, sources, cuts):
    block = sources[0].shape[0] // 8

    def put(chip, low, high):
        at = pl.multiple_of(chip * 2 * block, 2 * block)
        both = jnp.concatenate([low, high], axis=0).astype(BF)
        lo = 0
        for target, width in cuts:
            target[pl.ds(at, 2 * block), :] = both[:, lo : lo + width]
            lo += width

    place_rows(place, order, sources, block, put)


def param_rows(columns):
    return columns[...].astype(F32).T[:16]


def reorder_rows(place, order, source, target):
    block = source.shape[0] // 32
    for core in range(2):
        for m in range(16):
            dp, tr = scattered_block(order, m)
            device = ((place[0] ^ dp) * 2 + (place[1] ^ tr)) * 2 + (place[2] ^ core)
            at = pl.multiple_of(device * block, 8)
            to = (core * 16 + m) * block
            target[to : to + block, :] = source[pl.ds(at, block), :]


def write_halves(ordered, columns, outs, first=0, count=None):
    half_rows = ordered.shape[0] // 2
    block = half_rows // 16
    width = columns.shape[1] // 2
    count = width if count is None else count
    step = max(n for n in (384, 320, 256) if count % n == 0) if count != 640 else 640
    for core in range(2):
        rows = ordered[core * half_rows : (core + 1) * half_rows, :].astype(BF)
        for at in range(first, first + count, step):
            left = dot_nn(rows, columns[:, at : at + step])
            right = dot_nn(rows, columns[:, width + at : width + at + step])
            for m in range(16):
                both = [left[m * block : (m + 1) * block], right[m * block : (m + 1) * block]]
                outs[core][m * 2 * block : (m + 1) * 2 * block, at - first : at - first + step] = (
                    jnp.concatenate(both, axis=0).astype(BF)
                )


def write_whole(ordered, columns, outs, lo):
    half_rows = ordered.shape[0] // 2
    width = columns.shape[1]
    for core in range(2):
        rows = ordered[core * half_rows : (core + 1) * half_rows, :].astype(BF)
        for at in range(0, width, 256):
            outs[core][:, lo + at : lo + at + 256] = dot_nn(rows, columns[:, at : at + 256]).astype(BF)


def small_columns(small):
    table = jnp.concatenate([small[...], jnp.zeros((112, small.shape[1]), F32)], axis=0)
    return table.T


def pack_body(
    e_gains, e_biases, e_in, e_out, embed, d_gains, d_biases, token, d_in, d_out, one, two, three
):
    def columns(parts):
        total, lo = 0.0, 0
        for part in parts:
            count, rows = part.shape
            spot = lax.broadcasted_iota(jnp.int32, (count, 128), 1)
            want = lax.broadcasted_iota(jnp.int32, (count, 128), 0) + lo
            table = (spot == want).astype(F32).astype(BF)
            total = total + lax.dot_general(
                part[...], table, (((0,), (0,)), ((), ())), preferred_element_type=F32
            )
            lo += count
        return total

    e_par = columns([e_gains, e_biases])

    def halves(v):
        v = v[...].astype(F32)
        width = v.shape[1] // 2
        return jnp.concatenate([v[:, :width], v[:, width:]], axis=0).astype(BF)

    n = e_in.shape[1] // 2
    one[:, :n] = halves(e_in)
    one[:, n:] = jnp.concatenate([e_par, jnp.zeros_like(e_par)], axis=0).astype(BF)
    n = e_out.shape[1] // 2
    two[:, :n] = halves(e_out)
    two[:, n:] = halves(embed)
    n = d_in.shape[1]
    m = n + d_out.shape[1]
    three[:, :n] = d_in[...]
    three[:, n:m] = d_out[...]
    three[:, m:] = columns([d_gains, d_biases, token]).astype(BF)


def enc_attn_body(
    kept, place, x, s0, s1, s2, s3, r0, r1, r2, r3,
    normed, packed, att_t, lse, inproj, par_t, par_c,
):
    width = x.shape[1]
    n, shift = s0.shape[1], 3 * width // 2
    place_halves(place, GATHER_A, (s0, s1, s2, s3), ((inproj, 0, n, shift),))
    place_halves(
        place, GATHER_B, (r0, r1, r2, r3), ((inproj, n, shift - n, shift), (par_c, 0, 128, None))
    )
    save(inproj)
    par_t[...] = param_rows(par_c)
    project_in(x[...].astype(F32), par_t, inproj, normed, packed)
    bias = key_bias((place[5], place[6]), kept, x.shape[0], False)
    attention_forward(packed, att_t, lse, bias, width // HEADS)


def dec_attn_body(
    kept, place, e_low, embed, s0, s1, s2, s3,
    stream, normed, packed, att_t, lse, inproj, outproj, params, par_c,
):
    rows = e_low.shape[0]
    width = stream.shape[1]
    place_whole(
        place, GATHER_D, (s0, s1, s2, s3), ((inproj, 3 * width), (outproj, width), (par_c, 128))
    )
    save(inproj)
    save(outproj)
    params[...] = param_rows(par_c)
    embedded = dot_nn(e_low[...], embed[...]) + params[7:8, :]
    at = lax.broadcasted_iota(jnp.int32, (rows, 1), 0)
    decoded = jnp.where(at < kept, embedded, params[8:9, :])
    stream[...] = decoded
    save(stream)
    project_in(decoded, params, inproj, normed, packed)
    bias = key_bias((place[5], place[6]), kept, rows, True)
    attention_forward(packed, att_t, lse, bias, width // HEADS2)


def pack_feed_body(up, up_bias, down, down_bias, out):
    rows, width = up.shape[0], down.shape[1]
    out[:rows, :] = up[...]
    for at in range(0, up.shape[1], width):
        out[rows : 2 * rows, at : at + width] = down[at : at + width, :]
    row = lax.broadcasted_iota(jnp.int32, (16, up.shape[1]), 0)
    value = jnp.where(row == 0, up_bias[...].astype(F32), 0.0)
    out[2 * rows :, :] = value.astype(BF)
    row = lax.broadcasted_iota(jnp.int32, (16, width), 0)
    value = jnp.where(row == 1, down_bias[...].astype(F32), value[:, :width])
    out[2 * rows :, :width] = value.astype(BF)


def load_feed(place, gathered, up, down, sems, part=0, biases=None):
    copies = []
    groups = []
    half = up.shape[0] // 2
    units = up.shape[1] // 2
    block = gathered.shape[0] // 4

    def start(source, target):
        copies.append(pltpu.make_async_copy(source, target, sems.at[len(copies)]))
        copies[-1].start()

    for tr in range(2):
        for core in range(2):
            base = ((place[7] ^ tr) * 2 + core) * block

            def rows(at, count, base=base):
                return pl.ds(pl.multiple_of(base + at, 16), count)

            columns = pl.ds(tr * units, units)
            start(
                gathered.at[rows(0, half), pl.ds(part * units, units)],
                up.at[pl.ds(core * half, half), columns],
            )
            for at in range(0, units, half):
                start(
                    gathered.at[rows(half, half), pl.ds(part * units + at, half)],
                    down.at[pl.ds(tr * units + at, half), pl.ds(core * half, half)],
                )
            if biases is not None:
                start(gathered.at[rows(2 * half, 16), :], biases.at[2 * tr + core])
        groups.append(copies[sum(len(g) for g in groups) :])
    return groups


def wait(copies):
    for copy in copies:
        copy.wait()


def bias_rows(biases, half):
    return jnp.concatenate([biases[0, 1:2, :half], biases[1, 1:2, :half]], axis=1).astype(F32)


def middle_of(stream, att_t, outproj, params):
    return stream + dot_nn(att_t[...].T, outproj[...]) + params[5:6, :]


def feed_forward(
    normed_two, up, up_bias, down, active_out, slope_out, total, step, copies, biases
):
    units = up.shape[1] // 2
    total[...] = jnp.zeros_like(total)

    def chunk(c, carry):
        at = pl.multiple_of(c * step, step)
        hidden = dot_nn(normed_two, up[:, pl.ds(at, step)]) + up_bias[:, pl.ds(at, step)]
        phi = 0.5 * (1.0 + lax.erf(hidden * math.sqrt(0.5)))
        bell = jnp.exp2(hidden * hidden * (-0.5 * LOG2E)) * (1.0 / math.sqrt(2 * math.pi))
        active = (hidden * phi).astype(BF)
        active_out[:, pl.ds(at, step)] = active
        slope_out[:, pl.ds(at, step)] = (phi + hidden * bell).astype(BF)
        save(active_out, pl.ds(at, step))
        save(slope_out, pl.ds(at, step))
        total[...] += dot_nn(active, down[pl.ds(at, step), :])
        return carry

    for tr in range(2):
        wait(copies[tr])
        up_bias[:, tr * units : (tr + 1) * units] = biases[2 * tr, 0:1, :].astype(F32)
        lax.fori_loop(tr * units // step, (tr + 1) * units // step, chunk, 0)


def order_feed(place, source, target):
    block = source.shape[0] // 16
    for core in range(2):
        for m in range(8):
            at = ((place[4] ^ core) * 8 + (place[3] ^ feed_block(m))) * block
            to = (core * 8 + m) * block
            target[to : to + block, :] = source[pl.ds(pl.multiple_of(at, block), block), :]


def feed_backward(
    copies, place, part, parts, g_result, normed_two, active, slope, up, down,
    g_ups, g_downs, g_upbias, g_normed, step, rows_t, ordered_n, ordered_g,
):
    width = normed_two.shape[1]
    count = up.shape[1] // 2
    units = count * parts
    half = width // 2
    rows_t[...] = normed_two[...].T
    order_feed(place, rows_t, ordered_n)
    rows_t[...] = g_result[...].T
    order_feed(place, rows_t, ordered_g)
    for tr in range(2):
        wait(copies[tr])
        base = tr * units + part * count
        out_base = pl.multiple_of((place[7] ^ tr) * units + part * count, 128)

        def chunk(c, carry, tr=tr, base=base, out_base=out_base):
            at = pl.multiple_of(c * step, step)
            here = pl.ds(pl.multiple_of(tr * count + at, 128), step)
            g_active = dot_nt(g_result[...], down[here, :]).astype(BF).astype(F32)
            there = pl.ds(pl.multiple_of(base + at, 128), step)
            g_hidden = (slope[:, there].astype(F32) * g_active).astype(BF)
            g_upbias[:, pl.ds(pl.multiple_of(out_base + at, 128), step)] = jnp.sum(
                g_hidden.astype(F32), axis=0, keepdims=True
            )
            g_normed[...] += dot_nt(g_hidden, up[:, here])
            g_up = dot_nn(ordered_n[...], g_hidden).astype(BF)
            g_down = dot_nn(ordered_g[...], active[:, there]).astype(BF)
            for core in range(2):
                g_ups[2 * tr + core][:, pl.ds(at, step)] = g_up[core * half : (core + 1) * half]
                g_downs[2 * tr + core][:, pl.ds(at, step)] = g_down[core * half : (core + 1) * half]
            return carry

        lax.fori_loop(0, count // step, chunk, 0)


def after_feed_backward(
    place, order, g_out, g_normed, middle, params, att_t, outproj, g_middle, g_att, small, att_f, att_o
):
    u, r = norm_parts(middle)
    y = g_normed.astype(BF).astype(F32)
    back, g_gain, g_shift = norm_back(u, r, params[1:2, :], y)
    grad = g_out + back
    g_middle[...] = grad
    branch = grad.astype(BF)
    att_f[...] = att_t[...].astype(F32)
    reorder_rows(place, order, att_f, att_o)
    g_att[...] = dot_nt(branch, outproj[...]).astype(BF)
    small[1:2, :] = g_gain
    small[5:6, :] = jnp.sum(branch.astype(F32), axis=0, keepdims=True)
    small[6:7, :] = g_shift
    return branch


def enc_feed_body(
    place, x, att_t, s0, s1, s2, s3, params, weights,
    middle, normed_two, active, slope, e_low, outproj, embed,
    up, down, total, biases, up_bias, sems,
):
    copies = load_feed(place, weights, up, down, sems, 0, biases)
    width = x.shape[1]
    n, m = width // 2, embed.shape[1] // 2
    place_halves(place, GATHER_C, (s0, s1, s2, s3), ((outproj, 0, n, n), (embed, 0, m, m)))
    mid = middle_of(x[...].astype(F32), att_t, outproj, params)
    middle[...] = mid
    u, r = norm_parts(mid)
    n2 = (u * params[1:2, :] + params[6:7, :]).astype(BF)
    normed_two[...] = n2
    for ref in (middle, normed_two, outproj, embed):
        save(ref)
    feed_forward(n2, up, up_bias, down, active, slope, total, 512, copies, biases)
    down_bias = bias_rows(biases, width // 2)
    result = (total[...] + down_bias).astype(BF)
    e_low[...] = (middle[...] + result.astype(F32)).astype(BF)


def dec_feed_body(
    kept, place, stream, att_t, outproj, params, cot, weights,
    out, gu0, gu1, gu2, gu3, gd0, gd1, gd2, gd3, g_middle, g_att, go0, go1, small, g_biases,
    up, down, active, slope, total, n2_s, g_res, rows_t, ordered_n, ordered_g,
    att_f, att_o, branch_s, biases, up_bias, sems,
):
    copies = load_feed(place, weights, up, down, sems, 0, biases)
    mid = middle_of(stream[...], att_t, outproj, params)
    u, r = norm_parts(mid)
    n2 = (u * params[1:2, :] + params[6:7, :]).astype(BF)
    n2_s[...] = n2
    feed_forward(n2, up, up_bias, down, active, slope, total, 512, copies, biases)
    down_bias = bias_rows(biases, up.shape[0] // 2)
    result = (total[...] + down_bias).astype(BF)
    out[...] = mid + result.astype(F32)
    save(out)
    g_out = cot[...]
    g_res[...] = g_out.astype(BF)
    small[...] = jnp.zeros_like(small)
    units = up.shape[1]
    g_biases[:, units:] = jnp.sum(g_res[...].astype(F32), axis=0, keepdims=True)
    total[...] = jnp.zeros_like(total)
    feed_backward(
        ((), ()), place, 0, 1, g_res, n2_s, active, slope, up, down, (gu0, gu1, gu2, gu3), (gd0, gd1, gd2, gd3),
        g_biases, total, 512, rows_t, ordered_n, ordered_g,
    )
    branch = after_feed_backward(
        place, SCATTER_B, g_out, total[...], mid, params, att_t, outproj, g_middle, g_att, small,
        att_f, att_o,
    )
    branch_s[...] = branch
    write_whole(att_o, branch_s, (go0, go1), 0)


def enc_feed_back_one_body(
    place, g_enc, normed_two, active, slope, weights,
    gu0, gu1, gu2, gu3, gd0, gd1, gd2, gd3, total, biases, up, down, g_res, rows_t, ordered_n, ordered_g, sems,
):
    copies = load_feed(place, weights, up, down, sems)
    g_res[...] = g_enc[...].astype(BF)
    total[...] = jnp.zeros_like(total)
    biases[:, 2 * up.shape[1] :] = jnp.sum(g_res[...].astype(F32), axis=0, keepdims=True)
    feed_backward(
        copies, place, 0, 2, g_res, normed_two, active, slope, up, down, (gu0, gu1, gu2, gu3),
        (gd0, gd1, gd2, gd3), biases, total, 384, rows_t, ordered_n, ordered_g,
    )


def enc_feed_back_two_body(
    place, g_enc, normed_two, active, slope, total_in, biases_in, biases_dec, middle, params, att_t,
    outproj, weights,
    gu0, gu1, gu2, gu3, gd0, gd1, gd2, gd3, g_middle, g_att, go0, go1, small, biases,
    total, up, down, g_res, rows_t, ordered_n, ordered_g, att_f, att_o, branch_s, sems,
):
    copies = load_feed(place, weights, up, down, sems, 1)
    g_res[...] = g_enc[...].astype(BF)
    total[...] = total_in[...]
    count = biases_in.shape[1]
    biases[:, :count] = biases_in[...]
    biases[:, count:] = biases_dec[...]
    small[...] = jnp.zeros_like(small)
    feed_backward(
        copies, place, 1, 2, g_res, normed_two, active, slope, up, down, (gu0, gu1, gu2, gu3),
        (gd0, gd1, gd2, gd3), biases, total, 384, rows_t, ordered_n, ordered_g,
    )
    branch = after_feed_backward(
        place, SCATTER_A, g_enc[...], total[...], middle[...], params, att_t, outproj, g_middle,
        g_att, small, att_f, att_o,
    )
    branch_s[...] = branch
    write_halves(att_o, branch_s, (go0, go1))


def project_back(
    place, order, stream, normed, g_packed, g_middle, params, inproj, small, first, rows_f, rows_o
):
    width = stream.shape[1]
    rows_f[...] = normed[...].astype(F32).T
    reorder_rows(place, order, rows_f, rows_o)
    g_normed = dot_nt(g_packed[...], inproj[...])
    u, r = norm_parts(stream)
    back, g_gain, g_shift = norm_back(u, r, params[0:1, :], g_normed)
    small[...] = first[...]
    small[0:1, :] = g_gain
    small[2:3, :] = g_shift
    small[3:4, :] = jnp.sum(g_packed[:, :width].astype(F32), axis=0, keepdims=True)
    small[4:5, :] = jnp.sum(g_packed[:, 2 * width :].astype(F32), axis=0, keepdims=True)
    return g_middle[...] + back


def dec_attn_back_body(
    kept, place, packed, g_att, lse, stream, normed, g_middle, params, inproj, embed, e_low, first,
    go0, go1, ga0, ga1, gb0, gb1, g_enc, small, g_packed, gq_t, rows_f, rows_o, cols, cols_o,
    emb_f, emb_o, g_emb,
):
    rows = stream.shape[0]
    width = stream.shape[1]
    bias = key_bias((place[5], place[6]), kept, rows, True)
    attention_backward(packed, g_att, lse, g_packed, gq_t, bias, width // HEADS2)
    g_stream = project_back(
        place, SCATTER_A, stream[...], normed, g_packed, g_middle, params, inproj, small, first,
        rows_f, rows_o,
    )
    write_whole(rows_o, g_packed, (ga0, ga1), 0)
    at = lax.broadcasted_iota(jnp.int32, (rows, 1), 0)
    small[8:9, :] = jnp.sum(jnp.where(at == kept, g_stream, 0.0), axis=0, keepdims=True)
    g_embedded = jnp.where(at < kept, g_stream, 0.0).astype(BF)
    small[7:8, :] = jnp.sum(g_embedded.astype(F32), axis=0, keepdims=True)
    g_emb[...] = g_embedded
    g_enc[...] = dot_nt(g_embedded, embed[...])
    emb_f[...] = e_low[...].astype(F32).T
    reorder_rows(place, SCATTER_B, emb_f, emb_o)
    cols[...] = small_columns(small)
    reorder_rows(place, SCATTER_B, cols, cols_o)
    n = cols_o.shape[0] // 2
    half = emb_o.shape[0] // 2
    block, part = half // 16, g_emb.shape[1] // 2
    unit = n // 16
    for core, (gb, go) in enumerate(((gb0, go0), (gb1, go1))):
        gb[:, :width] = go[...]
        gb[:, width : width + 128] = cols_o[core * n : (core + 1) * n, :].astype(BF)
        rows_e = emb_o[core * half : (core + 1) * half, :].astype(BF)
        left, right = dot_nn(rows_e, g_emb[:, :part]), dot_nn(rows_e, g_emb[:, part:])
        for m in range(16):
            both = [left[m * block : (m + 1) * block], right[m * block : (m + 1) * block]]
            both = jnp.concatenate(both, axis=0).astype(BF)
            for k in range(2 * block // unit):
                lo = width + 128 + k * part
                gb[m * unit : (m + 1) * unit, lo : lo + part] = both[k * unit : (k + 1) * unit]


def enc_attn_back_one_body(kept, place, packed, g_att, lse, g_packed, gq_t):
    bias = key_bias((place[5], place[6]), kept, packed.shape[0], False)
    attention_backward(packed, g_att, lse, g_packed, gq_t, bias, g_att.shape[1] // HEADS)


def enc_attn_back_two_body(
    place, g_packed, x, normed, g_middle, params, inproj, first, go0, go1,
    ga0, ga1, gb0, gb1, g_stream, small, rows_f, rows_o, cols, cols_o,
):
    width = x.shape[1]
    g_stream[...] = project_back(
        place, SCATTER_A, x[...].astype(F32), normed, g_packed, g_middle, params, inproj, small, first,
        rows_f, rows_o,
    )
    m = gb0.shape[1] - 128
    n = 3 * width // 2 - m
    write_halves(rows_o, g_packed, (ga0, ga1), 0, n)
    reorder_rows(place, SCATTER_B, rows_f, rows_o)
    write_halves(rows_o, g_packed, (gb0, gb1), n, m)
    cols[...] = small_columns(small)
    reorder_rows(place, SCATTER_B, cols, cols_o)
    count = cols_o.shape[0] // 2
    block = count // 16
    for core, (a, b, go) in enumerate(((ga0, gb0, go0), (ga1, gb1, go1))):
        a[:, n:] = go[...]
        for k in range(16):
            part = cols_o[core * count + k * block : core * count + (k + 1) * block, :]
            both = jnp.concatenate([part, jnp.zeros_like(part)], axis=0).astype(BF)
            b[k * 2 * block : (k + 1) * 2 * block, m:] = both


def spread_body(kept, spots, out, g_stream, output, g_tokens):
    rows = out.shape[0]
    for limit, source, target in ((kept + 1, out, output), (kept, g_stream, g_tokens)):
        pick = spread_back(spots[...], rows, limit)
        hi, mid, low = split3(source[...])
        target[...] = dot_nn(pick, hi) + dot_nn(pick, mid) + dot_nn(pick, low)


def out_feed_body(part, *refs):
    place, halves = refs[0], refs[1:3]
    g_up, g_down, up, turned, down, sems = refs[-6:]
    units = up.shape[1]
    for x, ref in enumerate(halves):
        block = ref.shape[1] // 2
        for m in range(4):
            at = pl.multiple_of((place[3] ^ feed_block(4 * x + m)) * block, block)
            rows = ref[m].astype(F32)
            up[pl.ds(at, block), :] = rows[:block]
            turned[pl.ds(at, block), :] = rows[block:]
    here = pl.ds(part * units, units)
    first = pltpu.make_async_copy(up, g_up.at[:, here], sems.at[0])
    first.start()
    down[...] = turned[...].T
    second = pltpu.make_async_copy(down, g_down.at[here, :], sems.at[1])
    second.start()
    first.wait()
    second.wait()


def out_dec_body(mine, theirs, g_in, g_out, g_gains, g_biases, g_token, g_embed):
    total = mine[...].astype(F32) + theirs[...].astype(F32)
    n = g_in.shape[1]
    m = n + g_out.shape[1]
    g_in[...] = total[:, :n]
    g_out[...] = total[:, n:m]
    rows = total[:, m : m + 128].T
    g_gains[...] = rows[0:2]
    g_biases[...] = rows[2:8]
    g_token[...] = rows[8:9]
    half = g_embed.shape[1] // 2
    units = [total[:, m + 128 + k * half : m + 128 + (k + 1) * half] for k in range(3)]
    both = jnp.concatenate(units, axis=0)
    count = both.shape[0] // 2
    g_embed[:, :half] = both[:count]
    g_embed[:, half:] = both[count:]


def out_enc_body(mine, theirs, g_in, g_out, g_gains, g_biases):
    total = mine[...].astype(F32) + theirs[...].astype(F32)
    n, width, half = g_in.shape[0], g_in.shape[1] // 2, g_out.shape[1] // 2
    first = CUT_BACK
    a, b = total[:, : first + half], total[:, first + half :]
    rest = width - first
    g_in[:, :first] = a[:n, :first]
    g_in[:, first:width] = b[:n, :rest]
    g_in[:, width : width + first] = a[n:, :first]
    g_in[:, width + first :] = b[n:, :rest]
    g_out[:, :half] = a[:n, first:]
    g_out[:, half:] = a[n:, first:]
    rows = b[:n, rest:].T
    g_gains[...] = rows[0:2]
    g_biases[...] = rows[2:7]


def out_bias_body(place, biases, up1, down1, up2, down2):
    lo = 0
    for out, at in ((up1, place[7]), (down1, place[4]), (up2, place[7]), (down2, place[4])):
        n = out.shape[1]
        out[...] = biases[:, pl.ds(pl.multiple_of(lo + at * n, 128), n)]
        lo += 2 * n


def swap(v, axis, distance=1):
    return lax.ppermute(v, axis, [(i, i ^ distance) for i in range(lax.axis_size(axis))])


def add(a, b):
    return (a.astype(F32) + b.astype(F32)).astype(BF)


class Flight:
    def __init__(self, steps):
        self.steps, self.result = steps, None
        self.waits = next(steps)

    def land(self, arrays):
        try:
            self.waits = self.steps.send(arrays)
        except StopIteration as end:
            self.waits, self.result = None, end.value


def land(flights, outs=()):
    flights = [f for f in flights if f.waits is not None]
    outs, arrays = lax.optimization_barrier((outs, [f.waits for f in flights]))
    for flight, landed in zip(flights, arrays):
        flight.land(landed)
    return outs


def finish(flight):
    while flight.waits is not None:
        flight.land(flight.waits)
    return flight.result


def gather_all(v, order):
    for axis, distance in order[:-1]:
        (got,) = yield (swap(v, axis, distance),)
        v = jnp.concatenate([v, got], axis=0)
    (last,) = yield (swap(v, *order[-1]),)
    a, b = yield (swap(v, "tc"), swap(last, "tc"))
    return v, last, a, b


def gather_lanes(v, cut):
    for axis, distance in GATHER_A[:2]:
        (got,) = yield (swap(v, axis, distance),)
        v = jnp.concatenate([v, got], axis=0)
    a, b = v[:, :cut], v[:, cut:]
    one, two = yield (swap(a, *GATHER_A[2]), swap(b, *GATHER_B[2]))
    a, b = jnp.concatenate([a, one], axis=0), jnp.concatenate([b, two], axis=0)
    one, two = yield (swap(a, *GATHER_A[3]), swap(b, *GATHER_B[3]))
    got = yield (swap(a, "tc"), swap(one, "tc"), swap(b, "tc"), swap(two, "tc"))
    return (a, one, *got[:2]), (b, two, *got[2:])


def scatter_lanes(one, two, small=None):
    extra = [] if small is None else [small]
    a, b, *got = yield (swap(one[1], "tc"), swap(two[1], "tc"), *(swap(v, "tc") for v in extra))
    a, b = add(one[0], a), add(two[0], b)
    for k in range(2):
        extra = [v + w for v, w in zip(extra, got)]
        half = a.shape[0] // 2
        one, two, *got = yield (
            swap(a[half:], *SCATTER_A[k]), swap(b[half:], *SCATTER_B[k]), *(swap(v, *SCATTER_A[k]) for v in extra)
        )
        a, b = add(a[:half], one), add(b[:half], two)
    v = jnp.concatenate([a, b], axis=1)
    for k in (2, 3):
        extra = [v + w for v, w in zip(extra, got)]
        half = v.shape[0] // 2
        one, *got = yield (swap(v[half:], *SCATTER_A[k]), *(swap(w, *SCATTER_A[k]) for w in extra))
        v = (v[:half], one) if k == 3 else add(v[:half], one)
    return v, [v + w for v, w in zip(extra, got)]


def reduce_feed(ups, downs):
    got = yield tuple(swap(v, "tc") for v in (ups[1], ups[3], downs[1], downs[3]))
    up, up_far, down, down_far = (
        add(v, w) for v, w in zip((ups[0], ups[2], downs[0], downs[2]), got)
    )
    half = up.shape[0] // 2
    one, two, three = yield (
        swap(up_far, "tr"), swap(down[half:], "dp", 1), swap(down_far[half:], "dp", 1)
    )
    up, down, down_far = add(up, one), add(down[:half], two), add(down_far[:half], three)
    one, two = yield (swap(up[half:], "dp", 1), swap(down_far, "tr"))
    up, down = add(up[:half], one), add(down, two)
    shape = (4, half // 4, up.shape[1])
    v = jnp.concatenate([up.reshape(shape), down.reshape(shape)], axis=1)
    for distance in (2, 4):
        half = v.shape[0] // 2
        (got,) = yield (swap(v[half:], "dp", distance),)
        v = add(v[:half], got)
    for distance in (4, 2):
        (got,) = yield (swap(v, "dp", distance),)
        v = jnp.concatenate([v, got], axis=0)
    (got,) = yield (swap(v, "dp", 1),)
    return v, got


def chip_axes(order):
    return [{("dp", 4): 0, ("dp", 2): 1, ("dp", 1): 2, ("tr", 1): 3}[step] for step in order]


def cut_gathered(whole, order, halves):
    rows, width = whole.shape
    if halves:
        v = whole.reshape(32, rows // 32, 2, width // 2).transpose(0, 2, 1, 3)
        v = v.reshape(32, rows // 16, width // 2)
    else:
        v = whole.reshape(32, rows // 32, width)
    v = v.reshape((2, 2, 2, 2, 2) + v.shape[1:])
    first = chip_axes(order)
    v = v.transpose(first[3], 4, first[2], first[1], first[0], 5, 6)
    v = v.reshape(2, 2, -1, v.shape[-1])
    return v[0, 0], v[1, 0], v[0, 1], v[1, 1]


def join_scattered(pair, order, halves):
    v = jnp.stack(pair)
    v = v.reshape(2, 2, 2, 2, 2, v.shape[1] // 16, v.shape[2])
    first = chip_axes(order)
    v = v.transpose(*(1 + first.index(k) for k in range(4)), 0, 5, 6)
    v = v.reshape(32, v.shape[5], v.shape[6])
    if halves:
        v = v.reshape(32, 2, v.shape[1] // 2, v.shape[2]).transpose(0, 2, 1, 3)
        v = v.reshape(32, v.shape[1], -1)
    return v.reshape(-1, v.shape[-1])


def call2(body, outs, args, **more):
    return call(body, outs, args, smem=1, **more)


class Sentence:
    def __init__(self, place, tokens, mask_pos, cot):
        self.place = place
        span, self.width = tokens.shape
        masks = mask_pos.shape[1]
        self.span, self.kept = span, span - masks
        self.rows = -(-(self.kept + 1) // 16) * 16
        self.width2 = cot.shape[1]
        self.x, self.cot, self.spots = call(
            partial(prep_body, self.kept),
            [((self.rows, self.width), BF), ((self.rows, self.width2), F32), ((span, 1), jnp.int32)],
            [mask_pos.reshape(masks, 1), mask_pos, tokens, cot],
            us=3,
        )

    def enc_attn(self, one_a, one_b):
        rows, width = self.rows, self.width
        self.normed, self.packed, self.att_t, self.lse, self.e_in, self.e_par = call2(
            partial(enc_attn_body, self.kept),
            [((rows, width), BF), ((rows, 3 * width), BF), ((width, rows), BF),
             ((width // 128, rows * (128 * HEADS // width)), F32), ((width, 3 * width), BF),
             ((16, width), F32)],
            [self.place, self.x, *one_a, *one_b],
            scratch=[((width, 128), BF)],
            keep=(0, 1, 2, 3, 4, 5),
            us=12,
        )

    def enc_feed(self, two, weights):
        rows, width, units = self.rows, self.width, weights.shape[1]
        hidden = 2 * units
        self.e_weights = weights
        self.middle, self.normed_two, self.active, self.slope, self.e_low, self.e_out, self.embed = call2(
            enc_feed_body,
            [((rows, width), F32), ((rows, width), BF), ((rows, hidden), BF), ((rows, hidden), BF),
             ((rows, width), BF), ((width, width), BF), ((width, self.width2), BF)],
            [self.place, self.x, self.att_t, *two, self.e_par, weights],
            scratch=[((width, hidden), BF), ((hidden, width), BF), ((rows, width), F32),
                     ((4, 16, units), BF), ((1, hidden), F32)],
            hbm_args=1,
            sems=8 + 8 * units // width,
            keep=(0, 1, 2, 3, 4, 5, 6),
            from_hbm=True,
            us=15,
        )

    def dec_attn(self, three):
        rows, width = self.rows, self.width2
        (self.stream2, self.normed2, self.packed2, self.att2_t, self.lse2, self.d_in, self.d_out,
         self.d_par) = call2(
            partial(dec_attn_body, self.kept),
            [((rows, width), F32), ((rows, width), BF), ((rows, 3 * width), BF), ((width, rows), BF),
             ((width // 128, rows * (128 * HEADS2 // width)), F32), ((width, 3 * width), BF),
             ((width, width), BF), ((16, width), F32)],
            [self.place, self.e_low, self.embed, *three],
            scratch=[((width, 128), BF)],
            keep=(0, 1, 2, 3, 4, 5, 6, 7),
            from_hbm=True,
            us=11,
        )

    def dec_feed(self, weights):
        rows, width, units = self.rows, self.width2, weights.shape[1]
        hidden = 2 * units
        (self.out, *g_ff, self.g_middle2, self.g_att2, self.go20, self.go21, self.small2,
         self.biases2) = call2(
            partial(dec_feed_body, self.kept),
            [((rows, width), F32), *[((width // 2, hidden // 2), BF)] * 8, ((rows, width), F32),
             ((rows, width), BF), ((width // 2, width), BF), ((width // 2, width), BF),
             ((16, width), F32), ((1, hidden + width), F32)],
            [self.place, self.stream2, self.att2_t, self.d_out, self.d_par, self.cot, weights],
            scratch=[((width, hidden), BF), ((hidden, width), BF), ((rows, hidden), BF),
                     ((rows, hidden), BF), ((rows, width), F32), ((rows, width), BF),
                     ((rows, width), BF), ((width, rows), BF), ((width, rows), BF),
                     ((width, rows), BF), ((width, rows), F32), ((width, rows), F32),
                     ((rows, width), BF), ((4, 16, units), BF), ((1, hidden), F32)],
            hbm_args=1,
            sems=8 + 8 * units // width,
            keep=(0,),
            from_hbm=True,
            us=16,
        )
        self.ff2 = (g_ff[:4], g_ff[4:])

    def dec_attn_back(self):
        rows, width = self.rows, self.width2
        ga0, ga1, gb0, gb1, self.g_enc, _ = call2(
            partial(dec_attn_back_body, self.kept),
            [((width // 2, 3 * width), BF)] * 2 + [((width // 2, width + 128 + 3 * width // 2), BF)] * 2
            + [((rows, self.width), F32), ((16, width), F32)],
            [self.place, self.packed2, self.g_att2, self.lse2, self.stream2, self.normed2,
             self.g_middle2, self.d_par, self.d_in, self.embed, self.e_low, self.small2, self.go20,
             self.go21],
            scratch=[((rows, 3 * width), BF), ((width, rows), BF), ((width, rows), F32),
                     ((width, rows), F32), ((width, 128), F32), ((width, 128), F32),
                     ((self.width, rows), F32), ((self.width, rows), F32), ((rows, width), BF)],
            us=16,
        )
        self.gi2 = ((ga0, ga1), (gb0, gb1))

    def _feed_back(self, hidden):
        rows, width = self.rows, self.width
        scratch = [((width, hidden // 2), BF), ((hidden // 2, width), BF), ((rows, width), BF),
                   ((width, rows), BF), ((width, rows), BF), ((width, rows), BF)]
        return [((width // 2, hidden // 4), BF)] * 8, scratch

    def enc_feed_back_one(self):
        rows, width, hidden = self.rows, self.width, self.active.shape[1]
        ff, scratch = self._feed_back(hidden)
        (*g_ff, self.total, self.biases1) = call2(
            enc_feed_back_one_body,
            [*ff, ((rows, width), F32), ((1, hidden + width), F32)],
            [self.place, self.g_enc, self.normed_two, self.active, self.slope, self.e_weights],
            scratch=scratch,
            hbm_args=1,
            sems=4 + 4 * hidden // width,
            us=14,
        )
        self.ffa = (g_ff[:4], g_ff[4:])

    def enc_feed_back_two(self):
        rows, width, hidden = self.rows, self.width, self.active.shape[1]
        ff, scratch = self._feed_back(hidden)
        (*g_ff, self.g_middle, self.g_att, go0, go1, self.small, self.biases) = call2(
            enc_feed_back_two_body,
            [*ff, ((rows, width), F32), ((rows, width), BF), ((width, width // 2), BF),
             ((width, width // 2), BF), ((16, width), F32),
             ((1, self.biases1.shape[1] + self.biases2.shape[1]), F32)],
            [self.place, self.g_enc, self.normed_two, self.active, self.slope, self.total, self.biases1,
             self.biases2, self.middle, self.e_par, self.att_t, self.e_out, self.e_weights],
            scratch=[((rows, width), F32), *scratch, ((width, rows), F32), ((width, rows), F32),
                     ((rows, width), BF)],
            hbm_args=1,
            sems=4 + 4 * hidden // width,
            us=19,
        )
        self.ffb = (g_ff[:4], g_ff[4:])
        self.go = (go0, go1)

    def enc_attn_back_one(self):
        rows, width = self.rows, self.width
        (self.g_packed,) = call2(
            partial(enc_attn_back_one_body, self.kept),
            [((rows, 3 * width), BF)],
            [self.place, self.packed, self.g_att, self.lse],
            scratch=[((width, rows), BF)],
            us=12,
        )

    def enc_attn_back_two(self):
        rows, width = self.rows, self.width
        n = 3 * width // 2 - CUT_BACK
        ga0, ga1, gb0, gb1, self.g_stream, _ = call2(
            enc_attn_back_two_body,
            [((width, CUT_BACK + width // 2), BF)] * 2 + [((width, n + 128), BF)] * 2
            + [((rows, width), F32), ((16, width), F32)],
            [self.place, self.g_packed, self.x, self.normed, self.g_middle, self.e_par, self.e_in,
             self.small, *self.go],
            scratch=[((width, rows), F32), ((width, rows), F32), ((width, 128), F32),
                     ((width, 128), F32)],
            us=9,
        )
        self.gi = ((ga0, ga1), (gb0, gb1))

    def spread(self):
        return call(
            partial(spread_body, self.kept),
            [((self.span, self.width2), F32), ((self.span, self.width), F32)],
            [self.spots, self.out, self.g_stream],
            us=LAST,
        )

    def land(self, flights, names=(), more=()):
        names = ["place", *names]
        values, more = land(flights, ([getattr(self, n) for n in names], more))
        for name, value in zip(names, values):
            setattr(self, name, value)
        return more


CUT = 640
CUT_BACK = 512


def whole_weights(params, inproj, outproj, embed=None):
    columns = jnp.pad(params, ((0, 0), (0, 128 - params.shape[1])))
    if embed is None:
        return (jnp.concatenate([inproj, outproj, columns], axis=1),)
    n, m, k = inproj.shape[1] // 2, outproj.shape[1] // 2, embed.shape[1] // 2
    one_a = [inproj[:, :CUT], inproj[:, n : n + CUT]]
    one_b = [inproj[:, CUT:n], columns, inproj[:, n + CUT :], jnp.zeros_like(columns)]
    two = [outproj[:, :m], embed[:, :k], outproj[:, m:], embed[:, k:]]
    return tuple(jnp.concatenate(v, axis=1) for v in (one_a, one_b, two))


def local(
    tokens_in, valid_len, mask_pos,
    encoder_gains, encoder_biases, encoder_inproj, encoder_outproj,
    encoder_up, encoder_upbias, encoder_down, encoder_downbias,
    embed_weight, mask_token,
    decoder_gains, decoder_biases, decoder_inproj, decoder_outproj,
    decoder_up, decoder_upbias, decoder_down, decoder_downbias,
    cotangent,
):
    dp, tr, tc = (lax.axis_index(a) for a in ALL)
    blocks = tuple(lax.axis_size(a) for a in ALL) == (8, 2, 2)
    width, width2 = tokens_in.shape[1], cotangent.shape[1]
    hidden, hidden2 = 2 * encoder_up.shape[1], 2 * decoder_up.shape[1]
    masked = jnp.sum((mask_pos[0] < valid_len[0]).astype(jnp.int32))
    at = (dp, tr, tc, dp) if blocks else (0, 0, 0, 0)
    place = jnp.stack([jnp.int32(v) for v in (*at, tc, valid_len[0] - masked, masked, tr)])

    def feed(up, up_bias, down, down_bias):
        rows, units = 2 * up.shape[0] + 16, up.shape[1]
        args = [up, up_bias[None], down, down_bias[None]]
        (packed,) = call(pack_feed_body, [((rows, units), BF)], args, from_hbm=True)
        return lax.all_gather(packed, ("tr", "tc"), axis=0, tiled=True)

    enc = [encoder_up, encoder_upbias, encoder_down, encoder_downbias]
    dec = [decoder_up, decoder_upbias, decoder_down, decoder_downbias]
    if blocks:
        one, two, three = call(
            pack_body,
            [((48, 3 * width // 2 + 128), BF), ((48, width // 2 + width2 // 2), BF),
             ((16, 4 * width2 + 128), BF)],
            [encoder_gains.T, encoder_biases.T, encoder_inproj, encoder_outproj, embed_weight,
             decoder_gains.T, decoder_biases.T, mask_token[None], decoder_inproj, decoder_outproj],
            from_hbm=True,
        )
        enc = feed(*enc)
        one = Flight(gather_lanes(one, CUT))
        two, three = Flight(gather_all(two, GATHER_C)), Flight(gather_all(three, GATHER_D))
        place, dec = land([one], (place, dec))
        dec = feed(*dec)
        (tokens_in,) = land([one, two, three], (tokens_in,))
        sentence = Sentence(place, tokens_in, mask_pos, cotangent)
        sentence.land([one], ["x"])
        sentence.land([one, two], ["x"])
        sentence.land([one, two, three], ["x"])
        one_a, one_b = one.result
    else:
        def whole(v):
            return lax.all_gather(v, ALL, axis=0, tiled=True)

        e_par = whole(jnp.concatenate([encoder_gains, encoder_biases], axis=1))
        d_par = whole(jnp.concatenate([decoder_gains, decoder_biases, mask_token[:, None]], axis=1))
        one_a, one_b, two = whole_weights(
            e_par, whole(encoder_inproj), whole(encoder_outproj), whole(embed_weight)
        )
        (three,) = whole_weights(d_par, whole(decoder_inproj), whole(decoder_outproj))
        one_a, one_b = cut_gathered(one_a, GATHER_A, True), cut_gathered(one_b, GATHER_B, True)
        two = cut_gathered(two, GATHER_C, True)
        three = cut_gathered(three, GATHER_D, False)
        enc, dec = feed(*enc), feed(*dec)
        sentence = Sentence(place, tokens_in, mask_pos, cotangent)

    def feed_out(rows, units, halves):
        outs = []
        for part, pair in enumerate(halves):
            count = units // len(halves)
            outs = pl.pallas_call(
                partial(out_feed_body, part),
                out_shape=[jax.ShapeDtypeStruct((rows, units), F32), jax.ShapeDtypeStruct((units, rows), F32)],
                in_specs=[pl.BlockSpec(memory_space=pltpu.SMEM)]
                + [pl.BlockSpec(memory_space=pltpu.VMEM)] * 2 + [pl.BlockSpec(memory_space=pltpu.HBM)] * len(outs),
                out_specs=[pl.BlockSpec(memory_space=pltpu.HBM)] * 2,
                scratch_shapes=[pltpu.VMEM((rows, count), F32), pltpu.VMEM((rows, count), F32),
                                pltpu.VMEM((count, rows), F32), pltpu.SemaphoreType.DMA((2,))],
                input_output_aliases={3: 0, 4: 1} if outs else {},
                compiler_params=vmem([((rows, count), F32)] * 3),
                cost_estimate=cost(LAST),
            )(place, *pair, *outs)
        return outs

    def dec_out():
        n, n2 = width // 32, width2 // 32
        return call(
            out_dec_body,
            [((n2, 3 * width2), F32), ((n2, width2), F32), ((2, n2), F32), ((6, n2), F32), ((1, n2), F32),
             ((n, width2), F32)],
            finish(gi2)[0],
            us=LAST,
        )

    def bias_out(biases):
        sizes = [hidden // 2, width // 2, hidden2 // 2, width2 // 2]
        outs = call2(out_bias_body, [((1, n), F32) for n in sizes], [place, biases], us=LAST)
        return [v[0] for v in outs]

    gathers = [two, three] if blocks else []
    sentence.enc_attn(one_a, one_b)
    sentence.land(gathers, ["att_t", "e_par"])
    sentence.land(gathers[:1], ["att_t", "e_par"])
    two = two.result if blocks else two
    sentence.enc_feed(two, enc)
    sentence.land(gathers[1:], ["e_low", "embed"])
    sentence.land(gathers[1:], ["e_low", "embed"])
    three = three.result if blocks else three
    sentence.dec_attn(three)
    sentence.dec_feed(dec)

    if blocks:
        sentence.land([], ["g_middle2", "g_att2", "ff2"])
        ff2 = Flight(reduce_feed(*sentence.ff2))
        sentence.land([ff2], ["g_middle2", "g_att2"])
        sentence.dec_attn_back()
        sentence.land([ff2], ["g_enc", "gi2"])
        gi2 = Flight(scatter_lanes(*sentence.gi2))
        sentence.land([gi2], ["g_enc"])
        sentence.enc_feed_back_one()
        sentence.land([ff2, gi2], ["total", "biases1", "ffa"])
        ffa = Flight(reduce_feed(*sentence.ffa))
        sentence.land([ffa], ["total", "biases1"])
        sentence.enc_feed_back_two()
        sentence.land([ffa, ff2, gi2], ["g_middle", "g_att", "small", "go", "biases", "ffb"])
        ffb = Flight(reduce_feed(*sentence.ffb))
        sentence.land([ffb], ["g_middle", "g_att", "small", "biases"])
        sentence.enc_attn_back_one()
        sentence.land([ffa, ffb, ff2, gi2], ["g_packed"])
        sentence.enc_attn_back_two()
        sentence.land([ffb, ffa, ff2, gi2], ["gi", "g_stream"])
        gi = Flight(scatter_lanes(*sentence.gi, sentence.biases))
        sentence.land([gi])
        dec_outs = dec_out()
        sentence.output, sentence.g_tokens = sentence.spread()
        for flight in (ffb, ffa, ff2, ffb):
            land([flight])
        dec_outs, (sentence.output, sentence.g_tokens) = land(
            [gi], (dec_outs, (sentence.output, sentence.g_tokens))
        )
        for flight in (ffa, ffb, ff2, ffa):
            land([flight])
        land([gi])
        outs2 = feed_out(width2 // 2, hidden2 // 2, [finish(ff2)])
        outs2 = land([gi], outs2)
        for flight in (ffb, ffa, ffb):
            land([flight])
        land([gi])
        outs = feed_out(width // 2, hidden // 2, [finish(ffa), finish(ffb)])
        bias_outs = bias_out(finish(gi)[1][0])
    else:
        sentence.dec_attn_back()
        sentence.enc_feed_back_one()
        sentence.enc_feed_back_two()
        sentence.enc_attn_back_one()
        sentence.enc_attn_back_two()

        def halves_of(ups, downs):
            sums = []
            for v in (ups, downs):
                near, far = add(v[0], swap(v[1], "tc")), add(v[2], swap(v[3], "tc"))
                v = lax.psum(add(near, swap(far, "tr")), "dp")
                sums.append(v.reshape(8, -1, v.shape[1]))
            v = jnp.concatenate(sums, axis=1)
            return [v[:4], v[4:]]

        outs2 = feed_out(width2 // 2, hidden2 // 2, [halves_of(*sentence.ff2)])
        halves = [halves_of(*sentence.ffa), halves_of(*sentence.ffb)]
        outs = feed_out(width // 2, hidden // 2, halves)
        bias_outs = bias_out(lax.psum(sentence.biases, ALL))
        sentence.output, sentence.g_tokens = sentence.spread()

    (g_up2, g_down2), (g_up, g_down) = outs2, outs
    b_up, b_down, b_up2, b_down2 = bias_outs
    if blocks:
        n = width // 32
        g_in2, g_out2, g_gains2, g_biases2, g_token, g_embed = dec_outs
        g_in, g_out, g_gains, g_biases = call(
            out_enc_body,
            [((n, 3 * width), F32), ((n, width), F32), ((2, n), F32), ((5, n), F32)],
            finish(gi)[0],
            us=LAST,
        )
        g_gains, g_biases, g_gains2, g_biases2 = g_gains.T, g_biases.T, g_gains2.T, g_biases2.T
        g_token = g_token[0]
    else:
        def scatter(v):
            return lax.psum_scatter(v, ALL, scatter_dimension=0, tiled=True).astype(F32)

        a = join_scattered(sentence.gi[0], SCATTER_A, True)
        b = join_scattered(sentence.gi[1], SCATTER_B, True)
        m = 3 * width // 2 - CUT_BACK
        k = CUT_BACK + width // 2
        g_in = [a[:, :CUT_BACK], b[:, :m], a[:, k : k + CUT_BACK], b[:, m + 128 : 2 * m + 128]]
        g_in = scatter(jnp.concatenate(g_in, axis=1))
        small = scatter(b[:, m : m + 128])
        g_gains, g_biases = small[:, :2], small[:, 2:7]
        g_out = scatter(jnp.concatenate([a[:, CUT_BACK:k], a[:, k + CUT_BACK :]], axis=1))
        g_in2 = scatter(join_scattered(sentence.gi2[0], SCATTER_A, False))
        k = width2 + 128
        v = join_scattered([g[:, :k] for g in sentence.gi2[1]], SCATTER_B, False)
        g_out2, small = scatter(v[:, :width2]), scatter(v[:, width2:])
        g_gains2, g_biases2, g_token = small[:, :2], small[:, 2:8], small[:, 8]
        v = [g[:, k:].reshape(16, -1, 3, width2 // 2).transpose(0, 2, 1, 3) for g in sentence.gi2[1]]
        v = [g.reshape(-1, width2 // 2) for g in v]
        g_embed = scatter(join_scattered(v, SCATTER_B, True))
    return (
        sentence.output, sentence.g_tokens, g_gains, g_biases, g_in, g_out, g_up, b_up, g_down, b_down,
        g_embed, g_token, g_gains2, g_biases2, g_in2, g_out2, g_up2, b_up2, g_down2, b_down2,
    )


def solution(mesh):
    rows = P(ALL, None)
    attention = (rows, rows, rows, rows)
    feed = (P("tc", "tr"), P("tr"), P("tr", "tc"), P("tc"))
    in_specs = (
        (rows, P(ALL), rows) + attention + feed + (rows, P(ALL)) + attention + feed + (rows,)
    )
    out_specs = (rows, rows) + attention + feed + (rows, P(ALL)) + attention + feed
    return jax.shard_map(local, mesh=mesh, in_specs=in_specs, out_specs=out_specs, check_vma=False)
```

```python
import math
from functools import partial

import jax
import jax.numpy as jnp
from jax import lax
from jax.experimental import pallas as pl
from jax.experimental.pallas import tpu as pltpu
from jax.sharding import PartitionSpec as P

HEADS = 12
HEADS2 = 16
ALL = ("dp", "tr", "tc")
EPS = 1e-06
MASKED = -1e30
LOG2E = math.log2(math.e)
F32 = jnp.float32
BF = jnp.bfloat16
SPARE_BYTES = 12 * 1024 * 1024
LAST = 0.01
WHOLE_BYTES = 58 * 1024 * 1024


def dot_nn(a, b):
    return lax.dot_general(a, b, (((1,), (0,)), ((), ())), preferred_element_type=F32)


def dot_nt(a, b):
    return lax.dot_general(a, b, (((1,), (1,)), ((), ())), preferred_element_type=F32)


def cost(us):
    return pl.CostEstimate(flops=int(us * 1e9), bytes_accessed=int(us * 3e6), transcendentals=0)


def vmem(arrays):
    total = sum(math.prod(s) * jnp.dtype(d).itemsize for s, d in arrays)
    return pltpu.CompilerParams(vmem_limit_bytes=SPARE_BYTES + total)


SAVES = []


def save(ref, columns=None):
    for entry in SAVES[-1]:
        if entry["buffer"] is ref:
            source, target = ref, entry["out"]
            if columns is not None:
                source, target = source.at[:, columns], target.at[:, columns]
            pltpu.make_async_copy(source, target, entry["sem"]).start()
            entry["started"] = True


def call(body, outs, args, scratch=(), smem=0, hbm_args=0, sems=0, keep=(), us=2, alone=False, from_hbm=False):
    count = len(args) - smem - hbm_args
    specs = [pl.BlockSpec(memory_space=pltpu.SMEM)] * smem
    specs += [pl.BlockSpec(memory_space=pltpu.VMEM)] * count
    specs += [pl.BlockSpec(memory_space=pltpu.HBM)] * hbm_args
    buffers = [outs[k] for k in keep]
    shapes = [pltpu.VMEM(s, d) for s, d in [*buffers, *scratch]]
    shapes += [pltpu.SemaphoreType.DMA((max(n, 1),)) for n in (len(keep), sems)]

    def kernel(*refs):
        ins, rest = refs[: len(args)], refs[len(args) :]
        results, rest = list(rest[: len(outs)]), rest[len(outs) :]
        own, keep_sems, own_sems = rest[:-2], rest[-2], rest[-1]
        entries = []
        for n, k in enumerate(keep):
            entries.append({"buffer": own[n], "out": results[k], "sem": keep_sems.at[n], "started": False})
            results[k] = own[n]
        SAVES.append(entries)
        body(*ins, *results, *own[len(keep) :], *((own_sems,) if sems else ()))
        SAVES.pop()
        for entry in entries:
            copy = pltpu.make_async_copy(entry["buffer"], entry["out"], entry["sem"])
            if not entry["started"]:
                copy.start()
        for entry in entries:
            pltpu.make_async_copy(entry["buffer"], entry["out"], entry["sem"]).wait()

    args = list(args)
    for k in range(smem if from_hbm else len(args) - hbm_args, len(args)):
        args[k] = pltpu.with_memory_space_constraint(args[k], pltpu.HBM)
    spaces = [pltpu.HBM if k in keep else pltpu.VMEM for k in range(len(outs))]
    return pl.pallas_call(
        kernel,
        out_shape=[
            pltpu.HBM(s, d) if k in keep else jax.ShapeDtypeStruct(s, d) for k, (s, d) in enumerate(outs)
        ],
        in_specs=specs,
        out_specs=[pl.BlockSpec(memory_space=space) for space in spaces],
        scratch_shapes=shapes,
        compiler_params=pltpu.CompilerParams(vmem_limit_bytes=WHOLE_BYTES) if alone else vmem([*buffers, *scratch]),
        cost_estimate=cost(us),
    )(*args)


def norm_parts(v):
    center = v - jnp.mean(v, axis=-1, keepdims=True)
    r = lax.rsqrt(jnp.mean(center * center, axis=-1, keepdims=True) + EPS)
    return center * r, r


def norm_back(u, r, gain, y):
    e = y * gain
    back = r * (e - jnp.mean(e, axis=-1, keepdims=True) - u * jnp.mean(e * u, axis=-1, keepdims=True))
    return back, jnp.sum(y * u, axis=0, keepdims=True), jnp.sum(y, axis=0, keepdims=True)


def split3(v):
    hi = v.astype(BF)
    rest = v - hi.astype(F32)
    mid = rest.astype(BF)
    return hi, mid, (rest - mid.astype(F32)).astype(BF)


def head_masks(head_size):
    lane = lax.broadcasted_iota(jnp.int32, (1, 128), 1) // head_size
    return [(lane == h).astype(F32).astype(BF) for h in range(128 // head_size)]


def stack_heads(rows, masks):
    return jnp.concatenate([rows * m for m in masks], axis=0)


def prep_body(kept, mp_col, mp_row, tokens, cot, x_out, cot_out, place_out):
    rows, span = x_out.shape[0], tokens.shape[0]
    wide = lax.broadcasted_iota(jnp.int32, (mp_col.shape[0], span), 1)
    below = jnp.sum((mp_col[...] < wide).astype(F32), axis=0, keepdims=True)
    here = jnp.sum((mp_col[...] == wide).astype(F32), axis=0, keepdims=True)
    place = jnp.where(here > 0, kept, wide[:1] - below.astype(jnp.int32))
    pick = lax.broadcasted_iota(jnp.int32, (rows, span), 0) == place
    pick_f = pick.astype(F32)
    cot_out[...] = dot_nn(pick_f.astype(BF), cot[...])
    keep = lax.broadcasted_iota(jnp.int32, (rows, span), 0) < kept
    x_out[...] = dot_nn(jnp.where(keep, pick_f, 0.0).astype(BF), tokens[...]).astype(BF)
    tall = lax.broadcasted_iota(jnp.int32, (span, mp_row.shape[1]), 0)
    below_t = jnp.sum((mp_row[...] < tall).astype(F32), axis=1, keepdims=True)
    here_t = jnp.sum((mp_row[...] == tall).astype(F32), axis=1, keepdims=True)
    place_out[...] = jnp.where(here_t > 0, kept, tall[:, :1] - below_t.astype(jnp.int32))


def spread_back(place, rows, limit):
    at = lax.broadcasted_iota(jnp.int32, (place.shape[0], rows), 1)
    return jnp.where(at < limit, (at == place).astype(F32), 0.0).astype(BF)


def key_bias(lens, kept, rows, with_mask_row):
    at = lax.broadcasted_iota(jnp.int32, (rows, 1), 0)
    bias = jnp.where(at < lens[0], 0.0, MASKED)
    if with_mask_row:
        count = jnp.full((rows, 1), lens[1], jnp.int32).astype(F32)
        bias = jnp.where(at == kept, jnp.log(count) * LOG2E, bias)
    return bias


def attention_forward(packed, att_t, lse, bias, head_size):
    width = packed.shape[1] // 3
    rows = packed.shape[0]
    masks = head_masks(head_size)
    scale = head_size**-0.5 * LOG2E

    def group(g, carry):
        at = pl.multiple_of(g * 128, 128)
        q = packed[:, pl.ds(at, 128)]
        k = packed[:, pl.ds(width + at, 128)]
        v_t = packed[:, pl.ds(2 * width + at, 128)].T
        scores = dot_nt(k, stack_heads(q, masks)) * scale + bias
        peak = jnp.max(scores, axis=0, keepdims=True)
        weights = jnp.exp2(scores - peak)
        total = jnp.sum(weights, axis=0, keepdims=True)
        out = dot_nn(v_t, weights.astype(BF)) * (1.0 / total)
        for h in range(len(masks)):
            block = out[h * head_size : (h + 1) * head_size, h * rows : (h + 1) * rows]
            att_t[pl.ds(at + h * head_size, head_size), :] = block.astype(BF)
        lse[pl.ds(g, 1), :] = peak + jnp.log(total) * LOG2E
        return carry

    lax.fori_loop(0, width // 128, group, 0)


def attention_backward(packed, g_att, lse, g_packed, gq_t, bias, head_size):
    width = packed.shape[1] // 3
    rows = packed.shape[0]
    masks = head_masks(head_size)
    scale = head_size**-0.5

    def group(g, carry):
        at = pl.multiple_of(g * 128, 128)
        q = packed[:, pl.ds(at, 128)]
        k = packed[:, pl.ds(width + at, 128)]
        v = packed[:, pl.ds(2 * width + at, 128)]
        q_s = stack_heads(q, masks)
        g_s = stack_heads(g_att[:, pl.ds(at, 128)], masks)
        scores = dot_nt(k, q_s) * (scale * LOG2E) + bias
        probs = jnp.exp2(scores - lse[pl.ds(g, 1), :])
        g_v = dot_nn(probs.astype(BF), g_s)
        g_probs = dot_nt(v, g_s)
        delta = jnp.sum(g_probs * probs, axis=0, keepdims=True)
        g_scores = (probs * (g_probs - delta)).astype(BF)
        g_k = dot_nn(g_scores, q_s) * scale
        out = dot_nn(k.T, g_scores) * scale
        for h in range(len(masks)):
            block = out[h * head_size : (h + 1) * head_size, h * rows : (h + 1) * rows]
            gq_t[pl.ds(at + h * head_size, head_size), :] = block.astype(BF)
        g_packed[:, pl.ds(width + at, 128)] = g_k.astype(BF)
        g_packed[:, pl.ds(2 * width + at, 128)] = g_v.astype(BF)
        return carry

    lax.fori_loop(0, width // 128, group, 0)
    g_packed[:, :width] = gq_t[...].T


def project_in(stream, params, inproj, normed_out, packed_out):
    u, r = norm_parts(stream)
    normed = (u * params[0:1, :] + params[2:3, :]).astype(BF)
    normed_out[...] = normed
    save(normed_out)
    width = stream.shape[1]
    step = 256
    for part in range(3):
        for at in range(0, width, step):
            lo = part * width + at
            value = dot_nn(normed, inproj[:, lo : lo + step])
            if part == 0:
                value = value + params[3:4, at : at + step]
            if part == 2:
                value = value + params[4:5, at : at + step]
            packed_out[:, lo : lo + step] = value.astype(BF)
    save(packed_out)


GATHER_A = (("tr", 1), ("dp", 4), ("dp", 2), ("dp", 1))
GATHER_B = (("tr", 1), ("dp", 4), ("dp", 1), ("dp", 2))
GATHER_C = (("tr", 1), ("dp", 4), ("dp", 2), ("dp", 1))
GATHER_D = (("tr", 1), ("dp", 1), ("dp", 4), ("dp", 2))
SCATTER_A = (("dp", 1), ("tr", 1), ("dp", 2), ("dp", 4))
SCATTER_B = (("tr", 1), ("dp", 1), ("dp", 2), ("dp", 4))
FEED = (("dp", 1), ("dp", 2), ("dp", 4))


def differences(order, bits):
    dp = tr = 0
    for (axis, distance), bit in zip(order, bits):
        if axis == "dp":
            dp = dp + distance * bit
        else:
            tr = tr + bit
    return dp, tr


def gathered_block(order, j, last):
    return differences(order, (j & 1, (j >> 1) & 1, (j >> 2) & 1, last))


def scattered_block(order, m):
    return differences(order, (m >> 3, (m >> 2) & 1, (m >> 1) & 1, m & 1))


def feed_block(m):
    return differences(FEED, (m >> 2, (m >> 1) & 1, m & 1))[0]


def place_rows(place, order, sources, block, put):
    first = place[2] == 0
    for x in range(2):
        own_ref, oth_ref = sources[x], sources[2 + x]
        count = own_ref.shape[0] // block

        def one(j, carry, own_ref=own_ref, oth_ref=oth_ref, x=x):
            dp, tr = gathered_block(order, j, x)
            chip = (place[0] ^ dp) * 2 + (place[1] ^ tr)
            at = pl.multiple_of(j * block, block)
            own = own_ref[pl.ds(at, block), :].astype(F32)
            oth = oth_ref[pl.ds(at, block), :].astype(F32)
            put(chip, jnp.where(first, own, oth), jnp.where(first, oth, own))
            return carry

        lax.fori_loop(0, count, one, 0)


def place_halves(place, order, sources, cuts):
    block = sources[0].shape[0] // 8
    half = block // 2

    def put(chip, low, high):
        at = pl.multiple_of(chip * block, block)
        top = jnp.concatenate([low[:half], high[:half]], axis=0).astype(BF)
        bottom = jnp.concatenate([low[half:], high[half:]], axis=0).astype(BF)
        lo = 0
        for target, first, width, shift in cuts:
            target[pl.ds(at, block), first : first + width] = top[:, lo : lo + width]
            if shift is not None:
                right = first + shift
                target[pl.ds(at, block), right : right + width] = bottom[:, lo : lo + width]
            lo += width

    place_rows(place, order, sources, block, put)


def place_whole(place, order, sources, cuts):
    block = sources[0].shape[0] // 8

    def put(chip, low, high):
        at = pl.multiple_of(chip * 2 * block, 2 * block)
        both = jnp.concatenate([low, high], axis=0).astype(BF)
        lo = 0
        for target, width in cuts:
            target[pl.ds(at, 2 * block), :] = both[:, lo : lo + width]
            lo += width

    place_rows(place, order, sources, block, put)


def param_rows(columns):
    return columns[...].astype(F32).T[:16]


def reorder_rows(place, order, source, target):
    block = source.shape[0] // 32
    for core in range(2):
        for m in range(16):
            dp, tr = scattered_block(order, m)
            device = ((place[0] ^ dp) * 2 + (place[1] ^ tr)) * 2 + (place[2] ^ core)
            at = pl.multiple_of(device * block, 8)
            to = (core * 16 + m) * block
            target[to : to + block, :] = source[pl.ds(at, block), :]


def write_halves(ordered, columns, outs, first=0, count=None):
    half_rows = ordered.shape[0] // 2
    block = half_rows // 16
    width = columns.shape[1] // 2
    count = width if count is None else count
    step = max(n for n in (384, 320, 256) if count % n == 0) if count != 640 else 640
    for core in range(2):
        rows = ordered[core * half_rows : (core + 1) * half_rows, :].astype(BF)
        for at in range(first, first + count, step):
            left = dot_nn(rows, columns[:, at : at + step])
            right = dot_nn(rows, columns[:, width + at : width + at + step])
            for m in range(16):
                both = [left[m * block : (m + 1) * block], right[m * block : (m + 1) * block]]
                outs[core][m * 2 * block : (m + 1) * 2 * block, at - first : at - first + step] = (
                    jnp.concatenate(both, axis=0).astype(BF)
                )


def write_whole(ordered, columns, outs, lo):
    half_rows = ordered.shape[0] // 2
    width = columns.shape[1]
    for core in range(2):
        rows = ordered[core * half_rows : (core + 1) * half_rows, :].astype(BF)
        for at in range(0, width, 256):
            outs[core][:, lo + at : lo + at + 256] = dot_nn(rows, columns[:, at : at + 256]).astype(BF)


def small_columns(small):
    table = jnp.concatenate([small[...], jnp.zeros((112, small.shape[1]), F32)], axis=0)
    return table.T


def pack_body(
    e_gains, e_biases, e_in, e_out, embed, d_gains, d_biases, token, d_in, d_out, one, two, three
):
    def columns(parts):
        total, lo = 0.0, 0
        for part in parts:
            count, rows = part.shape
            spot = lax.broadcasted_iota(jnp.int32, (count, 128), 1)
            want = lax.broadcasted_iota(jnp.int32, (count, 128), 0) + lo
            table = (spot == want).astype(F32).astype(BF)
            total = total + lax.dot_general(
                part[...], table, (((0,), (0,)), ((), ())), preferred_element_type=F32
            )
            lo += count
        return total

    e_par = columns([e_gains, e_biases])

    def halves(v):
        v = v[...].astype(F32)
        width = v.shape[1] // 2
        return jnp.concatenate([v[:, :width], v[:, width:]], axis=0).astype(BF)

    n = e_in.shape[1] // 2
    one[:, :n] = halves(e_in)
    one[:, n:] = jnp.concatenate([e_par, jnp.zeros_like(e_par)], axis=0).astype(BF)
    n = e_out.shape[1] // 2
    two[:, :n] = halves(e_out)
    two[:, n:] = halves(embed)
    n = d_in.shape[1]
    m = n + d_out.shape[1]
    three[:, :n] = d_in[...]
    three[:, n:m] = d_out[...]
    three[:, m:] = columns([d_gains, d_biases, token]).astype(BF)


def enc_attn_body(
    kept, place, x, s0, s1, s2, s3, r0, r1, r2, r3,
    normed, packed, att_t, lse, inproj, par_t, par_c,
):
    width = x.shape[1]
    n, shift = s0.shape[1], 3 * width // 2
    place_halves(place, GATHER_A, (s0, s1, s2, s3), ((inproj, 0, n, shift),))
    place_halves(
        place, GATHER_B, (r0, r1, r2, r3), ((inproj, n, shift - n, shift), (par_c, 0, 128, None))
    )
    save(inproj)
    par_t[...] = param_rows(par_c)
    project_in(x[...].astype(F32), par_t, inproj, normed, packed)
    bias = key_bias((place[5], place[6]), kept, x.shape[0], False)
    attention_forward(packed, att_t, lse, bias, width // HEADS)


def dec_attn_body(
    kept, place, e_low, embed, s0, s1, s2, s3,
    stream, normed, packed, att_t, lse, inproj, outproj, params, par_c,
):
    rows = e_low.shape[0]
    width = stream.shape[1]
    place_whole(
        place, GATHER_D, (s0, s1, s2, s3), ((inproj, 3 * width), (outproj, width), (par_c, 128))
    )
    save(inproj)
    save(outproj)
    params[...] = param_rows(par_c)
    embedded = dot_nn(e_low[...], embed[...]) + params[7:8, :]
    at = lax.broadcasted_iota(jnp.int32, (rows, 1), 0)
    decoded = jnp.where(at < kept, embedded, params[8:9, :])
    stream[...] = decoded
    save(stream)
    project_in(decoded, params, inproj, normed, packed)
    bias = key_bias((place[5], place[6]), kept, rows, True)
    attention_forward(packed, att_t, lse, bias, width // HEADS2)


def pack_feed_body(up, up_bias, down, down_bias, out):
    rows, width = up.shape[0], down.shape[1]
    out[:rows, :] = up[...]
    for at in range(0, up.shape[1], width):
        out[rows : 2 * rows, at : at + width] = down[at : at + width, :]
    row = lax.broadcasted_iota(jnp.int32, (16, up.shape[1]), 0)
    value = jnp.where(row == 0, up_bias[...].astype(F32), 0.0)
    out[2 * rows :, :] = value.astype(BF)
    row = lax.broadcasted_iota(jnp.int32, (16, width), 0)
    value = jnp.where(row == 1, down_bias[...].astype(F32), value[:, :width])
    out[2 * rows :, :width] = value.astype(BF)


def load_feed(place, gathered, up, down, sems, part=0, biases=None):
    copies = []
    groups = []
    half = up.shape[0] // 2
    units = up.shape[1] // 2
    block = gathered.shape[0] // 4

    def start(source, target):
        copies.append(pltpu.make_async_copy(source, target, sems.at[len(copies)]))
        copies[-1].start()

    for tr in range(2):
        for core in range(2):
            base = ((place[7] ^ tr) * 2 + core) * block

            def rows(at, count, base=base):
                return pl.ds(pl.multiple_of(base + at, 16), count)

            columns = pl.ds(tr * units, units)
            start(
                gathered.at[rows(0, half), pl.ds(part * units, units)],
                up.at[pl.ds(core * half, half), columns],
            )
            for at in range(0, units, half):
                start(
                    gathered.at[rows(half, half), pl.ds(part * units + at, half)],
                    down.at[pl.ds(tr * units + at, half), pl.ds(core * half, half)],
                )
            if biases is not None:
                start(gathered.at[rows(2 * half, 16), :], biases.at[2 * tr + core])
        groups.append(copies[sum(len(g) for g in groups) :])
    return groups


def wait(copies):
    for copy in copies:
        copy.wait()


def bias_rows(biases, half):
    return jnp.concatenate([biases[0, 1:2, :half], biases[1, 1:2, :half]], axis=1).astype(F32)


def middle_of(stream, att_t, outproj, params):
    return stream + dot_nn(att_t[...].T, outproj[...]) + params[5:6, :]


def feed_forward(
    normed_two, up, up_bias, down, active_out, slope_out, total, step, copies, biases
):
    units = up.shape[1] // 2
    total[...] = jnp.zeros_like(total)

    def chunk(c, carry):
        at = pl.multiple_of(c * step, step)
        hidden = dot_nn(normed_two, up[:, pl.ds(at, step)]) + up_bias[:, pl.ds(at, step)]
        phi = 0.5 * (1.0 + lax.erf(hidden * math.sqrt(0.5)))
        bell = jnp.exp2(hidden * hidden * (-0.5 * LOG2E)) * (1.0 / math.sqrt(2 * math.pi))
        active = (hidden * phi).astype(BF)
        active_out[:, pl.ds(at, step)] = active
        slope_out[:, pl.ds(at, step)] = (phi + hidden * bell).astype(BF)
        save(active_out, pl.ds(at, step))
        save(slope_out, pl.ds(at, step))
        total[...] += dot_nn(active, down[pl.ds(at, step), :])
        return carry

    for tr in range(2):
        wait(copies[tr])
        up_bias[:, tr * units : (tr + 1) * units] = biases[2 * tr, 0:1, :].astype(F32)
        lax.fori_loop(tr * units // step, (tr + 1) * units // step, chunk, 0)


def order_feed(place, source, target):
    block = source.shape[0] // 16
    for core in range(2):
        for m in range(8):
            at = ((place[4] ^ core) * 8 + (place[3] ^ feed_block(m))) * block
            to = (core * 8 + m) * block
            target[to : to + block, :] = source[pl.ds(pl.multiple_of(at, block), block), :]


def feed_backward(
    copies, place, part, parts, g_result, normed_two, active, slope, up, down,
    g_ups, g_downs, g_upbias, g_normed, step, rows_t, ordered_n, ordered_g,
):
    width = normed_two.shape[1]
    count = up.shape[1] // 2
    units = count * parts
    half = width // 2
    rows_t[...] = normed_two[...].T
    order_feed(place, rows_t, ordered_n)
    rows_t[...] = g_result[...].T
    order_feed(place, rows_t, ordered_g)
    for tr in range(2):
        wait(copies[tr])
        base = tr * units + part * count
        out_base = pl.multiple_of((place[7] ^ tr) * units + part * count, 128)

        def chunk(c, carry, tr=tr, base=base, out_base=out_base):
            at = pl.multiple_of(c * step, step)
            here = pl.ds(pl.multiple_of(tr * count + at, 128), step)
            g_active = dot_nt(g_result[...], down[here, :]).astype(BF).astype(F32)
            there = pl.ds(pl.multiple_of(base + at, 128), step)
            g_hidden = (slope[:, there].astype(F32) * g_active).astype(BF)
            g_upbias[:, pl.ds(pl.multiple_of(out_base + at, 128), step)] = jnp.sum(
                g_hidden.astype(F32), axis=0, keepdims=True
            )
            g_normed[...] += dot_nt(g_hidden, up[:, here])
            g_up = dot_nn(ordered_n[...], g_hidden).astype(BF)
            g_down = dot_nn(ordered_g[...], active[:, there]).astype(BF)
            for core in range(2):
                g_ups[2 * tr + core][:, pl.ds(at, step)] = g_up[core * half : (core + 1) * half]
                g_downs[2 * tr + core][:, pl.ds(at, step)] = g_down[core * half : (core + 1) * half]
            return carry

        lax.fori_loop(0, count // step, chunk, 0)


def after_feed_backward(
    place, order, g_out, g_normed, middle, params, att_t, outproj, g_middle, g_att, small, att_f, att_o
):
    u, r = norm_parts(middle)
    y = g_normed.astype(BF).astype(F32)
    back, g_gain, g_shift = norm_back(u, r, params[1:2, :], y)
    grad = g_out + back
    g_middle[...] = grad
    branch = grad.astype(BF)
    att_f[...] = att_t[...].astype(F32)
    reorder_rows(place, order, att_f, att_o)
    g_att[...] = dot_nt(branch, outproj[...]).astype(BF)
    small[1:2, :] = g_gain
    small[5:6, :] = jnp.sum(branch.astype(F32), axis=0, keepdims=True)
    small[6:7, :] = g_shift
    return branch


def enc_feed_body(
    place, x, att_t, s0, s1, s2, s3, params, weights,
    middle, normed_two, active, slope, e_low, outproj, embed,
    up, down, total, biases, up_bias, sems,
):
    copies = load_feed(place, weights, up, down, sems, 0, biases)
    width = x.shape[1]
    n, m = width // 2, embed.shape[1] // 2
    place_halves(place, GATHER_C, (s0, s1, s2, s3), ((outproj, 0, n, n), (embed, 0, m, m)))
    mid = middle_of(x[...].astype(F32), att_t, outproj, params)
    middle[...] = mid
    u, r = norm_parts(mid)
    n2 = (u * params[1:2, :] + params[6:7, :]).astype(BF)
    normed_two[...] = n2
    for ref in (middle, normed_two, outproj, embed):
        save(ref)
    feed_forward(n2, up, up_bias, down, active, slope, total, 512, copies, biases)
    down_bias = bias_rows(biases, width // 2)
    result = (total[...] + down_bias).astype(BF)
    e_low[...] = (middle[...] + result.astype(F32)).astype(BF)


def dec_feed_body(
    kept, place, stream, att_t, outproj, params, cot, weights,
    out, gu0, gu1, gu2, gu3, gd0, gd1, gd2, gd3, g_middle, g_att, go0, go1, small, g_biases,
    up, down, active, slope, total, n2_s, g_res, rows_t, ordered_n, ordered_g,
    att_f, att_o, branch_s, biases, up_bias, sems,
):
    copies = load_feed(place, weights, up, down, sems, 0, biases)
    mid = middle_of(stream[...], att_t, outproj, params)
    u, r = norm_parts(mid)
    n2 = (u * params[1:2, :] + params[6:7, :]).astype(BF)
    n2_s[...] = n2
    feed_forward(n2, up, up_bias, down, active, slope, total, 512, copies, biases)
    down_bias = bias_rows(biases, up.shape[0] // 2)
    result = (total[...] + down_bias).astype(BF)
    out[...] = mid + result.astype(F32)
    save(out)
    g_out = cot[...]
    g_res[...] = g_out.astype(BF)
    small[...] = jnp.zeros_like(small)
    units = up.shape[1]
    g_biases[:, units:] = jnp.sum(g_res[...].astype(F32), axis=0, keepdims=True)
    total[...] = jnp.zeros_like(total)
    feed_backward(
        ((), ()), place, 0, 1, g_res, n2_s, active, slope, up, down, (gu0, gu1, gu2, gu3), (gd0, gd1, gd2, gd3),
        g_biases, total, 512, rows_t, ordered_n, ordered_g,
    )
    branch = after_feed_backward(
        place, SCATTER_B, g_out, total[...], mid, params, att_t, outproj, g_middle, g_att, small,
        att_f, att_o,
    )
    branch_s[...] = branch
    write_whole(att_o, branch_s, (go0, go1), 0)


def enc_feed_back_one_body(
    place, g_enc, normed_two, active, slope, weights,
    gu0, gu1, gu2, gu3, gd0, gd1, gd2, gd3, total, biases, up, down, g_res, rows_t, ordered_n, ordered_g, sems,
):
    copies = load_feed(place, weights, up, down, sems)
    g_res[...] = g_enc[...].astype(BF)
    total[...] = jnp.zeros_like(total)
    biases[:, 2 * up.shape[1] :] = jnp.sum(g_res[...].astype(F32), axis=0, keepdims=True)
    feed_backward(
        copies, place, 0, 2, g_res, normed_two, active, slope, up, down, (gu0, gu1, gu2, gu3),
        (gd0, gd1, gd2, gd3), biases, total, 384, rows_t, ordered_n, ordered_g,
    )


def enc_feed_back_two_body(
    place, g_enc, normed_two, active, slope, total_in, biases_in, biases_dec, middle, params, att_t,
    outproj, weights,
    gu0, gu1, gu2, gu3, gd0, gd1, gd2, gd3, g_middle, g_att, go0, go1, small, biases,
    total, up, down, g_res, rows_t, ordered_n, ordered_g, att_f, att_o, branch_s, sems,
):
    copies = load_feed(place, weights, up, down, sems, 1)
    g_res[...] = g_enc[...].astype(BF)
    total[...] = total_in[...]
    count = biases_in.shape[1]
    biases[:, :count] = biases_in[...]
    biases[:, count:] = biases_dec[...]
    small[...] = jnp.zeros_like(small)
    feed_backward(
        copies, place, 1, 2, g_res, normed_two, active, slope, up, down, (gu0, gu1, gu2, gu3),
        (gd0, gd1, gd2, gd3), biases, total, 384, rows_t, ordered_n, ordered_g,
    )
    branch = after_feed_backward(
        place, SCATTER_A, g_enc[...], total[...], middle[...], params, att_t, outproj, g_middle,
        g_att, small, att_f, att_o,
    )
    branch_s[...] = branch
    write_halves(att_o, branch_s, (go0, go1))


def project_back(
    place, order, stream, normed, g_packed, g_middle, params, inproj, small, first, rows_f, rows_o
):
    width = stream.shape[1]
    rows_f[...] = normed[...].astype(F32).T
    reorder_rows(place, order, rows_f, rows_o)
    g_normed = dot_nt(g_packed[...], inproj[...])
    u, r = norm_parts(stream)
    back, g_gain, g_shift = norm_back(u, r, params[0:1, :], g_normed)
    small[...] = first[...]
    small[0:1, :] = g_gain
    small[2:3, :] = g_shift
    small[3:4, :] = jnp.sum(g_packed[:, :width].astype(F32), axis=0, keepdims=True)
    small[4:5, :] = jnp.sum(g_packed[:, 2 * width :].astype(F32), axis=0, keepdims=True)
    return g_middle[...] + back


def dec_attn_back_body(
    kept, place, packed, g_att, lse, stream, normed, g_middle, params, inproj, embed, e_low, first,
    go0, go1, ga0, ga1, gb0, gb1, g_enc, small, g_packed, gq_t, rows_f, rows_o, cols, cols_o,
    emb_f, emb_o, g_emb,
):
    rows = stream.shape[0]
    width = stream.shape[1]
    bias = key_bias((place[5], place[6]), kept, rows, True)
    attention_backward(packed, g_att, lse, g_packed, gq_t, bias, width // HEADS2)
    g_stream = project_back(
        place, SCATTER_A, stream[...], normed, g_packed, g_middle, params, inproj, small, first,
        rows_f, rows_o,
    )
    write_whole(rows_o, g_packed, (ga0, ga1), 0)
    at = lax.broadcasted_iota(jnp.int32, (rows, 1), 0)
    small[8:9, :] = jnp.sum(jnp.where(at == kept, g_stream, 0.0), axis=0, keepdims=True)
    g_embedded = jnp.where(at < kept, g_stream, 0.0).astype(BF)
    small[7:8, :] = jnp.sum(g_embedded.astype(F32), axis=0, keepdims=True)
    g_emb[...] = g_embedded
    g_enc[...] = dot_nt(g_embedded, embed[...])
    emb_f[...] = e_low[...].astype(F32).T
    reorder_rows(place, SCATTER_B, emb_f, emb_o)
    cols[...] = small_columns(small)
    reorder_rows(place, SCATTER_B, cols, cols_o)
    n = cols_o.shape[0] // 2
    half = emb_o.shape[0] // 2
    block, part = half // 16, g_emb.shape[1] // 2
    unit = n // 16
    for core, (gb, go) in enumerate(((gb0, go0), (gb1, go1))):
        gb[:, :width] = go[...]
        gb[:, width : width + 128] = cols_o[core * n : (core + 1) * n, :].astype(BF)
        rows_e = emb_o[core * half : (core + 1) * half, :].astype(BF)
        left, right = dot_nn(rows_e, g_emb[:, :part]), dot_nn(rows_e, g_emb[:, part:])
        for m in range(16):
            both = [left[m * block : (m + 1) * block], right[m * block : (m + 1) * block]]
            both = jnp.concatenate(both, axis=0).astype(BF)
            for k in range(2 * block // unit):
                lo = width + 128 + k * part
                gb[m * unit : (m + 1) * unit, lo : lo + part] = both[k * unit : (k + 1) * unit]


def enc_attn_back_one_body(kept, place, packed, g_att, lse, g_packed, gq_t):
    bias = key_bias((place[5], place[6]), kept, packed.shape[0], False)
    attention_backward(packed, g_att, lse, g_packed, gq_t, bias, g_att.shape[1] // HEADS)


def enc_attn_back_two_body(
    place, g_packed, x, normed, g_middle, params, inproj, first, go0, go1,
    ga0, ga1, gb0, gb1, g_stream, small, rows_f, rows_o, cols, cols_o,
):
    width = x.shape[1]
    g_stream[...] = project_back(
        place, SCATTER_A, x[...].astype(F32), normed, g_packed, g_middle, params, inproj, small, first,
        rows_f, rows_o,
    )
    m = gb0.shape[1] - 128
    n = 3 * width // 2 - m
    write_halves(rows_o, g_packed, (ga0, ga1), 0, n)
    reorder_rows(place, SCATTER_B, rows_f, rows_o)
    write_halves(rows_o, g_packed, (gb0, gb1), n, m)
    cols[...] = small_columns(small)
    reorder_rows(place, SCATTER_B, cols, cols_o)
    count = cols_o.shape[0] // 2
    block = count // 16
    for core, (a, b, go) in enumerate(((ga0, gb0, go0), (ga1, gb1, go1))):
        a[:, n:] = go[...]
        for k in range(16):
            part = cols_o[core * count + k * block : core * count + (k + 1) * block, :]
            both = jnp.concatenate([part, jnp.zeros_like(part)], axis=0).astype(BF)
            b[k * 2 * block : (k + 1) * 2 * block, m:] = both


def spread_body(kept, spots, out, g_stream, output, g_tokens):
    rows = out.shape[0]
    for limit, source, target in ((kept + 1, out, output), (kept, g_stream, g_tokens)):
        pick = spread_back(spots[...], rows, limit)
        hi, mid, low = split3(source[...])
        target[...] = dot_nn(pick, hi) + dot_nn(pick, mid) + dot_nn(pick, low)


def out_feed_body(part, count, *refs):
    place, arrays = refs[0], refs[1 : 1 + count]
    g_up, g_down, up, turned, down, sems = refs[-6:]
    units = up.shape[1]
    for k, ref in enumerate(arrays):
        block = ref.shape[1] // 2
        for m in range(ref.shape[0]):
            dp = place[3] ^ feed_block(ref.shape[0] * k + m)
            at = pl.multiple_of(dp * block, block)
            rows = ref[m].astype(F32)
            up[pl.ds(at, block), :] = rows[:block]
            turned[pl.ds(at, block), :] = rows[block:]
    here = pl.ds(part * units, units)
    first = pltpu.make_async_copy(up, g_up.at[:, here], sems.at[0])
    first.start()
    down[...] = turned[...].T
    second = pltpu.make_async_copy(down, g_down.at[here, :], sems.at[1])
    second.start()
    first.wait()
    second.wait()


def out_dec_body(mine, theirs, g_in, g_out, g_gains, g_biases, g_token, g_embed):
    total = mine[...].astype(F32) + theirs[...].astype(F32)
    n = g_in.shape[1]
    m = n + g_out.shape[1]
    g_in[...] = total[:, :n]
    g_out[...] = total[:, n:m]
    rows = total[:, m : m + 128].T
    g_gains[...] = rows[0:2]
    g_biases[...] = rows[2:8]
    g_token[...] = rows[8:9]
    half = g_embed.shape[1] // 2
    units = [total[:, m + 128 + k * half : m + 128 + (k + 1) * half] for k in range(3)]
    both = jnp.concatenate(units, axis=0)
    count = both.shape[0] // 2
    g_embed[:, :half] = both[:count]
    g_embed[:, half:] = both[count:]


def out_enc_body(mine, theirs, g_in, g_out, g_gains, g_biases):
    total = mine[...].astype(F32) + theirs[...].astype(F32)
    n, width, half = g_in.shape[0], g_in.shape[1] // 2, g_out.shape[1] // 2
    first = CUT_BACK
    a, b = total[:, : first + half], total[:, first + half :]
    rest = width - first
    g_in[:, :first] = a[:n, :first]
    g_in[:, first:width] = b[:n, :rest]
    g_in[:, width : width + first] = a[n:, :first]
    g_in[:, width + first :] = b[n:, :rest]
    g_out[:, :half] = a[:n, first:]
    g_out[:, half:] = a[n:, first:]
    rows = b[:n, rest:].T
    g_gains[...] = rows[0:2]
    g_biases[...] = rows[2:7]


def out_bias_body(place, biases, up1, down1, up2, down2):
    lo = 0
    for out, at in ((up1, place[7]), (down1, place[4]), (up2, place[7]), (down2, place[4])):
        n = out.shape[1]
        out[...] = biases[:, pl.ds(pl.multiple_of(lo + at * n, 128), n)]
        lo += 2 * n


def swap(v, axis, distance=1):
    return lax.ppermute(v, axis, [(i, i ^ distance) for i in range(lax.axis_size(axis))])


def add(a, b):
    return (a.astype(F32) + b.astype(F32)).astype(BF)


class Flight:
    def __init__(self, steps):
        self.steps, self.result = steps, None
        self.waits = next(steps)

    def land(self, arrays):
        try:
            self.waits = self.steps.send(arrays)
        except StopIteration as end:
            self.waits, self.result = None, end.value


def land(flights, outs=()):
    flights = [f for f in flights if f.waits is not None]
    outs, arrays = lax.optimization_barrier((outs, [f.waits for f in flights]))
    for flight, landed in zip(flights, arrays):
        flight.land(landed)
    return outs


def finish(flight):
    while flight.waits is not None:
        flight.land(flight.waits)
    return flight.result


def gather_all(v, order):
    for axis, distance in order[:-1]:
        (got,) = yield (swap(v, axis, distance),)
        v = jnp.concatenate([v, got], axis=0)
    (last,) = yield (swap(v, *order[-1]),)
    a, b = yield (swap(v, "tc"), swap(last, "tc"))
    return v, last, a, b


def gather_lanes(v, cut):
    for axis, distance in GATHER_A[:2]:
        (got,) = yield (swap(v, axis, distance),)
        v = jnp.concatenate([v, got], axis=0)
    a, b = v[:, :cut], v[:, cut:]
    one, two = yield (swap(a, *GATHER_A[2]), swap(b, *GATHER_B[2]))
    a, b = jnp.concatenate([a, one], axis=0), jnp.concatenate([b, two], axis=0)
    one, two = yield (swap(a, *GATHER_A[3]), swap(b, *GATHER_B[3]))
    got = yield (swap(a, "tc"), swap(one, "tc"), swap(b, "tc"), swap(two, "tc"))
    return (a, one, *got[:2]), (b, two, *got[2:])


def scatter_lanes(one, two, small=None):
    extra = [] if small is None else [small]
    a, b, *got = yield (swap(one[1], "tc"), swap(two[1], "tc"), *(swap(v, "tc") for v in extra))
    a, b = add(one[0], a), add(two[0], b)
    for k in range(2):
        extra = [v + w for v, w in zip(extra, got)]
        half = a.shape[0] // 2
        one, two, *got = yield (
            swap(a[half:], *SCATTER_A[k]), swap(b[half:], *SCATTER_B[k]), *(swap(v, *SCATTER_A[k]) for v in extra)
        )
        a, b = add(a[:half], one), add(b[:half], two)
    v = jnp.concatenate([a, b], axis=1)
    for k in (2, 3):
        extra = [v + w for v, w in zip(extra, got)]
        half = v.shape[0] // 2
        one, *got = yield (swap(v[half:], *SCATTER_A[k]), *(swap(w, *SCATTER_A[k]) for w in extra))
        v = (v[:half], one) if k == 3 else add(v[:half], one)
    return v, [v + w for v, w in zip(extra, got)]


def reduce_feed(ups, downs, x_last):
    got = yield tuple(swap(v, "tc") for v in (ups[1], ups[3], downs[1], downs[3]))
    up, up_far, down, down_far = (
        add(v, w) for v, w in zip((ups[0], ups[2], downs[0], downs[2]), got)
    )
    half = up.shape[0] // 2
    one, two, three = yield (
        swap(up_far, "tr"), swap(down[half:], "dp", 1), swap(down_far[half:], "dp", 1)
    )
    up, down, down_far = add(up, one), add(down[:half], two), add(down_far[:half], three)
    one, two = yield (swap(up[half:], "dp", 1), swap(down_far, "tr"))
    up, down = add(up[:half], one), add(down, two)
    shape = (4, half // 4, up.shape[1])
    v = jnp.concatenate([up.reshape(shape), down.reshape(shape)], axis=1)
    for distance in (2, 4):
        half = v.shape[0] // 2
        (got,) = yield (swap(v[half:], "dp", distance),)
        v = add(v[:half], got)
    (got,) = yield (swap(v, "dp", 4),)
    v = jnp.concatenate([v, got], axis=0)
    if x_last:
        (got,) = yield (swap(v, "dp", 2),)
        v = jnp.concatenate([v, got], axis=0)
        (got,) = yield (swap(v, "dp", 1),)
        return v, got
    (w,) = yield (swap(v, "dp", 1),)
    one, two = yield (swap(v, "dp", 2), swap(w, "dp", 2))
    return v, one, w, two


def chip_axes(order):
    return [{("dp", 4): 0, ("dp", 2): 1, ("dp", 1): 2, ("tr", 1): 3}[step] for step in order]


def cut_gathered(whole, order, halves):
    rows, width = whole.shape
    if halves:
        v = whole.reshape(32, rows // 32, 2, width // 2).transpose(0, 2, 1, 3)
        v = v.reshape(32, rows // 16, width // 2)
    else:
        v = whole.reshape(32, rows // 32, width)
    v = v.reshape((2, 2, 2, 2, 2) + v.shape[1:])
    first = chip_axes(order)
    v = v.transpose(first[3], 4, first[2], first[1], first[0], 5, 6)
    v = v.reshape(2, 2, -1, v.shape[-1])
    return v[0, 0], v[1, 0], v[0, 1], v[1, 1]


def join_scattered(pair, order, halves):
    v = jnp.stack(pair)
    v = v.reshape(2, 2, 2, 2, 2, v.shape[1] // 16, v.shape[2])
    first = chip_axes(order)
    v = v.transpose(*(1 + first.index(k) for k in range(4)), 0, 5, 6)
    v = v.reshape(32, v.shape[5], v.shape[6])
    if halves:
        v = v.reshape(32, 2, v.shape[1] // 2, v.shape[2]).transpose(0, 2, 1, 3)
        v = v.reshape(32, v.shape[1], -1)
    return v.reshape(-1, v.shape[-1])


def call2(body, outs, args, **more):
    return call(body, outs, args, smem=1, **more)


class Sentence:
    def __init__(self, place, tokens, mask_pos, cot):
        self.place = place
        span, self.width = tokens.shape
        masks = mask_pos.shape[1]
        self.span, self.kept = span, span - masks
        self.rows = -(-(self.kept + 1) // 16) * 16
        self.width2 = cot.shape[1]
        self.x, self.cot, self.spots = call(
            partial(prep_body, self.kept),
            [((self.rows, self.width), BF), ((self.rows, self.width2), F32), ((span, 1), jnp.int32)],
            [mask_pos.reshape(masks, 1), mask_pos, tokens, cot],
            us=3,
        )

    def enc_attn(self, one_a, one_b):
        rows, width = self.rows, self.width
        self.normed, self.packed, self.att_t, self.lse, self.e_in, self.e_par = call2(
            partial(enc_attn_body, self.kept),
            [((rows, width), BF), ((rows, 3 * width), BF), ((width, rows), BF),
             ((width // 128, rows * (128 * HEADS // width)), F32), ((width, 3 * width), BF),
             ((16, width), F32)],
            [self.place, self.x, *one_a, *one_b],
            scratch=[((width, 128), BF)],
            keep=(0, 1, 2, 3, 4, 5),
            us=12,
        )

    def enc_feed(self, two, weights):
        rows, width, units = self.rows, self.width, weights.shape[1]
        hidden = 2 * units
        self.e_weights = weights
        self.middle, self.normed_two, self.active, self.slope, self.e_low, self.e_out, self.embed = call2(
            enc_feed_body,
            [((rows, width), F32), ((rows, width), BF), ((rows, hidden), BF), ((rows, hidden), BF),
             ((rows, width), BF), ((width, width), BF), ((width, self.width2), BF)],
            [self.place, self.x, self.att_t, *two, self.e_par, weights],
            scratch=[((width, hidden), BF), ((hidden, width), BF), ((rows, width), F32),
                     ((4, 16, units), BF), ((1, hidden), F32)],
            hbm_args=1,
            sems=8 + 8 * units // width,
            keep=(0, 1, 2, 3, 4, 5, 6),
            from_hbm=True,
            us=15,
        )

    def dec_attn(self, three):
        rows, width = self.rows, self.width2
        (self.stream2, self.normed2, self.packed2, self.att2_t, self.lse2, self.d_in, self.d_out,
         self.d_par) = call2(
            partial(dec_attn_body, self.kept),
            [((rows, width), F32), ((rows, width), BF), ((rows, 3 * width), BF), ((width, rows), BF),
             ((width // 128, rows * (128 * HEADS2 // width)), F32), ((width, 3 * width), BF),
             ((width, width), BF), ((16, width), F32)],
            [self.place, self.e_low, self.embed, *three],
            scratch=[((width, 128), BF)],
            keep=(0, 1, 2, 3, 4, 5, 6, 7),
            from_hbm=True,
            us=11,
        )

    def dec_feed(self, weights):
        rows, width, units = self.rows, self.width2, weights.shape[1]
        hidden = 2 * units
        (self.out, *g_ff, self.g_middle2, self.g_att2, self.go20, self.go21, self.small2,
         self.biases2) = call2(
            partial(dec_feed_body, self.kept),
            [((rows, width), F32), *[((width // 2, hidden // 2), BF)] * 8, ((rows, width), F32),
             ((rows, width), BF), ((width // 2, width), BF), ((width // 2, width), BF),
             ((16, width), F32), ((1, hidden + width), F32)],
            [self.place, self.stream2, self.att2_t, self.d_out, self.d_par, self.cot, weights],
            scratch=[((width, hidden), BF), ((hidden, width), BF), ((rows, hidden), BF),
                     ((rows, hidden), BF), ((rows, width), F32), ((rows, width), BF),
                     ((rows, width), BF), ((width, rows), BF), ((width, rows), BF),
                     ((width, rows), BF), ((width, rows), F32), ((width, rows), F32),
                     ((rows, width), BF), ((4, 16, units), BF), ((1, hidden), F32)],
            hbm_args=1,
            sems=8 + 8 * units // width,
            keep=(0,),
            from_hbm=True,
            us=16,
        )
        self.ff2 = (g_ff[:4], g_ff[4:])

    def dec_attn_back(self):
        rows, width = self.rows, self.width2
        ga0, ga1, gb0, gb1, self.g_enc, _ = call2(
            partial(dec_attn_back_body, self.kept),
            [((width // 2, 3 * width), BF)] * 2 + [((width // 2, width + 128 + 3 * width // 2), BF)] * 2
            + [((rows, self.width), F32), ((16, width), F32)],
            [self.place, self.packed2, self.g_att2, self.lse2, self.stream2, self.normed2,
             self.g_middle2, self.d_par, self.d_in, self.embed, self.e_low, self.small2, self.go20,
             self.go21],
            scratch=[((rows, 3 * width), BF), ((width, rows), BF), ((width, rows), F32),
                     ((width, rows), F32), ((width, 128), F32), ((width, 128), F32),
                     ((self.width, rows), F32), ((self.width, rows), F32), ((rows, width), BF)],
            us=16,
        )
        self.gi2 = ((ga0, ga1), (gb0, gb1))

    def _feed_back(self, hidden):
        rows, width = self.rows, self.width
        scratch = [((width, hidden // 2), BF), ((hidden // 2, width), BF), ((rows, width), BF),
                   ((width, rows), BF), ((width, rows), BF), ((width, rows), BF)]
        return [((width // 2, hidden // 4), BF)] * 8, scratch

    def enc_feed_back_one(self):
        rows, width, hidden = self.rows, self.width, self.active.shape[1]
        ff, scratch = self._feed_back(hidden)
        (*g_ff, self.total, self.biases1) = call2(
            enc_feed_back_one_body,
            [*ff, ((rows, width), F32), ((1, hidden + width), F32)],
            [self.place, self.g_enc, self.normed_two, self.active, self.slope, self.e_weights],
            scratch=scratch,
            hbm_args=1,
            sems=4 + 4 * hidden // width,
            us=14,
        )
        self.ffa = (g_ff[:4], g_ff[4:])

    def enc_feed_back_two(self):
        rows, width, hidden = self.rows, self.width, self.active.shape[1]
        ff, scratch = self._feed_back(hidden)
        (*g_ff, self.g_middle, self.g_att, go0, go1, self.small, self.biases) = call2(
            enc_feed_back_two_body,
            [*ff, ((rows, width), F32), ((rows, width), BF), ((width, width // 2), BF),
             ((width, width // 2), BF), ((16, width), F32),
             ((1, self.biases1.shape[1] + self.biases2.shape[1]), F32)],
            [self.place, self.g_enc, self.normed_two, self.active, self.slope, self.total, self.biases1,
             self.biases2, self.middle, self.e_par, self.att_t, self.e_out, self.e_weights],
            scratch=[((rows, width), F32), *scratch, ((width, rows), F32), ((width, rows), F32),
                     ((rows, width), BF)],
            hbm_args=1,
            sems=4 + 4 * hidden // width,
            us=19,
        )
        self.ffb = (g_ff[:4], g_ff[4:])
        self.go = (go0, go1)

    def enc_attn_back_one(self):
        rows, width = self.rows, self.width
        (self.g_packed,) = call2(
            partial(enc_attn_back_one_body, self.kept),
            [((rows, 3 * width), BF)],
            [self.place, self.packed, self.g_att, self.lse],
            scratch=[((width, rows), BF)],
            us=12,
        )

    def enc_attn_back_two(self):
        rows, width = self.rows, self.width
        n = 3 * width // 2 - CUT_BACK
        ga0, ga1, gb0, gb1, self.g_stream, _ = call2(
            enc_attn_back_two_body,
            [((width, CUT_BACK + width // 2), BF)] * 2 + [((width, n + 128), BF)] * 2
            + [((rows, width), F32), ((16, width), F32)],
            [self.place, self.g_packed, self.x, self.normed, self.g_middle, self.e_par, self.e_in,
             self.small, *self.go],
            scratch=[((width, rows), F32), ((width, rows), F32), ((width, 128), F32),
                     ((width, 128), F32)],
            us=9,
        )
        self.gi = ((ga0, ga1), (gb0, gb1))

    def spread(self):
        return call(
            partial(spread_body, self.kept),
            [((self.span, self.width2), F32), ((self.span, self.width), F32)],
            [self.spots, self.out, self.g_stream],
            us=LAST,
        )

    def land(self, flights, names=(), more=()):
        names = ["place", *names]
        values, more = land(flights, ([getattr(self, n) for n in names], more))
        for name, value in zip(names, values):
            setattr(self, name, value)
        return more


CUT = 640
CUT_BACK = 512


def whole_weights(params, inproj, outproj, embed=None):
    columns = jnp.pad(params, ((0, 0), (0, 128 - params.shape[1])))
    if embed is None:
        return (jnp.concatenate([inproj, outproj, columns], axis=1),)
    n, m, k = inproj.shape[1] // 2, outproj.shape[1] // 2, embed.shape[1] // 2
    one_a = [inproj[:, :CUT], inproj[:, n : n + CUT]]
    one_b = [inproj[:, CUT:n], columns, inproj[:, n + CUT :], jnp.zeros_like(columns)]
    two = [outproj[:, :m], embed[:, :k], outproj[:, m:], embed[:, k:]]
    return tuple(jnp.concatenate(v, axis=1) for v in (one_a, one_b, two))


def local(
    tokens_in, valid_len, mask_pos,
    encoder_gains, encoder_biases, encoder_inproj, encoder_outproj,
    encoder_up, encoder_upbias, encoder_down, encoder_downbias,
    embed_weight, mask_token,
    decoder_gains, decoder_biases, decoder_inproj, decoder_outproj,
    decoder_up, decoder_upbias, decoder_down, decoder_downbias,
    cotangent,
):
    dp, tr, tc = (lax.axis_index(a) for a in ALL)
    blocks = tuple(lax.axis_size(a) for a in ALL) == (8, 2, 2)
    width, width2 = tokens_in.shape[1], cotangent.shape[1]
    hidden, hidden2 = 2 * encoder_up.shape[1], 2 * decoder_up.shape[1]
    masked = jnp.sum((mask_pos[0] < valid_len[0]).astype(jnp.int32))
    at = (dp, tr, tc, dp) if blocks else (0, 0, 0, 0)
    place = jnp.stack([jnp.int32(v) for v in (*at, tc, valid_len[0] - masked, masked, tr)])

    def feed(up, up_bias, down, down_bias):
        rows, units = 2 * up.shape[0] + 16, up.shape[1]
        args = [up, up_bias[None], down, down_bias[None]]
        (packed,) = call(pack_feed_body, [((rows, units), BF)], args, from_hbm=True)
        return lax.all_gather(packed, ("tr", "tc"), axis=0, tiled=True)

    enc = [encoder_up, encoder_upbias, encoder_down, encoder_downbias]
    dec = [decoder_up, decoder_upbias, decoder_down, decoder_downbias]
    if blocks:
        one, two, three = call(
            pack_body,
            [((48, 3 * width // 2 + 128), BF), ((48, width // 2 + width2 // 2), BF),
             ((16, 4 * width2 + 128), BF)],
            [encoder_gains.T, encoder_biases.T, encoder_inproj, encoder_outproj, embed_weight,
             decoder_gains.T, decoder_biases.T, mask_token[None], decoder_inproj, decoder_outproj],
            from_hbm=True,
        )
        enc = feed(*enc)
        one = Flight(gather_lanes(one, CUT))
        two, three = Flight(gather_all(two, GATHER_C)), Flight(gather_all(three, GATHER_D))
        place, dec = land([one], (place, dec))
        dec = feed(*dec)
        (tokens_in,) = land([one, two, three], (tokens_in,))
        sentence = Sentence(place, tokens_in, mask_pos, cotangent)
        sentence.land([one], ["x"])
        sentence.land([one, two], ["x"])
        sentence.land([one, two, three], ["x"])
        one_a, one_b = one.result
    else:
        def whole(v):
            return lax.all_gather(v, ALL, axis=0, tiled=True)

        e_par = whole(jnp.concatenate([encoder_gains, encoder_biases], axis=1))
        d_par = whole(jnp.concatenate([decoder_gains, decoder_biases, mask_token[:, None]], axis=1))
        one_a, one_b, two = whole_weights(
            e_par, whole(encoder_inproj), whole(encoder_outproj), whole(embed_weight)
        )
        (three,) = whole_weights(d_par, whole(decoder_inproj), whole(decoder_outproj))
        one_a, one_b = cut_gathered(one_a, GATHER_A, True), cut_gathered(one_b, GATHER_B, True)
        two = cut_gathered(two, GATHER_C, True)
        three = cut_gathered(three, GATHER_D, False)
        enc, dec = feed(*enc), feed(*dec)
        sentence = Sentence(place, tokens_in, mask_pos, cotangent)

    def feed_out(rows, units, halves):
        outs = []
        for part, pair in enumerate(halves):
            count = units // len(halves)
            outs = pl.pallas_call(
                partial(out_feed_body, part, len(pair)),
                out_shape=[jax.ShapeDtypeStruct((rows, units), F32), jax.ShapeDtypeStruct((units, rows), F32)],
                in_specs=[pl.BlockSpec(memory_space=pltpu.SMEM)]
                + [pl.BlockSpec(memory_space=pltpu.VMEM)] * len(pair) + [pl.BlockSpec(memory_space=pltpu.HBM)] * len(outs),
                out_specs=[pl.BlockSpec(memory_space=pltpu.HBM)] * 2,
                scratch_shapes=[pltpu.VMEM((rows, count), F32), pltpu.VMEM((rows, count), F32),
                                pltpu.VMEM((count, rows), F32), pltpu.SemaphoreType.DMA((2,))],
                input_output_aliases={len(pair) + 1: 0, len(pair) + 2: 1} if outs else {},
                compiler_params=vmem([((rows, count), F32)] * 3),
                cost_estimate=cost(LAST),
            )(place, *pair, *outs)
        return outs

    def dec_out():
        n, n2 = width // 32, width2 // 32
        return call(
            out_dec_body,
            [((n2, 3 * width2), F32), ((n2, width2), F32), ((2, n2), F32), ((6, n2), F32), ((1, n2), F32),
             ((n, width2), F32)],
            finish(gi2)[0],
            us=LAST,
        )

    def bias_out(biases):
        sizes = [hidden // 2, width // 2, hidden2 // 2, width2 // 2]
        outs = call2(out_bias_body, [((1, n), F32) for n in sizes], [place, biases], us=LAST)
        return [v[0] for v in outs]

    gathers = [two, three] if blocks else []
    sentence.enc_attn(one_a, one_b)
    sentence.land(gathers, ["att_t", "e_par"])
    sentence.land(gathers[:1], ["att_t", "e_par"])
    two = two.result if blocks else two
    sentence.enc_feed(two, enc)
    sentence.land(gathers[1:], ["e_low", "embed"])
    sentence.land(gathers[1:], ["e_low", "embed"])
    three = three.result if blocks else three
    sentence.dec_attn(three)
    sentence.dec_feed(dec)

    if blocks:
        sentence.land([], ["g_middle2", "g_att2", "ff2"])
        ff2 = Flight(reduce_feed(*sentence.ff2, True))
        sentence.land([ff2], ["g_middle2", "g_att2"])
        sentence.dec_attn_back()
        sentence.land([ff2], ["g_enc", "gi2"])
        gi2 = Flight(scatter_lanes(*sentence.gi2))
        sentence.land([gi2], ["g_enc"])
        sentence.enc_feed_back_one()
        sentence.land([ff2, gi2], ["total", "biases1", "ffa"])
        ffa = Flight(reduce_feed(*sentence.ffa, True))
        sentence.land([ffa], ["total", "biases1"])
        sentence.enc_feed_back_two()
        sentence.land([ffa, ff2, gi2], ["g_middle", "g_att", "small", "go", "biases", "ffb"])
        ffb = Flight(reduce_feed(*sentence.ffb, False))
        sentence.land([ffb], ["g_middle", "g_att", "small", "biases"])
        sentence.enc_attn_back_one()
        sentence.land([ffa, ffb, ff2, gi2], ["g_packed"])
        sentence.enc_attn_back_two()
        sentence.land([ffb, ffa, ff2, gi2], ["gi", "g_stream"])
        gi = Flight(scatter_lanes(*sentence.gi, sentence.biases))
        sentence.land([gi], ["g_stream"])
        dec_outs = dec_out()
        sentence.output, sentence.g_tokens = sentence.spread()
        for flight in (ffb, ffa, ff2, ffb):
            land([flight])
        dec_outs, (sentence.output, sentence.g_tokens) = land(
            [gi], (dec_outs, (sentence.output, sentence.g_tokens))
        )
        for flight in (ffa, ffb, ff2, ffa):
            land([flight])
        land([gi])
        outs2 = feed_out(width2 // 2, hidden2 // 2, [finish(ff2)])
        outs2 = land([gi], outs2)
        for flight in (ffb, ffa, ffb):
            land([flight])
        land([gi])
        outs = feed_out(width // 2, hidden // 2, [finish(ffa), finish(ffb)])
        bias_outs = bias_out(finish(gi)[1][0])
    else:
        sentence.dec_attn_back()
        sentence.enc_feed_back_one()
        sentence.enc_feed_back_two()
        sentence.enc_attn_back_one()
        sentence.enc_attn_back_two()

        def halves_of(ups, downs):
            sums = []
            for v in (ups, downs):
                near, far = add(v[0], swap(v[1], "tc")), add(v[2], swap(v[3], "tc"))
                v = lax.psum(add(near, swap(far, "tr")), "dp")
                sums.append(v.reshape(8, -1, v.shape[1]))
            v = jnp.concatenate(sums, axis=1)
            return [v[:4], v[4:]]

        outs2 = feed_out(width2 // 2, hidden2 // 2, [halves_of(*sentence.ff2)])
        halves = [halves_of(*sentence.ffa), halves_of(*sentence.ffb)]
        outs = feed_out(width // 2, hidden // 2, halves)
        bias_outs = bias_out(lax.psum(sentence.biases, ALL))
        sentence.output, sentence.g_tokens = sentence.spread()

    (g_up2, g_down2), (g_up, g_down) = outs2, outs
    b_up, b_down, b_up2, b_down2 = bias_outs
    if blocks:
        n = width // 32
        g_in2, g_out2, g_gains2, g_biases2, g_token, g_embed = dec_outs
        g_in, g_out, g_gains, g_biases = call(
            out_enc_body,
            [((n, 3 * width), F32), ((n, width), F32), ((2, n), F32), ((5, n), F32)],
            finish(gi)[0],
            us=LAST,
        )
        g_gains, g_biases, g_gains2, g_biases2 = g_gains.T, g_biases.T, g_gains2.T, g_biases2.T
        g_token = g_token[0]
    else:
        def scatter(v):
            return lax.psum_scatter(v, ALL, scatter_dimension=0, tiled=True).astype(F32)

        a = join_scattered(sentence.gi[0], SCATTER_A, True)
        b = join_scattered(sentence.gi[1], SCATTER_B, True)
        m = 3 * width // 2 - CUT_BACK
        k = CUT_BACK + width // 2
        g_in = [a[:, :CUT_BACK], b[:, :m], a[:, k : k + CUT_BACK], b[:, m + 128 : 2 * m + 128]]
        g_in = scatter(jnp.concatenate(g_in, axis=1))
        small = scatter(b[:, m : m + 128])
        g_gains, g_biases = small[:, :2], small[:, 2:7]
        g_out = scatter(jnp.concatenate([a[:, CUT_BACK:k], a[:, k + CUT_BACK :]], axis=1))
        g_in2 = scatter(join_scattered(sentence.gi2[0], SCATTER_A, False))
        k = width2 + 128
        v = join_scattered([g[:, :k] for g in sentence.gi2[1]], SCATTER_B, False)
        g_out2, small = scatter(v[:, :width2]), scatter(v[:, width2:])
        g_gains2, g_biases2, g_token = small[:, :2], small[:, 2:8], small[:, 8]
        v = [g[:, k:].reshape(16, -1, 3, width2 // 2).transpose(0, 2, 1, 3) for g in sentence.gi2[1]]
        v = [g.reshape(-1, width2 // 2) for g in v]
        g_embed = scatter(join_scattered(v, SCATTER_B, True))
    return (
        sentence.output, sentence.g_tokens, g_gains, g_biases, g_in, g_out, g_up, b_up, g_down, b_down,
        g_embed, g_token, g_gains2, g_biases2, g_in2, g_out2, g_up2, b_up2, g_down2, b_down2,
    )


def solution(mesh):
    rows = P(ALL, None)
    attention = (rows, rows, rows, rows)
    feed = (P("tc", "tr"), P("tr"), P("tr", "tc"), P("tc"))
    in_specs = (
        (rows, P(ALL), rows) + attention + feed + (rows, P(ALL)) + attention + feed + (rows,)
    )
    out_specs = (rows, rows) + attention + feed + (rows, P(ALL)) + attention + feed
    return jax.shard_map(local, mesh=mesh, in_specs=in_specs, out_specs=out_specs, check_vma=False)
```

```python
import math
from functools import partial

import jax
import jax.numpy as jnp
from jax import lax
from jax.experimental import pallas as pl
from jax.experimental.pallas import tpu as pltpu
from jax.sharding import PartitionSpec as P

HEADS = 12
HEADS2 = 16
ALL = ("dp", "tr", "tc")
EPS = 1e-06
MASKED = -1e30
LOG2E = math.log2(math.e)
F32 = jnp.float32
BF = jnp.bfloat16
SPARE_BYTES = 12 * 1024 * 1024
LAST = 0.01
WHOLE_BYTES = 58 * 1024 * 1024


def dot_nn(a, b):
    return lax.dot_general(a, b, (((1,), (0,)), ((), ())), preferred_element_type=F32)


def dot_nt(a, b):
    return lax.dot_general(a, b, (((1,), (1,)), ((), ())), preferred_element_type=F32)


def cost(us):
    return pl.CostEstimate(flops=int(us * 1e9), bytes_accessed=int(us * 3e6), transcendentals=0)


def vmem(arrays):
    total = sum(math.prod(s) * jnp.dtype(d).itemsize for s, d in arrays)
    return pltpu.CompilerParams(vmem_limit_bytes=SPARE_BYTES + total)


SAVES = []


def save(ref, columns=None):
    for entry in SAVES[-1]:
        if entry["buffer"] is ref:
            source, target = ref, entry["out"]
            if columns is not None:
                source, target = source.at[:, columns], target.at[:, columns]
            pltpu.make_async_copy(source, target, entry["sem"]).start()
            entry["started"] = True


def call(body, outs, args, scratch=(), smem=0, hbm_args=0, sems=0, keep=(), us=2, alone=False, from_hbm=False):
    count = len(args) - smem - hbm_args
    specs = [pl.BlockSpec(memory_space=pltpu.SMEM)] * smem
    specs += [pl.BlockSpec(memory_space=pltpu.VMEM)] * count
    specs += [pl.BlockSpec(memory_space=pltpu.HBM)] * hbm_args
    buffers = [outs[k] for k in keep]
    shapes = [pltpu.VMEM(s, d) for s, d in [*buffers, *scratch]]
    shapes += [pltpu.SemaphoreType.DMA((max(n, 1),)) for n in (len(keep), sems)]

    def kernel(*refs):
        ins, rest = refs[: len(args)], refs[len(args) :]
        results, rest = list(rest[: len(outs)]), rest[len(outs) :]
        own, keep_sems, own_sems = rest[:-2], rest[-2], rest[-1]
        entries = []
        for n, k in enumerate(keep):
            entries.append({"buffer": own[n], "out": results[k], "sem": keep_sems.at[n], "started": False})
            results[k] = own[n]
        SAVES.append(entries)
        body(*ins, *results, *own[len(keep) :], *((own_sems,) if sems else ()))
        SAVES.pop()
        for entry in entries:
            copy = pltpu.make_async_copy(entry["buffer"], entry["out"], entry["sem"])
            if not entry["started"]:
                copy.start()
        for entry in entries:
            pltpu.make_async_copy(entry["buffer"], entry["out"], entry["sem"]).wait()

    args = list(args)
    for k in range(smem if from_hbm else len(args) - hbm_args, len(args)):
        args[k] = pltpu.with_memory_space_constraint(args[k], pltpu.HBM)
    spaces = [pltpu.HBM if k in keep else pltpu.VMEM for k in range(len(outs))]
    return pl.pallas_call(
        kernel,
        out_shape=[
            pltpu.HBM(s, d) if k in keep else jax.ShapeDtypeStruct(s, d) for k, (s, d) in enumerate(outs)
        ],
        in_specs=specs,
        out_specs=[pl.BlockSpec(memory_space=space) for space in spaces],
        scratch_shapes=shapes,
        compiler_params=pltpu.CompilerParams(vmem_limit_bytes=WHOLE_BYTES) if alone else vmem([*buffers, *scratch]),
        cost_estimate=cost(us),
    )(*args)


def norm_parts(v):
    center = v - jnp.mean(v, axis=-1, keepdims=True)
    r = lax.rsqrt(jnp.mean(center * center, axis=-1, keepdims=True) + EPS)
    return center * r, r


def norm_back(u, r, gain, y):
    e = y * gain
    back = r * (e - jnp.mean(e, axis=-1, keepdims=True) - u * jnp.mean(e * u, axis=-1, keepdims=True))
    return back, jnp.sum(y * u, axis=0, keepdims=True), jnp.sum(y, axis=0, keepdims=True)


def split3(v):
    hi = v.astype(BF)
    rest = v - hi.astype(F32)
    mid = rest.astype(BF)
    return hi, mid, (rest - mid.astype(F32)).astype(BF)


def head_masks(head_size):
    lane = lax.broadcasted_iota(jnp.int32, (1, 128), 1) // head_size
    return [(lane == h).astype(F32).astype(BF) for h in range(128 // head_size)]


def stack_heads(rows, masks):
    return jnp.concatenate([rows * m for m in masks], axis=0)


def prep_body(kept, mp_col, mp_row, tokens, cot, x_out, cot_out, place_out):
    rows, span = x_out.shape[0], tokens.shape[0]
    wide = lax.broadcasted_iota(jnp.int32, (mp_col.shape[0], span), 1)
    below = jnp.sum((mp_col[...] < wide).astype(F32), axis=0, keepdims=True)
    here = jnp.sum((mp_col[...] == wide).astype(F32), axis=0, keepdims=True)
    place = jnp.where(here > 0, kept, wide[:1] - below.astype(jnp.int32))
    pick = lax.broadcasted_iota(jnp.int32, (rows, span), 0) == place
    pick_f = pick.astype(F32)
    cot_out[...] = dot_nn(pick_f.astype(BF), cot[...])
    keep = lax.broadcasted_iota(jnp.int32, (rows, span), 0) < kept
    x_out[...] = dot_nn(jnp.where(keep, pick_f, 0.0).astype(BF), tokens[...]).astype(BF)
    tall = lax.broadcasted_iota(jnp.int32, (span, mp_row.shape[1]), 0)
    below_t = jnp.sum((mp_row[...] < tall).astype(F32), axis=1, keepdims=True)
    here_t = jnp.sum((mp_row[...] == tall).astype(F32), axis=1, keepdims=True)
    place_out[...] = jnp.where(here_t > 0, kept, tall[:, :1] - below_t.astype(jnp.int32))


def spread_back(place, rows, limit):
    at = lax.broadcasted_iota(jnp.int32, (place.shape[0], rows), 1)
    return jnp.where(at < limit, (at == place).astype(F32), 0.0).astype(BF)


def key_bias(lens, kept, rows, with_mask_row):
    at = lax.broadcasted_iota(jnp.int32, (rows, 1), 0)
    bias = jnp.where(at < lens[0], 0.0, MASKED)
    if with_mask_row:
        count = jnp.full((rows, 1), lens[1], jnp.int32).astype(F32)
        bias = jnp.where(at == kept, jnp.log(count) * LOG2E, bias)
    return bias


def attention_forward(packed, att_t, lse, bias, head_size):
    width = packed.shape[1] // 3
    rows = packed.shape[0]
    masks = head_masks(head_size)
    scale = head_size**-0.5 * LOG2E

    def group(g, carry):
        at = pl.multiple_of(g * 128, 128)
        q = packed[:, pl.ds(at, 128)]
        k = packed[:, pl.ds(width + at, 128)]
        v_t = packed[:, pl.ds(2 * width + at, 128)].T
        scores = dot_nt(k, stack_heads(q, masks)) * scale + bias
        peak = jnp.max(scores, axis=0, keepdims=True)
        weights = jnp.exp2(scores - peak)
        total = jnp.sum(weights, axis=0, keepdims=True)
        out = dot_nn(v_t, weights.astype(BF)) * (1.0 / total)
        for h in range(len(masks)):
            block = out[h * head_size : (h + 1) * head_size, h * rows : (h + 1) * rows]
            att_t[pl.ds(at + h * head_size, head_size), :] = block.astype(BF)
        lse[pl.ds(g, 1), :] = peak + jnp.log(total) * LOG2E
        return carry

    lax.fori_loop(0, width // 128, group, 0)


def attention_backward(packed, g_att, lse, g_packed, gq_t, bias, head_size):
    width = packed.shape[1] // 3
    rows = packed.shape[0]
    masks = head_masks(head_size)
    scale = head_size**-0.5

    def group(g, carry):
        at = pl.multiple_of(g * 128, 128)
        q = packed[:, pl.ds(at, 128)]
        k = packed[:, pl.ds(width + at, 128)]
        v = packed[:, pl.ds(2 * width + at, 128)]
        q_s = stack_heads(q, masks)
        g_s = stack_heads(g_att[:, pl.ds(at, 128)], masks)
        scores = dot_nt(k, q_s) * (scale * LOG2E) + bias
        probs = jnp.exp2(scores - lse[pl.ds(g, 1), :])
        g_v = dot_nn(probs.astype(BF), g_s)
        g_probs = dot_nt(v, g_s)
        delta = jnp.sum(g_probs * probs, axis=0, keepdims=True)
        g_scores = (probs * (g_probs - delta)).astype(BF)
        g_k = dot_nn(g_scores, q_s) * scale
        out = dot_nn(k.T, g_scores) * scale
        for h in range(len(masks)):
            block = out[h * head_size : (h + 1) * head_size, h * rows : (h + 1) * rows]
            gq_t[pl.ds(at + h * head_size, head_size), :] = block.astype(BF)
        g_packed[:, pl.ds(width + at, 128)] = g_k.astype(BF)
        g_packed[:, pl.ds(2 * width + at, 128)] = g_v.astype(BF)
        return carry

    lax.fori_loop(0, width // 128, group, 0)
    g_packed[:, :width] = gq_t[...].T


def project_in(stream, params, inproj, normed_out, packed_out):
    u, r = norm_parts(stream)
    normed = (u * params[0:1, :] + params[2:3, :]).astype(BF)
    normed_out[...] = normed
    save(normed_out)
    width = stream.shape[1]
    step = 256
    for part in range(3):
        for at in range(0, width, step):
            lo = part * width + at
            value = dot_nn(normed, inproj[:, lo : lo + step])
            if part == 0:
                value = value + params[3:4, at : at + step]
            if part == 2:
                value = value + params[4:5, at : at + step]
            packed_out[:, lo : lo + step] = value.astype(BF)
    save(packed_out)


GATHER_A = (("tr", 1), ("dp", 4), ("dp", 2), ("dp", 1))
GATHER_B = (("tr", 1), ("dp", 4), ("dp", 1), ("dp", 2))
GATHER_C = (("tr", 1), ("dp", 4), ("dp", 2), ("dp", 1))
GATHER_D = (("tr", 1), ("dp", 1), ("dp", 4), ("dp", 2))
SCATTER_A = (("dp", 1), ("tr", 1), ("dp", 2), ("dp", 4))
SCATTER_B = (("tr", 1), ("dp", 1), ("dp", 2), ("dp", 4))
FEED = (("dp", 1), ("dp", 2), ("dp", 4))


def differences(order, bits):
    dp = tr = 0
    for (axis, distance), bit in zip(order, bits):
        if axis == "dp":
            dp = dp + distance * bit
        else:
            tr = tr + bit
    return dp, tr


def gathered_block(order, j, last):
    return differences(order, (j & 1, (j >> 1) & 1, (j >> 2) & 1, last))


def scattered_block(order, m):
    return differences(order, (m >> 3, (m >> 2) & 1, (m >> 1) & 1, m & 1))


def feed_block(m):
    return differences(FEED, (m >> 2, (m >> 1) & 1, m & 1))[0]


def place_rows(place, order, sources, block, put):
    first = place[2] == 0
    for x in range(2):
        own_ref, oth_ref = sources[x], sources[2 + x]
        count = own_ref.shape[0] // block

        def one(j, carry, own_ref=own_ref, oth_ref=oth_ref, x=x):
            dp, tr = gathered_block(order, j, x)
            chip = (place[0] ^ dp) * 2 + (place[1] ^ tr)
            at = pl.multiple_of(j * block, block)
            own = own_ref[pl.ds(at, block), :].astype(F32)
            oth = oth_ref[pl.ds(at, block), :].astype(F32)
            put(chip, jnp.where(first, own, oth), jnp.where(first, oth, own))
            return carry

        lax.fori_loop(0, count, one, 0)


def place_halves(place, order, sources, cuts):
    block = sources[0].shape[0] // 8
    half = block // 2

    def put(chip, low, high):
        at = pl.multiple_of(chip * block, block)
        top = jnp.concatenate([low[:half], high[:half]], axis=0).astype(BF)
        bottom = jnp.concatenate([low[half:], high[half:]], axis=0).astype(BF)
        lo = 0
        for target, first, width, shift in cuts:
            target[pl.ds(at, block), first : first + width] = top[:, lo : lo + width]
            if shift is not None:
                right = first + shift
                target[pl.ds(at, block), right : right + width] = bottom[:, lo : lo + width]
            lo += width

    place_rows(place, order, sources, block, put)


def place_whole(place, order, sources, cuts):
    block = sources[0].shape[0] // 8

    def put(chip, low, high):
        at = pl.multiple_of(chip * 2 * block, 2 * block)
        both = jnp.concatenate([low, high], axis=0).astype(BF)
        lo = 0
        for target, width in cuts:
            target[pl.ds(at, 2 * block), :] = both[:, lo : lo + width]
            lo += width

    place_rows(place, order, sources, block, put)


def param_rows(columns):
    return columns[...].astype(F32).T[:16]


def reorder_rows(place, order, source, target):
    block = source.shape[0] // 32
    for core in range(2):
        for m in range(16):
            dp, tr = scattered_block(order, m)
            device = ((place[0] ^ dp) * 2 + (place[1] ^ tr)) * 2 + (place[2] ^ core)
            at = pl.multiple_of(device * block, 8)
            to = (core * 16 + m) * block
            target[to : to + block, :] = source[pl.ds(at, block), :]


def write_halves(ordered, columns, outs, first=0, count=None):
    half_rows = ordered.shape[0] // 2
    block = half_rows // 16
    width = columns.shape[1] // 2
    count = width if count is None else count
    step = max(n for n in (384, 320, 256) if count % n == 0) if count != 640 else 640
    for core in range(2):
        rows = ordered[core * half_rows : (core + 1) * half_rows, :].astype(BF)
        for at in range(first, first + count, step):
            left = dot_nn(rows, columns[:, at : at + step])
            right = dot_nn(rows, columns[:, width + at : width + at + step])
            for m in range(16):
                both = [left[m * block : (m + 1) * block], right[m * block : (m + 1) * block]]
                outs[core][m * 2 * block : (m + 1) * 2 * block, at - first : at - first + step] = (
                    jnp.concatenate(both, axis=0).astype(BF)
                )


def write_whole(ordered, columns, outs, lo):
    half_rows = ordered.shape[0] // 2
    width = columns.shape[1]
    for core in range(2):
        rows = ordered[core * half_rows : (core + 1) * half_rows, :].astype(BF)
        for at in range(0, width, 256):
            outs[core][:, lo + at : lo + at + 256] = dot_nn(rows, columns[:, at : at + 256]).astype(BF)


def small_columns(small):
    table = jnp.concatenate([small[...], jnp.zeros((112, small.shape[1]), F32)], axis=0)
    return table.T


def pack_body(
    e_gains, e_biases, e_in, e_out, embed, d_gains, d_biases, token, d_in, d_out, one, two, three
):
    def columns(parts):
        total, lo = 0.0, 0
        for part in parts:
            count, rows = part.shape
            spot = lax.broadcasted_iota(jnp.int32, (count, 128), 1)
            want = lax.broadcasted_iota(jnp.int32, (count, 128), 0) + lo
            table = (spot == want).astype(F32).astype(BF)
            total = total + lax.dot_general(
                part[...], table, (((0,), (0,)), ((), ())), preferred_element_type=F32
            )
            lo += count
        return total

    e_par = columns([e_gains, e_biases])

    def halves(v):
        v = v[...].astype(F32)
        width = v.shape[1] // 2
        return jnp.concatenate([v[:, :width], v[:, width:]], axis=0).astype(BF)

    n = e_in.shape[1] // 2
    one[:, :n] = halves(e_in)
    one[:, n:] = jnp.concatenate([e_par, jnp.zeros_like(e_par)], axis=0).astype(BF)
    n = e_out.shape[1] // 2
    two[:, :n] = halves(e_out)
    two[:, n:] = halves(embed)
    n = d_in.shape[1]
    m = n + d_out.shape[1]
    three[:, :n] = d_in[...]
    three[:, n:m] = d_out[...]
    three[:, m:] = columns([d_gains, d_biases, token]).astype(BF)


def enc_attn_body(
    kept, place, x, s0, s1, s2, s3, r0, r1, r2, r3,
    normed, packed, att_t, lse, inproj, par_t, par_c,
):
    width = x.shape[1]
    n, shift = s0.shape[1], 3 * width // 2
    place_halves(place, GATHER_A, (s0, s1, s2, s3), ((inproj, 0, n, shift),))
    place_halves(
        place, GATHER_B, (r0, r1, r2, r3), ((inproj, n, shift - n, shift), (par_c, 0, 128, None))
    )
    save(inproj)
    par_t[...] = param_rows(par_c)
    project_in(x[...].astype(F32), par_t, inproj, normed, packed)
    bias = key_bias((place[5], place[6]), kept, x.shape[0], False)
    attention_forward(packed, att_t, lse, bias, width // HEADS)


def dec_attn_body(
    kept, place, e_low, embed, s0, s1, s2, s3,
    stream, normed, packed, att_t, lse, inproj, outproj, params, par_c,
):
    rows = e_low.shape[0]
    width = stream.shape[1]
    place_whole(
        place, GATHER_D, (s0, s1, s2, s3), ((inproj, 3 * width), (outproj, width), (par_c, 128))
    )
    save(inproj)
    save(outproj)
    params[...] = param_rows(par_c)
    embedded = dot_nn(e_low[...], embed[...]) + params[7:8, :]
    at = lax.broadcasted_iota(jnp.int32, (rows, 1), 0)
    decoded = jnp.where(at < kept, embedded, params[8:9, :])
    stream[...] = decoded
    save(stream)
    project_in(decoded, params, inproj, normed, packed)
    bias = key_bias((place[5], place[6]), kept, rows, True)
    attention_forward(packed, att_t, lse, bias, width // HEADS2)


def pack_feed_body(up, up_bias, down, down_bias, out):
    rows, width = up.shape[0], down.shape[1]
    out[:rows, :] = up[...]
    for at in range(0, up.shape[1], width):
        out[rows : 2 * rows, at : at + width] = down[at : at + width, :]
    row = lax.broadcasted_iota(jnp.int32, (16, up.shape[1]), 0)
    value = jnp.where(row == 0, up_bias[...].astype(F32), 0.0)
    out[2 * rows :, :] = value.astype(BF)
    row = lax.broadcasted_iota(jnp.int32, (16, width), 0)
    value = jnp.where(row == 1, down_bias[...].astype(F32), value[:, :width])
    out[2 * rows :, :width] = value.astype(BF)


def load_feed(place, gathered, up, down, sems, part=0, biases=None):
    copies = []
    groups = []
    half = up.shape[0] // 2
    units = up.shape[1] // 2
    block = gathered.shape[0] // 4

    def start(source, target):
        copies.append(pltpu.make_async_copy(source, target, sems.at[len(copies)]))
        copies[-1].start()

    for tr in range(2):
        for core in range(2):
            base = ((place[7] ^ tr) * 2 + core) * block

            def rows(at, count, base=base):
                return pl.ds(pl.multiple_of(base + at, 16), count)

            columns = pl.ds(tr * units, units)
            start(
                gathered.at[rows(0, half), pl.ds(part * units, units)],
                up.at[pl.ds(core * half, half), columns],
            )
            for at in range(0, units, half):
                start(
                    gathered.at[rows(half, half), pl.ds(part * units + at, half)],
                    down.at[pl.ds(tr * units + at, half), pl.ds(core * half, half)],
                )
            if biases is not None:
                start(gathered.at[rows(2 * half, 16), :], biases.at[2 * tr + core])
        groups.append(copies[sum(len(g) for g in groups) :])
    return groups


def wait(copies):
    for copy in copies:
        copy.wait()


def bias_rows(biases, half):
    return jnp.concatenate([biases[0, 1:2, :half], biases[1, 1:2, :half]], axis=1).astype(F32)


def middle_of(stream, att_t, outproj, params):
    return stream + dot_nn(att_t[...].T, outproj[...]) + params[5:6, :]


def feed_forward(
    normed_two, up, up_bias, down, active_out, slope_out, total, step, copies, biases
):
    units = up.shape[1] // 2
    total[...] = jnp.zeros_like(total)

    def chunk(c, carry):
        at = pl.multiple_of(c * step, step)
        hidden = dot_nn(normed_two, up[:, pl.ds(at, step)]) + up_bias[:, pl.ds(at, step)]
        phi = 0.5 * (1.0 + lax.erf(hidden * math.sqrt(0.5)))
        bell = jnp.exp2(hidden * hidden * (-0.5 * LOG2E)) * (1.0 / math.sqrt(2 * math.pi))
        active = (hidden * phi).astype(BF)
        active_out[:, pl.ds(at, step)] = active
        slope_out[:, pl.ds(at, step)] = (phi + hidden * bell).astype(BF)
        save(active_out, pl.ds(at, step))
        save(slope_out, pl.ds(at, step))
        total[...] += dot_nn(active, down[pl.ds(at, step), :])
        return carry

    for tr in range(2):
        wait(copies[tr])
        up_bias[:, tr * units : (tr + 1) * units] = biases[2 * tr, 0:1, :].astype(F32)
        lax.fori_loop(tr * units // step, (tr + 1) * units // step, chunk, 0)


def order_feed(place, source, target):
    block = source.shape[0] // 16
    for core in range(2):
        for m in range(8):
            at = ((place[4] ^ core) * 8 + (place[3] ^ feed_block(m))) * block
            to = (core * 8 + m) * block
            target[to : to + block, :] = source[pl.ds(pl.multiple_of(at, block), block), :]


def feed_backward(
    copies, place, part, parts, g_result, normed_two, active, slope, up, down,
    g_ups, g_downs, g_upbias, g_normed, step, rows_t, ordered_n, ordered_g,
):
    width = normed_two.shape[1]
    count = up.shape[1] // 2
    units = count * parts
    half = width // 2
    rows_t[...] = normed_two[...].T
    order_feed(place, rows_t, ordered_n)
    rows_t[...] = g_result[...].T
    order_feed(place, rows_t, ordered_g)
    for tr in range(2):
        wait(copies[tr])
        base = tr * units + part * count
        out_base = pl.multiple_of((place[7] ^ tr) * units + part * count, 128)

        def chunk(c, carry, tr=tr, base=base, out_base=out_base):
            at = pl.multiple_of(c * step, step)
            here = pl.ds(pl.multiple_of(tr * count + at, 128), step)
            g_active = dot_nt(g_result[...], down[here, :]).astype(BF).astype(F32)
            there = pl.ds(pl.multiple_of(base + at, 128), step)
            g_hidden = (slope[:, there].astype(F32) * g_active).astype(BF)
            g_upbias[:, pl.ds(pl.multiple_of(out_base + at, 128), step)] = jnp.sum(
                g_hidden.astype(F32), axis=0, keepdims=True
            )
            g_normed[...] += dot_nt(g_hidden, up[:, here])
            g_up = dot_nn(ordered_n[...], g_hidden).astype(BF)
            g_down = dot_nn(ordered_g[...], active[:, there]).astype(BF)
            for core in range(2):
                g_ups[2 * tr + core][:, pl.ds(at, step)] = g_up[core * half : (core + 1) * half]
                g_downs[2 * tr + core][:, pl.ds(at, step)] = g_down[core * half : (core + 1) * half]
            return carry

        lax.fori_loop(0, count // step, chunk, 0)


def after_feed_backward(
    place, order, g_out, g_normed, middle, params, att_t, outproj, g_middle, g_att, small, att_f, att_o
):
    u, r = norm_parts(middle)
    y = g_normed.astype(BF).astype(F32)
    back, g_gain, g_shift = norm_back(u, r, params[1:2, :], y)
    grad = g_out + back
    g_middle[...] = grad
    branch = grad.astype(BF)
    att_f[...] = att_t[...].astype(F32)
    reorder_rows(place, order, att_f, att_o)
    g_att[...] = dot_nt(branch, outproj[...]).astype(BF)
    small[1:2, :] = g_gain
    small[5:6, :] = jnp.sum(branch.astype(F32), axis=0, keepdims=True)
    small[6:7, :] = g_shift
    return branch


def enc_feed_body(
    place, x, att_t, s0, s1, s2, s3, params, weights,
    middle, normed_two, active, slope, e_low, outproj, embed,
    up, down, total, biases, up_bias, sems,
):
    copies = load_feed(place, weights, up, down, sems, 0, biases)
    width = x.shape[1]
    n, m = width // 2, embed.shape[1] // 2
    place_halves(place, GATHER_C, (s0, s1, s2, s3), ((outproj, 0, n, n), (embed, 0, m, m)))
    mid = middle_of(x[...].astype(F32), att_t, outproj, params)
    middle[...] = mid
    u, r = norm_parts(mid)
    n2 = (u * params[1:2, :] + params[6:7, :]).astype(BF)
    normed_two[...] = n2
    for ref in (middle, normed_two, outproj, embed):
        save(ref)
    feed_forward(n2, up, up_bias, down, active, slope, total, 512, copies, biases)
    down_bias = bias_rows(biases, width // 2)
    result = (total[...] + down_bias).astype(BF)
    e_low[...] = (middle[...] + result.astype(F32)).astype(BF)


def dec_feed_body(
    kept, place, stream, att_t, outproj, params, cot, weights,
    out, gu0, gu1, gu2, gu3, gd0, gd1, gd2, gd3, g_middle, g_att, go0, go1, small, g_biases,
    up, down, active, slope, total, n2_s, g_res, rows_t, ordered_n, ordered_g,
    att_f, att_o, branch_s, biases, up_bias, sems,
):
    copies = load_feed(place, weights, up, down, sems, 0, biases)
    mid = middle_of(stream[...], att_t, outproj, params)
    u, r = norm_parts(mid)
    n2 = (u * params[1:2, :] + params[6:7, :]).astype(BF)
    n2_s[...] = n2
    feed_forward(n2, up, up_bias, down, active, slope, total, 512, copies, biases)
    down_bias = bias_rows(biases, up.shape[0] // 2)
    result = (total[...] + down_bias).astype(BF)
    out[...] = mid + result.astype(F32)
    save(out)
    g_out = cot[...]
    g_res[...] = g_out.astype(BF)
    small[...] = jnp.zeros_like(small)
    units = up.shape[1]
    g_biases[:, units:] = jnp.sum(g_res[...].astype(F32), axis=0, keepdims=True)
    total[...] = jnp.zeros_like(total)
    feed_backward(
        ((), ()), place, 0, 1, g_res, n2_s, active, slope, up, down, (gu0, gu1, gu2, gu3), (gd0, gd1, gd2, gd3),
        g_biases, total, 512, rows_t, ordered_n, ordered_g,
    )
    branch = after_feed_backward(
        place, SCATTER_B, g_out, total[...], mid, params, att_t, outproj, g_middle, g_att, small,
        att_f, att_o,
    )
    branch_s[...] = branch
    write_whole(att_o, branch_s, (go0, go1), 0)


def enc_feed_back_one_body(
    place, g_enc, normed_two, active, slope, weights,
    gu0, gu1, gu2, gu3, gd0, gd1, gd2, gd3, total, biases, up, down, g_res, rows_t, ordered_n, ordered_g, sems,
):
    copies = load_feed(place, weights, up, down, sems)
    g_res[...] = g_enc[...].astype(BF)
    total[...] = jnp.zeros_like(total)
    biases[:, 2 * up.shape[1] :] = jnp.sum(g_res[...].astype(F32), axis=0, keepdims=True)
    feed_backward(
        copies, place, 0, 2, g_res, normed_two, active, slope, up, down, (gu0, gu1, gu2, gu3),
        (gd0, gd1, gd2, gd3), biases, total, 384, rows_t, ordered_n, ordered_g,
    )


def enc_feed_back_two_body(
    place, g_enc, normed_two, active, slope, total_in, biases_in, biases_dec, middle, params, att_t,
    outproj, weights,
    gu0, gu1, gu2, gu3, gd0, gd1, gd2, gd3, g_middle, g_att, go0, go1, small, biases,
    total, up, down, g_res, rows_t, ordered_n, ordered_g, att_f, att_o, branch_s, sems,
):
    copies = load_feed(place, weights, up, down, sems, 1)
    g_res[...] = g_enc[...].astype(BF)
    total[...] = total_in[...]
    count = biases_in.shape[1]
    biases[:, :count] = biases_in[...]
    biases[:, count:] = biases_dec[...]
    small[...] = jnp.zeros_like(small)
    feed_backward(
        copies, place, 1, 2, g_res, normed_two, active, slope, up, down, (gu0, gu1, gu2, gu3),
        (gd0, gd1, gd2, gd3), biases, total, 384, rows_t, ordered_n, ordered_g,
    )
    branch = after_feed_backward(
        place, SCATTER_A, g_enc[...], total[...], middle[...], params, att_t, outproj, g_middle,
        g_att, small, att_f, att_o,
    )
    branch_s[...] = branch
    write_halves(att_o, branch_s, (go0, go1))


def project_back(
    place, order, stream, normed, g_packed, g_middle, params, inproj, small, first, rows_f, rows_o
):
    width = stream.shape[1]
    rows_f[...] = normed[...].astype(F32).T
    reorder_rows(place, order, rows_f, rows_o)
    g_normed = dot_nt(g_packed[...], inproj[...])
    u, r = norm_parts(stream)
    back, g_gain, g_shift = norm_back(u, r, params[0:1, :], g_normed)
    small[...] = first[...]
    small[0:1, :] = g_gain
    small[2:3, :] = g_shift
    small[3:4, :] = jnp.sum(g_packed[:, :width].astype(F32), axis=0, keepdims=True)
    small[4:5, :] = jnp.sum(g_packed[:, 2 * width :].astype(F32), axis=0, keepdims=True)
    return g_middle[...] + back


def dec_attn_back_body(
    kept, place, packed, g_att, lse, stream, normed, g_middle, params, inproj, embed, e_low, first,
    go0, go1, ga0, ga1, gb0, gb1, g_enc, small, g_packed, gq_t, rows_f, rows_o, cols, cols_o,
    emb_f, emb_o, g_emb,
):
    rows = stream.shape[0]
    width = stream.shape[1]
    bias = key_bias((place[5], place[6]), kept, rows, True)
    attention_backward(packed, g_att, lse, g_packed, gq_t, bias, width // HEADS2)
    g_stream = project_back(
        place, SCATTER_A, stream[...], normed, g_packed, g_middle, params, inproj, small, first,
        rows_f, rows_o,
    )
    write_whole(rows_o, g_packed, (ga0, ga1), 0)
    at = lax.broadcasted_iota(jnp.int32, (rows, 1), 0)
    small[8:9, :] = jnp.sum(jnp.where(at == kept, g_stream, 0.0), axis=0, keepdims=True)
    g_embedded = jnp.where(at < kept, g_stream, 0.0).astype(BF)
    small[7:8, :] = jnp.sum(g_embedded.astype(F32), axis=0, keepdims=True)
    g_emb[...] = g_embedded
    g_enc[...] = dot_nt(g_embedded, embed[...])
    emb_f[...] = e_low[...].astype(F32).T
    reorder_rows(place, SCATTER_B, emb_f, emb_o)
    cols[...] = small_columns(small)
    reorder_rows(place, SCATTER_B, cols, cols_o)
    n = cols_o.shape[0] // 2
    half = emb_o.shape[0] // 2
    block, part = half // 16, g_emb.shape[1] // 2
    unit = n // 16
    for core, (gb, go) in enumerate(((gb0, go0), (gb1, go1))):
        gb[:, :width] = go[...]
        gb[:, width : width + 128] = cols_o[core * n : (core + 1) * n, :].astype(BF)
        rows_e = emb_o[core * half : (core + 1) * half, :].astype(BF)
        left, right = dot_nn(rows_e, g_emb[:, :part]), dot_nn(rows_e, g_emb[:, part:])
        for m in range(16):
            both = [left[m * block : (m + 1) * block], right[m * block : (m + 1) * block]]
            both = jnp.concatenate(both, axis=0).astype(BF)
            for k in range(2 * block // unit):
                lo = width + 128 + k * part
                gb[m * unit : (m + 1) * unit, lo : lo + part] = both[k * unit : (k + 1) * unit]


def enc_attn_back_one_body(kept, place, packed, g_att, lse, g_packed, gq_t):
    bias = key_bias((place[5], place[6]), kept, packed.shape[0], False)
    attention_backward(packed, g_att, lse, g_packed, gq_t, bias, g_att.shape[1] // HEADS)


def enc_attn_back_two_body(
    place, g_packed, x, normed, g_middle, params, inproj, first, go0, go1,
    ga0, ga1, gb0, gb1, g_stream, small, rows_f, rows_o, cols, cols_o,
):
    width = x.shape[1]
    g_stream[...] = project_back(
        place, SCATTER_A, x[...].astype(F32), normed, g_packed, g_middle, params, inproj, small, first,
        rows_f, rows_o,
    )
    m = gb0.shape[1] - 128
    n = 3 * width // 2 - m
    write_halves(rows_o, g_packed, (ga0, ga1), 0, n)
    reorder_rows(place, SCATTER_B, rows_f, rows_o)
    write_halves(rows_o, g_packed, (gb0, gb1), n, m)
    cols[...] = small_columns(small)
    reorder_rows(place, SCATTER_B, cols, cols_o)
    count = cols_o.shape[0] // 2
    block = count // 16
    for core, (a, b, go) in enumerate(((ga0, gb0, go0), (ga1, gb1, go1))):
        a[:, n:] = go[...]
        for k in range(16):
            part = cols_o[core * count + k * block : core * count + (k + 1) * block, :]
            both = jnp.concatenate([part, jnp.zeros_like(part)], axis=0).astype(BF)
            b[k * 2 * block : (k + 1) * 2 * block, m:] = both


def spread_body(kept, spots, out, g_stream, output, g_tokens):
    rows = out.shape[0]
    for limit, source, target in ((kept + 1, out, output), (kept, g_stream, g_tokens)):
        pick = spread_back(spots[...], rows, limit)
        hi, mid, low = split3(source[...])
        target[...] = dot_nn(pick, hi) + dot_nn(pick, mid) + dot_nn(pick, low)


def out_feed_body(counts, *refs):
    place = refs[0]
    g_up, g_down, up, turned, down, sems = refs[-6:]
    units = up.shape[2]
    copies, first = [], 1
    for part, count in enumerate(counts):
        for k, ref in enumerate(refs[first : first + count]):
            block = ref.shape[1] // 2
            for m in range(ref.shape[0]):
                dp = place[3] ^ feed_block(ref.shape[0] * k + m)
                at = pl.multiple_of(dp * block, block)
                rows = ref[m].astype(F32)
                up[part, pl.ds(at, block), :] = rows[:block]
                turned[pl.ds(at, block), :] = rows[block:]
        first += count
        here = pl.ds(part * units, units)
        copies.append(pltpu.make_async_copy(up.at[part], g_up.at[:, here], sems.at[2 * part]))
        copies[-1].start()
        down[part] = turned[...].T
        copies.append(pltpu.make_async_copy(down.at[part], g_down.at[here, :], sems.at[2 * part + 1]))
        copies[-1].start()
    for copy in copies:
        copy.wait()


def out_dec_body(mine, theirs, g_in, g_out, g_gains, g_biases, g_token, g_embed):
    total = mine[...].astype(F32) + theirs[...].astype(F32)
    n = g_in.shape[1]
    m = n + g_out.shape[1]
    g_in[...] = total[:, :n]
    g_out[...] = total[:, n:m]
    rows = total[:, m : m + 128].T
    g_gains[...] = rows[0:2]
    g_biases[...] = rows[2:8]
    g_token[...] = rows[8:9]
    half = g_embed.shape[1] // 2
    units = [total[:, m + 128 + k * half : m + 128 + (k + 1) * half] for k in range(3)]
    both = jnp.concatenate(units, axis=0)
    count = both.shape[0] // 2
    g_embed[:, :half] = both[:count]
    g_embed[:, half:] = both[count:]


def out_enc_body(mine, theirs, g_in, g_out, g_gains, g_biases):
    total = mine[...].astype(F32) + theirs[...].astype(F32)
    n, width, half = g_in.shape[0], g_in.shape[1] // 2, g_out.shape[1] // 2
    first = CUT_BACK
    a, b = total[:, : first + half], total[:, first + half :]
    rest = width - first
    g_in[:, :first] = a[:n, :first]
    g_in[:, first:width] = b[:n, :rest]
    g_in[:, width : width + first] = a[n:, :first]
    g_in[:, width + first :] = b[n:, :rest]
    g_out[:, :half] = a[:n, first:]
    g_out[:, half:] = a[n:, first:]
    rows = b[:n, rest:].T
    g_gains[...] = rows[0:2]
    g_biases[...] = rows[2:7]


def out_bias_body(place, biases, up1, down1, up2, down2):
    lo = 0
    for out, at in ((up1, place[7]), (down1, place[4]), (up2, place[7]), (down2, place[4])):
        n = out.shape[1]
        out[...] = biases[:, pl.ds(pl.multiple_of(lo + at * n, 128), n)]
        lo += 2 * n


def swap(v, axis, distance=1):
    return lax.ppermute(v, axis, [(i, i ^ distance) for i in range(lax.axis_size(axis))])


def add(a, b):
    return (a.astype(F32) + b.astype(F32)).astype(BF)


class Flight:
    def __init__(self, steps):
        self.steps, self.result = steps, None
        self.waits = next(steps)

    def land(self, arrays):
        try:
            self.waits = self.steps.send(arrays)
        except StopIteration as end:
            self.waits, self.result = None, end.value


def land(flights, outs=()):
    flights = [f for f in flights if f.waits is not None]
    outs, arrays = lax.optimization_barrier((outs, [f.waits for f in flights]))
    for flight, landed in zip(flights, arrays):
        flight.land(landed)
    return outs


def finish(flight):
    while flight.waits is not None:
        flight.land(flight.waits)
    return flight.result


def gather_all(v, order):
    for axis, distance in order[:-1]:
        (got,) = yield (swap(v, axis, distance),)
        v = jnp.concatenate([v, got], axis=0)
    (last,) = yield (swap(v, *order[-1]),)
    a, b = yield (swap(v, "tc"), swap(last, "tc"))
    return v, last, a, b


def gather_lanes(v, cut):
    for axis, distance in GATHER_A[:2]:
        (got,) = yield (swap(v, axis, distance),)
        v = jnp.concatenate([v, got], axis=0)
    a, b = v[:, :cut], v[:, cut:]
    one, two = yield (swap(a, *GATHER_A[2]), swap(b, *GATHER_B[2]))
    a, b = jnp.concatenate([a, one], axis=0), jnp.concatenate([b, two], axis=0)
    one, two = yield (swap(a, *GATHER_A[3]), swap(b, *GATHER_B[3]))
    got = yield (swap(a, "tc"), swap(one, "tc"), swap(b, "tc"), swap(two, "tc"))
    return (a, one, *got[:2]), (b, two, *got[2:])


def scatter_lanes(one, two, small=None):
    extra = [] if small is None else [small]
    a, b, *got = yield (swap(one[1], "tc"), swap(two[1], "tc"), *(swap(v, "tc") for v in extra))
    a, b = add(one[0], a), add(two[0], b)
    for k in range(2):
        extra = [v + w for v, w in zip(extra, got)]
        half = a.shape[0] // 2
        one, two, *got = yield (
            swap(a[half:], *SCATTER_A[k]), swap(b[half:], *SCATTER_B[k]), *(swap(v, *SCATTER_A[k]) for v in extra)
        )
        a, b = add(a[:half], one), add(b[:half], two)
    v = jnp.concatenate([a, b], axis=1)
    for k in (2, 3):
        extra = [v + w for v, w in zip(extra, got)]
        half = v.shape[0] // 2
        one, *got = yield (swap(v[half:], *SCATTER_A[k]), *(swap(w, *SCATTER_A[k]) for w in extra))
        v = (v[:half], one) if k == 3 else add(v[:half], one)
    return v, [v + w for v, w in zip(extra, got)]


def reduce_feed(ups, downs, x_last):
    got = yield tuple(swap(v, "tc") for v in (ups[1], ups[3], downs[1], downs[3]))
    up, up_far, down, down_far = (
        add(v, w) for v, w in zip((ups[0], ups[2], downs[0], downs[2]), got)
    )
    half = up.shape[0] // 2
    one, two, three = yield (
        swap(up_far, "tr"), swap(down[half:], "dp", 1), swap(down_far[half:], "dp", 1)
    )
    up, down, down_far = add(up, one), add(down[:half], two), add(down_far[:half], three)
    one, two = yield (swap(up[half:], "dp", 1), swap(down_far, "tr"))
    up, down = add(up[:half], one), add(down, two)
    shape = (4, half // 4, up.shape[1])
    v = jnp.concatenate([up.reshape(shape), down.reshape(shape)], axis=1)
    for distance in (2, 4):
        half = v.shape[0] // 2
        (got,) = yield (swap(v[half:], "dp", distance),)
        v = add(v[:half], got)
    (got,) = yield (swap(v, "dp", 4),)
    v = jnp.concatenate([v, got], axis=0)
    if x_last:
        (got,) = yield (swap(v, "dp", 2),)
        v = jnp.concatenate([v, got], axis=0)
        (got,) = yield (swap(v, "dp", 1),)
        return v, got
    (w,) = yield (swap(v, "dp", 1),)
    one, two = yield (swap(v, "dp", 2), swap(w, "dp", 2))
    return v, one, w, two


def chip_axes(order):
    return [{("dp", 4): 0, ("dp", 2): 1, ("dp", 1): 2, ("tr", 1): 3}[step] for step in order]


def cut_gathered(whole, order, halves):
    rows, width = whole.shape
    if halves:
        v = whole.reshape(32, rows // 32, 2, width // 2).transpose(0, 2, 1, 3)
        v = v.reshape(32, rows // 16, width // 2)
    else:
        v = whole.reshape(32, rows // 32, width)
    v = v.reshape((2, 2, 2, 2, 2) + v.shape[1:])
    first = chip_axes(order)
    v = v.transpose(first[3], 4, first[2], first[1], first[0], 5, 6)
    v = v.reshape(2, 2, -1, v.shape[-1])
    return v[0, 0], v[1, 0], v[0, 1], v[1, 1]


def join_scattered(pair, order, halves):
    v = jnp.stack(pair)
    v = v.reshape(2, 2, 2, 2, 2, v.shape[1] // 16, v.shape[2])
    first = chip_axes(order)
    v = v.transpose(*(1 + first.index(k) for k in range(4)), 0, 5, 6)
    v = v.reshape(32, v.shape[5], v.shape[6])
    if halves:
        v = v.reshape(32, 2, v.shape[1] // 2, v.shape[2]).transpose(0, 2, 1, 3)
        v = v.reshape(32, v.shape[1], -1)
    return v.reshape(-1, v.shape[-1])


def call2(body, outs, args, **more):
    return call(body, outs, args, smem=1, **more)


class Sentence:
    def __init__(self, place, tokens, mask_pos, cot):
        self.place = place
        span, self.width = tokens.shape
        masks = mask_pos.shape[1]
        self.span, self.kept = span, span - masks
        self.rows = -(-(self.kept + 1) // 16) * 16
        self.width2 = cot.shape[1]
        self.x, self.cot, self.spots = call(
            partial(prep_body, self.kept),
            [((self.rows, self.width), BF), ((self.rows, self.width2), F32), ((span, 1), jnp.int32)],
            [mask_pos.reshape(masks, 1), mask_pos, tokens, cot],
            us=3,
        )

    def enc_attn(self, one_a, one_b):
        rows, width = self.rows, self.width
        self.normed, self.packed, self.att_t, self.lse, self.e_in, self.e_par = call2(
            partial(enc_attn_body, self.kept),
            [((rows, width), BF), ((rows, 3 * width), BF), ((width, rows), BF),
             ((width // 128, rows * (128 * HEADS // width)), F32), ((width, 3 * width), BF),
             ((16, width), F32)],
            [self.place, self.x, *one_a, *one_b],
            scratch=[((width, 128), BF)],
            keep=(0, 1, 2, 3, 4, 5),
            us=12,
        )

    def enc_feed(self, two, weights):
        rows, width, units = self.rows, self.width, weights.shape[1]
        hidden = 2 * units
        self.e_weights = weights
        self.middle, self.normed_two, self.active, self.slope, self.e_low, self.e_out, self.embed = call2(
            enc_feed_body,
            [((rows, width), F32), ((rows, width), BF), ((rows, hidden), BF), ((rows, hidden), BF),
             ((rows, width), BF), ((width, width), BF), ((width, self.width2), BF)],
            [self.place, self.x, self.att_t, *two, self.e_par, weights],
            scratch=[((width, hidden), BF), ((hidden, width), BF), ((rows, width), F32),
                     ((4, 16, units), BF), ((1, hidden), F32)],
            hbm_args=1,
            sems=8 + 8 * units // width,
            keep=(0, 1, 2, 3, 4, 5, 6),
            from_hbm=True,
            us=15,
        )

    def dec_attn(self, three):
        rows, width = self.rows, self.width2
        (self.stream2, self.normed2, self.packed2, self.att2_t, self.lse2, self.d_in, self.d_out,
         self.d_par) = call2(
            partial(dec_attn_body, self.kept),
            [((rows, width), F32), ((rows, width), BF), ((rows, 3 * width), BF), ((width, rows), BF),
             ((width // 128, rows * (128 * HEADS2 // width)), F32), ((width, 3 * width), BF),
             ((width, width), BF), ((16, width), F32)],
            [self.place, self.e_low, self.embed, *three],
            scratch=[((width, 128), BF)],
            keep=(0, 1, 2, 3, 4, 5, 6, 7),
            from_hbm=True,
            us=11,
        )

    def dec_feed(self, weights):
        rows, width, units = self.rows, self.width2, weights.shape[1]
        hidden = 2 * units
        (self.out, *g_ff, self.g_middle2, self.g_att2, self.go20, self.go21, self.small2,
         self.biases2) = call2(
            partial(dec_feed_body, self.kept),
            [((rows, width), F32), *[((width // 2, hidden // 2), BF)] * 8, ((rows, width), F32),
             ((rows, width), BF), ((width // 2, width), BF), ((width // 2, width), BF),
             ((16, width), F32), ((1, hidden + width), F32)],
            [self.place, self.stream2, self.att2_t, self.d_out, self.d_par, self.cot, weights],
            scratch=[((width, hidden), BF), ((hidden, width), BF), ((rows, hidden), BF),
                     ((rows, hidden), BF), ((rows, width), F32), ((rows, width), BF),
                     ((rows, width), BF), ((width, rows), BF), ((width, rows), BF),
                     ((width, rows), BF), ((width, rows), F32), ((width, rows), F32),
                     ((rows, width), BF), ((4, 16, units), BF), ((1, hidden), F32)],
            hbm_args=1,
            sems=8 + 8 * units // width,
            keep=(0,),
            from_hbm=True,
            us=16,
        )
        self.ff2 = (g_ff[:4], g_ff[4:])

    def dec_attn_back(self):
        rows, width = self.rows, self.width2
        ga0, ga1, gb0, gb1, self.g_enc, _ = call2(
            partial(dec_attn_back_body, self.kept),
            [((width // 2, 3 * width), BF)] * 2 + [((width // 2, width + 128 + 3 * width // 2), BF)] * 2
            + [((rows, self.width), F32), ((16, width), F32)],
            [self.place, self.packed2, self.g_att2, self.lse2, self.stream2, self.normed2,
             self.g_middle2, self.d_par, self.d_in, self.embed, self.e_low, self.small2, self.go20,
             self.go21],
            scratch=[((rows, 3 * width), BF), ((width, rows), BF), ((width, rows), F32),
                     ((width, rows), F32), ((width, 128), F32), ((width, 128), F32),
                     ((self.width, rows), F32), ((self.width, rows), F32), ((rows, width), BF)],
            us=16,
        )
        self.gi2 = ((ga0, ga1), (gb0, gb1))

    def _feed_back(self, hidden):
        rows, width = self.rows, self.width
        scratch = [((width, hidden // 2), BF), ((hidden // 2, width), BF), ((rows, width), BF),
                   ((width, rows), BF), ((width, rows), BF), ((width, rows), BF)]
        return [((width // 2, hidden // 4), BF)] * 8, scratch

    def enc_feed_back_one(self):
        rows, width, hidden = self.rows, self.width, self.active.shape[1]
        ff, scratch = self._feed_back(hidden)
        (*g_ff, self.total, self.biases1) = call2(
            enc_feed_back_one_body,
            [*ff, ((rows, width), F32), ((1, hidden + width), F32)],
            [self.place, self.g_enc, self.normed_two, self.active, self.slope, self.e_weights],
            scratch=scratch,
            hbm_args=1,
            sems=4 + 4 * hidden // width,
            us=14,
        )
        self.ffa = (g_ff[:4], g_ff[4:])

    def enc_feed_back_two(self):
        rows, width, hidden = self.rows, self.width, self.active.shape[1]
        ff, scratch = self._feed_back(hidden)
        (*g_ff, self.g_middle, self.g_att, go0, go1, self.small, self.biases) = call2(
            enc_feed_back_two_body,
            [*ff, ((rows, width), F32), ((rows, width), BF), ((width, width // 2), BF),
             ((width, width // 2), BF), ((16, width), F32),
             ((1, self.biases1.shape[1] + self.biases2.shape[1]), F32)],
            [self.place, self.g_enc, self.normed_two, self.active, self.slope, self.total, self.biases1,
             self.biases2, self.middle, self.e_par, self.att_t, self.e_out, self.e_weights],
            scratch=[((rows, width), F32), *scratch, ((width, rows), F32), ((width, rows), F32),
                     ((rows, width), BF)],
            hbm_args=1,
            sems=4 + 4 * hidden // width,
            us=19,
        )
        self.ffb = (g_ff[:4], g_ff[4:])
        self.go = (go0, go1)

    def enc_attn_back_one(self):
        rows, width = self.rows, self.width
        (self.g_packed,) = call2(
            partial(enc_attn_back_one_body, self.kept),
            [((rows, 3 * width), BF)],
            [self.place, self.packed, self.g_att, self.lse],
            scratch=[((width, rows), BF)],
            us=12,
        )

    def enc_attn_back_two(self):
        rows, width = self.rows, self.width
        n = 3 * width // 2 - CUT_BACK
        ga0, ga1, gb0, gb1, self.g_stream, _ = call2(
            enc_attn_back_two_body,
            [((width, CUT_BACK + width // 2), BF)] * 2 + [((width, n + 128), BF)] * 2
            + [((rows, width), F32), ((16, width), F32)],
            [self.place, self.g_packed, self.x, self.normed, self.g_middle, self.e_par, self.e_in,
             self.small, *self.go],
            scratch=[((width, rows), F32), ((width, rows), F32), ((width, 128), F32),
                     ((width, 128), F32)],
            us=9,
        )
        self.gi = ((ga0, ga1), (gb0, gb1))

    def spread(self):
        return call(
            partial(spread_body, self.kept),
            [((self.span, self.width2), F32), ((self.span, self.width), F32)],
            [self.spots, self.out, self.g_stream],
            us=LAST,
        )

    def land(self, flights, names=(), more=()):
        names = ["place", *names]
        values, more = land(flights, ([getattr(self, n) for n in names], more))
        for name, value in zip(names, values):
            setattr(self, name, value)
        return more


CUT = 640
CUT_BACK = 512


def whole_weights(params, inproj, outproj, embed=None):
    columns = jnp.pad(params, ((0, 0), (0, 128 - params.shape[1])))
    if embed is None:
        return (jnp.concatenate([inproj, outproj, columns], axis=1),)
    n, m, k = inproj.shape[1] // 2, outproj.shape[1] // 2, embed.shape[1] // 2
    one_a = [inproj[:, :CUT], inproj[:, n : n + CUT]]
    one_b = [inproj[:, CUT:n], columns, inproj[:, n + CUT :], jnp.zeros_like(columns)]
    two = [outproj[:, :m], embed[:, :k], outproj[:, m:], embed[:, k:]]
    return tuple(jnp.concatenate(v, axis=1) for v in (one_a, one_b, two))


def local(
    tokens_in, valid_len, mask_pos,
    encoder_gains, encoder_biases, encoder_inproj, encoder_outproj,
    encoder_up, encoder_upbias, encoder_down, encoder_downbias,
    embed_weight, mask_token,
    decoder_gains, decoder_biases, decoder_inproj, decoder_outproj,
    decoder_up, decoder_upbias, decoder_down, decoder_downbias,
    cotangent,
):
    dp, tr, tc = (lax.axis_index(a) for a in ALL)
    blocks = tuple(lax.axis_size(a) for a in ALL) == (8, 2, 2)
    width, width2 = tokens_in.shape[1], cotangent.shape[1]
    hidden, hidden2 = 2 * encoder_up.shape[1], 2 * decoder_up.shape[1]
    masked = jnp.sum((mask_pos[0] < valid_len[0]).astype(jnp.int32))
    at = (dp, tr, tc, dp) if blocks else (0, 0, 0, 0)
    place = jnp.stack([jnp.int32(v) for v in (*at, tc, valid_len[0] - masked, masked, tr)])

    def feed(up, up_bias, down, down_bias):
        rows, units = 2 * up.shape[0] + 16, up.shape[1]
        args = [up, up_bias[None], down, down_bias[None]]
        (packed,) = call(pack_feed_body, [((rows, units), BF)], args, from_hbm=True)
        return lax.all_gather(packed, ("tr", "tc"), axis=0, tiled=True)

    enc = [encoder_up, encoder_upbias, encoder_down, encoder_downbias]
    dec = [decoder_up, decoder_upbias, decoder_down, decoder_downbias]
    if blocks:
        one, two, three = call(
            pack_body,
            [((48, 3 * width // 2 + 128), BF), ((48, width // 2 + width2 // 2), BF),
             ((16, 4 * width2 + 128), BF)],
            [encoder_gains.T, encoder_biases.T, encoder_inproj, encoder_outproj, embed_weight,
             decoder_gains.T, decoder_biases.T, mask_token[None], decoder_inproj, decoder_outproj],
            from_hbm=True,
        )
        enc = feed(*enc)
        one = Flight(gather_lanes(one, CUT))
        two, three = Flight(gather_all(two, GATHER_C)), Flight(gather_all(three, GATHER_D))
        place, dec = land([one], (place, dec))
        dec = feed(*dec)
        (tokens_in,) = land([one, two, three], (tokens_in,))
        sentence = Sentence(place, tokens_in, mask_pos, cotangent)
        sentence.land([one], ["x"])
        sentence.land([one, two], ["x"])
        sentence.land([one, two, three], ["x"])
        one_a, one_b = one.result
    else:
        def whole(v):
            return lax.all_gather(v, ALL, axis=0, tiled=True)

        e_par = whole(jnp.concatenate([encoder_gains, encoder_biases], axis=1))
        d_par = whole(jnp.concatenate([decoder_gains, decoder_biases, mask_token[:, None]], axis=1))
        one_a, one_b, two = whole_weights(
            e_par, whole(encoder_inproj), whole(encoder_outproj), whole(embed_weight)
        )
        (three,) = whole_weights(d_par, whole(decoder_inproj), whole(decoder_outproj))
        one_a, one_b = cut_gathered(one_a, GATHER_A, True), cut_gathered(one_b, GATHER_B, True)
        two = cut_gathered(two, GATHER_C, True)
        three = cut_gathered(three, GATHER_D, False)
        enc, dec = feed(*enc), feed(*dec)
        sentence = Sentence(place, tokens_in, mask_pos, cotangent)

    def feed_out(rows, units, halves):
        parts = len(halves)
        count = units // parts
        arrays = [v for part in halves for v in part]
        return pl.pallas_call(
            partial(out_feed_body, tuple(len(part) for part in halves)),
            out_shape=[jax.ShapeDtypeStruct((rows, units), F32), jax.ShapeDtypeStruct((units, rows), F32)],
            in_specs=[pl.BlockSpec(memory_space=pltpu.SMEM)]
            + [pl.BlockSpec(memory_space=pltpu.VMEM)] * len(arrays),
            out_specs=[pl.BlockSpec(memory_space=pltpu.HBM)] * 2,
            scratch_shapes=[pltpu.VMEM((parts, rows, count), F32), pltpu.VMEM((rows, count), F32),
                            pltpu.VMEM((parts, count, rows), F32), pltpu.SemaphoreType.DMA((2 * parts,))],
            compiler_params=vmem([((rows, units), F32)] * 3),
            cost_estimate=cost(LAST),
        )(place, *arrays)

    def dec_out():
        n, n2 = width // 32, width2 // 32
        return call(
            out_dec_body,
            [((n2, 3 * width2), F32), ((n2, width2), F32), ((2, n2), F32), ((6, n2), F32), ((1, n2), F32),
             ((n, width2), F32)],
            finish(gi2)[0],
            us=LAST,
        )

    def bias_out(biases):
        sizes = [hidden // 2, width // 2, hidden2 // 2, width2 // 2]
        outs = call2(out_bias_body, [((1, n), F32) for n in sizes], [place, biases], us=LAST)
        return [v[0] for v in outs]

    gathers = [two, three] if blocks else []
    sentence.enc_attn(one_a, one_b)
    sentence.land(gathers, ["att_t", "e_par"])
    sentence.land(gathers[:1], ["att_t", "e_par"])
    two = two.result if blocks else two
    sentence.enc_feed(two, enc)
    sentence.land(gathers[1:], ["e_low", "embed"])
    sentence.land(gathers[1:], ["e_low", "embed"])
    three = three.result if blocks else three
    sentence.dec_attn(three)
    sentence.dec_feed(dec)

    if blocks:
        sentence.land([], ["g_middle2", "g_att2", "ff2"])
        ff2 = Flight(reduce_feed(*sentence.ff2, True))
        sentence.land([ff2], ["g_middle2", "g_att2"])
        sentence.dec_attn_back()
        sentence.land([ff2], ["g_enc", "gi2"])
        gi2 = Flight(scatter_lanes(*sentence.gi2))
        sentence.land([gi2], ["g_enc"])
        sentence.enc_feed_back_one()
        sentence.land([ff2, gi2], ["total", "biases1", "ffa"])
        ffa = Flight(reduce_feed(*sentence.ffa, True))
        sentence.land([ffa], ["total", "biases1"])
        sentence.enc_feed_back_two()
        sentence.land([ffa, ff2, gi2], ["g_middle", "g_att", "small", "go", "biases", "ffb"])
        ffb = Flight(reduce_feed(*sentence.ffb, False))
        sentence.land([ffb], ["g_middle", "g_att", "small", "biases"])
        sentence.enc_attn_back_one()
        sentence.land([ffa, ffb, ff2, gi2], ["g_packed"])
        sentence.enc_attn_back_two()
        sentence.land([ffb, ffa, ff2, gi2], ["gi", "g_stream"])
        gi = Flight(scatter_lanes(*sentence.gi, sentence.biases))
        sentence.land([gi], ["g_stream"])
        dec_outs = dec_out()
        sentence.output, sentence.g_tokens = sentence.spread()
        for flight in (ffb, ffa, ff2, ffb):
            land([flight])
        dec_outs, (sentence.output, sentence.g_tokens) = land(
            [gi], (dec_outs, (sentence.output, sentence.g_tokens))
        )
        for flight in (ffa, ffb, ff2, ffa):
            land([flight])
        land([gi])
        outs2 = feed_out(width2 // 2, hidden2 // 2, [finish(ff2)])
        outs2 = land([gi], outs2)
        for flight in (ffb, ffa, ffb):
            land([flight])
        land([gi])
        outs = feed_out(width // 2, hidden // 2, [finish(ffa), finish(ffb)])
        bias_outs = bias_out(finish(gi)[1][0])
    else:
        sentence.dec_attn_back()
        sentence.enc_feed_back_one()
        sentence.enc_feed_back_two()
        sentence.enc_attn_back_one()
        sentence.enc_attn_back_two()

        def halves_of(ups, downs):
            sums = []
            for v in (ups, downs):
                near, far = add(v[0], swap(v[1], "tc")), add(v[2], swap(v[3], "tc"))
                v = lax.psum(add(near, swap(far, "tr")), "dp")
                sums.append(v.reshape(8, -1, v.shape[1]))
            v = jnp.concatenate(sums, axis=1)
            return [v[:4], v[4:]]

        outs2 = feed_out(width2 // 2, hidden2 // 2, [halves_of(*sentence.ff2)])
        halves = [halves_of(*sentence.ffa), halves_of(*sentence.ffb)]
        outs = feed_out(width // 2, hidden // 2, halves)
        bias_outs = bias_out(lax.psum(sentence.biases, ALL))
        sentence.output, sentence.g_tokens = sentence.spread()

    (g_up2, g_down2), (g_up, g_down) = outs2, outs
    b_up, b_down, b_up2, b_down2 = bias_outs
    if blocks:
        n = width // 32
        g_in2, g_out2, g_gains2, g_biases2, g_token, g_embed = dec_outs
        g_in, g_out, g_gains, g_biases = call(
            out_enc_body,
            [((n, 3 * width), F32), ((n, width), F32), ((2, n), F32), ((5, n), F32)],
            finish(gi)[0],
            us=LAST,
        )
        g_gains, g_biases, g_gains2, g_biases2 = g_gains.T, g_biases.T, g_gains2.T, g_biases2.T
        g_token = g_token[0]
    else:
        def scatter(v):
            return lax.psum_scatter(v, ALL, scatter_dimension=0, tiled=True).astype(F32)

        a = join_scattered(sentence.gi[0], SCATTER_A, True)
        b = join_scattered(sentence.gi[1], SCATTER_B, True)
        m = 3 * width // 2 - CUT_BACK
        k = CUT_BACK + width // 2
        g_in = [a[:, :CUT_BACK], b[:, :m], a[:, k : k + CUT_BACK], b[:, m + 128 : 2 * m + 128]]
        g_in = scatter(jnp.concatenate(g_in, axis=1))
        small = scatter(b[:, m : m + 128])
        g_gains, g_biases = small[:, :2], small[:, 2:7]
        g_out = scatter(jnp.concatenate([a[:, CUT_BACK:k], a[:, k + CUT_BACK :]], axis=1))
        g_in2 = scatter(join_scattered(sentence.gi2[0], SCATTER_A, False))
        k = width2 + 128
        v = join_scattered([g[:, :k] for g in sentence.gi2[1]], SCATTER_B, False)
        g_out2, small = scatter(v[:, :width2]), scatter(v[:, width2:])
        g_gains2, g_biases2, g_token = small[:, :2], small[:, 2:8], small[:, 8]
        v = [g[:, k:].reshape(16, -1, 3, width2 // 2).transpose(0, 2, 1, 3) for g in sentence.gi2[1]]
        v = [g.reshape(-1, width2 // 2) for g in v]
        g_embed = scatter(join_scattered(v, SCATTER_B, True))
    return (
        sentence.output, sentence.g_tokens, g_gains, g_biases, g_in, g_out, g_up, b_up, g_down, b_down,
        g_embed, g_token, g_gains2, g_biases2, g_in2, g_out2, g_up2, b_up2, g_down2, b_down2,
    )


def solution(mesh):
    rows = P(ALL, None)
    attention = (rows, rows, rows, rows)
    feed = (P("tc", "tr"), P("tr"), P("tr", "tc"), P("tc"))
    in_specs = (
        (rows, P(ALL), rows) + attention + feed + (rows, P(ALL)) + attention + feed + (rows,)
    )
    out_specs = (rows, rows) + attention + feed + (rows, P(ALL)) + attention + feed
    return jax.shard_map(local, mesh=mesh, in_specs=in_specs, out_specs=out_specs, check_vma=False)
```
